128 devices in a mesh: row: 16 (over z, x), col: 8 (over y, core).
Axes of the slice: x: 4, y: 4, z: 4, core: 2. Of those that a mesh axis runs over, the one named last changes fastest.
Arguments:
- fine_coeffs: float32 [2048, 4096], P(('row', 'col')), may hold values from -6 to 6
- fine_slot: int32 [2048], P(('row', 'col')), may hold values from 0 to 2047, as said below
- neighbours: int32 [256, 6], P('row'), may hold values from -1 to 255, as said below
- filter_matrix: float32 [32, 32], replicated, may hold values from -1 to 1
- kernel_ops: float32 [20, 3, 3, 1024], replicated, may hold values from -0.625 to 0.625
Outputs:
- fine_result: float32 [2048, 4096], P(('row', 'col'))
The draws below stay inside these ranges and needn't reach their ends.
Inputs may be any that keep to these rules, and one draw needn't show every extreme that they name: `fine_slot`: every value appears once. Run r holds the parents r * 16 to (r + 1) * 16 - 1. A fine box on a device with col index c has its parent in the c-th block of 2 consecutive parents of the parent's run. Of the 16 fine boxes of one device, at most 2 have parents in one run, and some device has exactly 2 in some run. -1 where the grid of parents ends. neighbours[neighbours[p, d], d XOR 1] = p. For a parent of run r, the neighbours in directions 0, 2, 4 lie in run (r + 1) mod 16 and those in directions 1, 3, 5 in run (r - 1) mod 16.
All inputs are finite; a program needn't handle non-finite values.
Results may differ from the reference program's by a relative error of at most 0.0001.
Values sent between devices are 32-bit elements; how exact they have to be, the bound alone decides.
A program may use at most 64 MiB of HBM per device.

```python
import jax
import jax.numpy as jnp
import numpy as np
from jax import lax

K = 16
TERMS = 20
GRID_X = 4
GRID_Y = 2
BLOCK = 32
FINE_DEV = 16
PARENTS = 256
FINE = 2048
GRID_Z = 32
N_ROW = 16
N_COL = 8


def draw_fine_slot(key, part):
    base_share = FINE_DEV // N_ROW
    couples = N_ROW // 2
    key_first, key_second, key_amount, key_child, key_place = jax.random.split(jax.random.fold_in(key, 11), 5)
    first_row = jax.random.randint(key_first, (couples, N_COL), 0, N_ROW)
    second_row = (first_row + jax.random.randint(key_second, (couples, N_COL), 1, N_ROW)) % N_ROW
    amount = jax.random.randint(key_amount, (couples, N_COL), 1, base_share + 1).at[0, 0].set(base_share)
    row_iota = jnp.arange(N_ROW)
    raised = (row_iota[None, None, :] == first_row[:, :, None]).astype(jnp.int32)
    lowered = (row_iota[None, None, :] == second_row[:, :, None]).astype(jnp.int32)
    change = amount[:, :, None] * (raised - lowered)
    counts = base_share + jnp.stack([change, -change], axis=1).reshape(N_ROW, N_COL, N_ROW)
    running = jnp.transpose(jnp.cumsum(counts, axis=0), (2, 1, 0))
    item_iota = jnp.arange(FINE_DEV)
    source_row = jnp.sum((running[:, :, None, :] <= item_iota[None, None, :, None]).astype(jnp.int32), axis=3)
    shuffles = jax.vmap(lambda subkey: jax.random.permutation(subkey, FINE_DEV))(jax.random.split(key_child, N_ROW * N_COL))
    handler = jnp.arange(N_ROW * N_COL).reshape(N_ROW, N_COL, 1)
    child_id = handler * FINE_DEV + shuffles.reshape(N_ROW, N_COL, FINE_DEV)
    source_device = source_row * N_COL + jnp.arange(N_COL)[None, :, None]
    sort_key = source_device.reshape(-1) * FINE + jax.random.permutation(key_place, FINE)
    return child_id.reshape(-1)[jnp.argsort(sort_key, stable=True)].astype(jnp.int32)


def draw_neighbours(key, part):
    layer_size = GRID_X * GRID_Y
    cell_iota = jnp.arange(PARENTS)
    along_x = cell_iota % GRID_X
    along_y = cell_iota // GRID_X % GRID_Y
    along_z = cell_iota // layer_size
    owner_row = (along_x + along_y + along_z) % N_ROW
    shuffle = jax.random.permutation(jax.random.fold_in(key, 23), PARENTS)
    ranking = jnp.argsort(owner_row * PARENTS + shuffle, stable=True)
    parent_of = jnp.zeros((PARENTS,), jnp.int32).at[ranking].set(cell_iota.astype(jnp.int32))
    stepping = [(along_x < GRID_X - 1, 1), (along_x > 0, -1), (along_y < GRID_Y - 1, GRID_X), (along_y > 0, -GRID_X), (along_z < GRID_Z - 1, layer_size), (along_z > 0, -layer_size)]
    columns = [jnp.where(inside, parent_of[jnp.clip(cell_iota + stride, 0, PARENTS - 1)], -1) for inside, stride in stepping]
    return jnp.zeros((PARENTS, 6), jnp.int32).at[parent_of].set(jnp.stack(columns, axis=1).astype(jnp.int32))


def levels(own_key, dims, shards, least, high):
    factor_of = 1.0
    for axis_at, blocks in shards:
        heights = jax.random.uniform(jax.random.fold_in(jax.random.fold_in(own_key, 6), axis_at), (blocks,), jnp.float32, least / len(shards), high / len(shards))
        factor_of = factor_of * jnp.repeat(jnp.exp(heights), dims[axis_at] // blocks).reshape((-1,) + (1,) * (len(dims) - 1 - axis_at))
    return factor_of


def scatter_about(stream_key, extent, width, bound, cuts=(), kind=jnp.bfloat16):
    values = jax.random.normal(stream_key, extent, jnp.float32) * width
    if len(cuts) > 0:
        values = levels(stream_key, extent, cuts, -0.22, 0.18) * values
    return jnp.clip(values, min=-bound, max=bound).astype(kind)


def setup_inputs(seed: int = 0) -> dict:
    seeds = jax.random.split(jax.random.key(seed), 6)
    fine_coeffs = scatter_about(seeds[0], (FINE, K ** 3), 1.0, 6.0, ((0, 128),), jnp.float32)
    fine_slot = draw_fine_slot(jax.random.fold_in(seeds[5], 71), 0)
    neighbours = draw_neighbours(jax.random.fold_in(seeds[5], 71), 0)
    filter_matrix = scatter_about(seeds[3], (BLOCK, BLOCK), BLOCK ** -0.5, 1.0, (), jnp.float32)
    kernel_ops = scatter_about(seeds[4], (TERMS, 3, 3, BLOCK * BLOCK), (3 * BLOCK) ** -0.5, 0.625, (), jnp.float32)
    return dict(fine_coeffs=fine_coeffs, fine_slot=fine_slot, neighbours=neighbours, filter_matrix=filter_matrix, kernel_ops=kernel_ops)


exact_mode = lax.Precision.HIGHEST
offset_order = np.array([1, 2, 0])


def rotate_batch(blocks, matrices):
    breadth = matrices.shape[-1]
    viewed = blocks.reshape(blocks.shape[:2] + (-1, breadth))
    result = jnp.einsum('ekc,enmc->enkm', matrices, viewed, precision=exact_mode)
    return result.reshape(blocks.shape[:2] + (-1,))


def rotate_single(blocks, matrix):
    breadth = matrix.shape[-1]
    viewed = blocks.reshape(blocks.shape[:-1] + (-1, breadth))
    result = jnp.einsum('kc,...mc->...km', matrix, viewed, precision=exact_mode)
    return result.reshape(blocks.shape[:-1] + (-1,))


def rotate_many(blocks, matrices):
    breadth = matrices.shape[-1]
    viewed = blocks.reshape(blocks.shape[:1] + (-1, breadth))
    result = jnp.einsum('ekc,nmc->enkm', matrices, viewed, precision=exact_mode)
    return result.reshape((matrices.shape[0], blocks.shape[0], -1))


def octant_tables(pieces):
    octants = np.arange(8)
    return pieces[octants % 2], pieces[(octants // 2) % 2], pieces[octants // 4]


def filter_children(children, filter_matrix):
    breadth = filter_matrix.shape[0]
    pieces = jnp.transpose(filter_matrix.reshape(breadth, 2, breadth // 2), (1, 0, 2))
    along_z, along_y, along_x = octant_tables(pieces)
    sectioned = rotate_batch(children, along_z)
    sectioned = rotate_batch(sectioned, along_y)
    sectioned = rotate_batch(sectioned, along_x)
    return jnp.sum(sectioned, axis=0)


def unfilter_blocks(applied, filter_matrix):
    breadth = filter_matrix.shape[0]
    pieces = jnp.transpose(filter_matrix.reshape(breadth, 2, breadth // 2), (1, 2, 0))
    along_z, along_y, along_x = octant_tables(pieces)
    sectioned = rotate_many(applied, along_z)
    sectioned = rotate_batch(sectioned, along_y)
    return rotate_batch(sectioned, along_x)


def displaced(filtered, kernel_ops):
    amount = filtered.shape[0]
    volume = filtered.shape[1]

    def one_term(totals, factors):
        first_section = rotate_many(filtered, factors[2])
        mid_centre = rotate_many(first_section[1], factors[1][offset_order])
        mid_sides = rotate_single(first_section[np.array([2, 0])], factors[1, 1])
        last_centre = rotate_many(mid_centre[0], factors[0][offset_order])
        last_mid = rotate_single(mid_centre[1:], factors[0, 1])
        last_sides = rotate_single(mid_sides, factors[0, 1])
        return (totals[0] + last_centre, totals[1] + last_mid, totals[2] + last_sides), None

    initial = (jnp.zeros((3, amount, volume), jnp.float32), jnp.zeros((2, amount, volume), jnp.float32), jnp.zeros((2, amount, volume), jnp.float32))
    totals, unused = lax.scan(one_term, initial, kernel_ops)
    return totals


def regroup(stacked, parents, volume):
    return jnp.transpose(stacked, (1, 0, 2, 3)).reshape(stacked.shape[1], parents, volume)


def reference(fine_coeffs, fine_slot, neighbours, filter_matrix, kernel_ops):
    breadth = filter_matrix.shape[0]
    factor_set = kernel_ops.reshape(kernel_ops.shape[:3] + (breadth, breadth))
    parents = neighbours.shape[0]
    volume = fine_coeffs.shape[1]
    ordered = jnp.zeros((parents * 8, volume), jnp.float32).at[fine_slot].set(fine_coeffs)
    children = jnp.transpose(ordered.reshape(parents, 8, volume), (1, 0, 2))
    filtered = filter_children(children, filter_matrix)
    grouped = filtered.reshape(parents // 16, 16, -1)
    centre, middle, side_terms = lax.map(lambda group: displaced(group, factor_set), grouped)
    big_volume = filtered.shape[1]
    centre = regroup(centre, parents, big_volume)
    middle = regroup(middle, parents, big_volume)
    side_terms = regroup(side_terms, parents, big_volume)
    by_direction = [centre[1], centre[2], middle[0], middle[1], side_terms[0], side_terms[1]]
    applied = centre[0]
    for direction in range(6):
        source = neighbours[:, direction ^ 1]
        picked = by_direction[direction][jnp.clip(source, 0, parents - 1)]
        applied = applied + jnp.where((source >= 0)[:, None], picked, 0.0)
    unfiltered = lax.map(lambda group: unfilter_blocks(group, filter_matrix), applied.reshape(parents // 16, 16, -1))
    unfiltered = jnp.transpose(unfiltered, (0, 2, 1, 3)).reshape(parents * 8, volume)
    return unfiltered[fine_slot]
```

```python
import functools

import jax
import jax.numpy as jnp
from jax import lax
from jax.experimental import pallas as pl
from jax.experimental.pallas import tpu as pltpu
from jax.sharding import PartitionSpec as P

exact_mode = lax.Precision.HIGHEST
f32, bf16 = jnp.float32, jnp.bfloat16
TERMS, N, PAIRS = 20, 32, 10


def split(x):
    hi = x.astype(bf16)
    return hi, (x - hi.astype(f32)).astype(bf16)


def split_outside(x):
    rounded = lax.reduce_precision(x, 8, 7)
    return rounded.astype(bf16), (x - rounded).astype(bf16)


def dot(a, b):
    return jnp.dot(a, b, preferred_element_type=f32)


def packed_rows(x):
    hi, lo = split(x)
    return jnp.concatenate([hi, lo, hi], axis=1)


def low_half(rows):
    return lax.broadcasted_iota(jnp.int32, (rows, 128), 1) < 64


def centre_pass(xk, wz, wy, wx, t_hi, t_lo, ys, out):
    mask = low_half(N)

    def pair(mp, carry):
        weights = wz[mp]
        for q in range(4):
            z = dot(xk[q * 256 : (q + 1) * 256, :], weights)
            hi, lo = split(z)
            t_hi[q * 256 : (q + 1) * 256, 0:128] = hi
            t_lo[q * 256 : (q + 1) * 256, 0:128] = lo
        left = wy[mp]

        def line(i8, carry):
            for k in range(8):
                i = i8 * 8 + k
                at = pl.ds(pl.multiple_of(i * N, N), N)
                hi, lo = t_hi[at, 0:128], t_lo[at, 0:128]
                y = dot(left, jnp.concatenate([hi, lo, hi], axis=0))
                ys[pl.ds(mp * N + i, N, stride=PAIRS * N), :] = jnp.where(mask, y[:N], y[N:])
            return carry

        return lax.fori_loop(0, N // 8, line, carry)

    lax.fori_loop(0, PAIRS, pair, 0)

    def column(b, carry):
        at = pl.ds(pl.multiple_of(b * PAIRS * N, PAIRS * N), PAIRS * N)
        hi, lo = split(ys[at, :])
        first = dot(wx[...], hi)
        r = first[:64] + first[64:] + dot(wx[0:64, :], lo)
        out[pl.ds(pl.multiple_of(b * N, N), N), :] = r[:N] + pltpu.roll(r[N:], 64, 1)
        return carry

    lax.fori_loop(0, N, column, 0, unroll=2)


def sides_pass(xkb, xka, wzb, wza, wy, wx, wx0, t_hi, t_lo, ya, yb, yc, out):
    mask = low_half(N)

    def pair(mp, carry):
        for xk, wz, base in ((xkb, wzb, 0), (xka, wza, 128)):
            weights = wz[mp]
            for q in range(4):
                z = dot(xk[q * 256 : (q + 1) * 256, :], weights)
                hi, lo = split(z)
                for odd in range(2):
                    t_hi[odd * 1024 + q * 256 : odd * 1024 + (q + 1) * 256, base : base + 128] = hi[
                        :, odd * 128 : (odd + 1) * 128
                    ]
                    t_lo[odd * 1024 + q * 256 : odd * 1024 + (q + 1) * 256, base : base + 128] = lo[
                        :, odd * 128 : (odd + 1) * 128
                    ]
        for odd in range(2):
            m = mp * 2 + odd
            left = wy[m]

            def line(i8, carry, odd=odd, m=m, left=left):
                for k in range(8):
                    i = i8 * 8 + k
                    at = pl.ds(pl.multiple_of(odd * 1024 + i * N, N), N)
                    hi, lo = t_hi[at, :], t_lo[at, :]
                    y = dot(left, jnp.concatenate([hi, lo, hi], axis=0))
                    to = pl.ds(m * N + i, N, stride=TERMS * N)
                    ya[to, :] = y[:N, :128]
                    yb[to, :] = y[:N, 128:]
                    yc[to, :] = jnp.where(mask, y[N : 2 * N, :128], y[2 * N :, 128:])
                return carry

            lax.fori_loop(0, N // 8, line, 0)
        return carry

    lax.fori_loop(0, PAIRS, pair, 0)

    def column(b, carry):
        at = pl.ds(pl.multiple_of(b * TERMS * N, TERMS * N), TERMS * N)
        rows = pl.ds(pl.multiple_of(b * N, N), N)
        hi, lo = split(ya[at, :])
        first = dot(wx[0:128, :], hi)
        r = first[:64] + first[64:128] + dot(wx[0:64, :], lo)
        out[rows, 0:128] = jnp.where(mask, r[:N], r[N:])
        hi, lo = split(yb[at, :])
        first = dot(wx[128:256, :], hi)
        r = first[:64] + first[64:128] + dot(wx[128:192, :], lo)
        out[rows, 128:256] = jnp.where(mask, r[:N], r[N:])
        hi, lo = split(yc[at, :])
        first = dot(wx0[...], hi)
        out[rows, 256:384] = first[:N] + first[N:] + dot(wx0[0:N, :], lo)
        return carry

    lax.fori_loop(0, N, column, 0)


def kernel(xo, xb, xa, wzo, wzb, wza, wyo, wys, wxo, wxs, wx0, sel, part, centre,
           xk, xkb, t_hi, t_lo, yo, ya, yb, yc, terms):
    xk[...] = packed_rows(xo[...])
    centre_pass(xk, wzo, wyo, wxo, t_hi, t_lo, yo, centre)
    xk[...] = packed_rows(xa[...])
    xkb[...] = packed_rows(xb[...])
    sides_pass(xkb, xk, wzb, wza, wys, wxs, wx0, t_hi, t_lo, ya, yb, yc, terms)
    for q in range(4):
        rows = slice(q * 256, (q + 1) * 256)
        hi, lo = split(terms[rows, :])
        summed = dot(hi, sel[...]) + dot(lo, sel[...])
        for y in range(4):
            part[y, rows, :] = summed[:, y * 128 : (y + 1) * 128]


def convolve(xo, xb, xa, weights, sel):
    vm = pl.BlockSpec(memory_space=pltpu.VMEM)
    operands = (xo, xb, xa, *weights, sel)
    return pl.pallas_call(
        kernel,
        out_shape=(
            jax.ShapeDtypeStruct((4, 1024, 128), f32),
            jax.ShapeDtypeStruct((1024, 128), f32),
        ),
        in_specs=[vm] * len(operands),
        out_specs=(vm, vm),
        scratch_shapes=[
            pltpu.VMEM((1024, 192), bf16),
            pltpu.VMEM((1024, 192), bf16),
            pltpu.VMEM((2048, 256), bf16),
            pltpu.VMEM((2048, 256), bf16),
            pltpu.VMEM((N * PAIRS * N, 128), f32),
            pltpu.VMEM((N * TERMS * N, 128), f32),
            pltpu.VMEM((N * TERMS * N, 128), f32),
            pltpu.VMEM((N * TERMS * N, 128), f32),
            pltpu.VMEM((1024, 384), f32),
        ],
        compiler_params=pltpu.CompilerParams(vmem_limit_bytes=60 * 2**20),
    )(*operands)


def both(mats):
    return jnp.einsum("...ci,pq->...piqc", mats, jnp.eye(2, dtype=f32))


def z_weights(mats):
    g, v = mats.shape[:2]
    wide = jnp.transpose(both(mats), (0, 2, 3, 1, 4, 5)).reshape(g, 64, v * 64)
    hi, lo = split_outside(wide)
    return jnp.concatenate([hi, hi, lo], axis=1)


def y_weights(mats):
    hi, lo = split_outside(mats.reshape(mats.shape[0], -1, N))
    return jnp.concatenate([hi, hi, lo], axis=2)


def x_weights(mats):
    return jnp.concatenate(split_outside(mats.reshape(-1, mats.shape[-1])), axis=0)


def take(array, axis, places):
    return jnp.stack([lax.index_in_dim(array, k, axis, False) for k in places], axis)


def prepare(filter_matrix, kernel_ops):
    raw = kernel_ops.reshape(TERMS, 3, 3, N, N)
    folded = jnp.einsum("...ab,bj->...aj", raw, filter_matrix, precision=exact_mode)
    folded = jnp.einsum("...aj,ai->...ij", folded, filter_matrix, precision=exact_mode)
    fx, fy, fz = folded[:, 0], folded[:, 1], folded[:, 2]
    z_pair = fz.reshape(PAIRS, 2, 3, N, N)
    wzo = z_weights(z_pair[:, :, 1])
    wzb = z_weights(take(z_pair, 2, (1, 2)).reshape(PAIRS, 4, N, N))
    wza = z_weights(take(z_pair, 2, (0, 1)).reshape(PAIRS, 4, N, N))
    wyo = y_weights(fy[:, 1].reshape(PAIRS, 2, N, N))
    wys = y_weights(take(fy, 1, (1, 2, 0)))
    along = jnp.transpose(fx, (1, 2, 0, 3))
    paired = along[1].reshape(N, PAIRS, 2, N)
    wxo = x_weights(jnp.transpose(paired, (2, 0, 1, 3)).reshape(2, N, PAIRS * N))
    flat = along.reshape(3, N, TERMS * N)
    wxs = jnp.concatenate([x_weights(take(flat, 0, (2, 1))), x_weights(take(flat, 0, (1, 0)))])
    wx0 = x_weights(flat[1:2])
    return wzo, wzb, wza, wyo, wys, wxo, wxs, wx0


def selection(neighbours, col_index):
    order = (1, 5, 4, 0, 3, 2)
    sender = take(neighbours, 1, order)
    within = sender % 16 - col_index * 2
    hit = (sender >= 0)[:, :, None] & (within[:, :, None] == jnp.arange(2)[None, None, :])
    hit = jnp.transpose(hit, (1, 2, 0)).astype(bf16)
    return (
        hit[:, :, None, :, None] * jnp.eye(N, dtype=bf16)[None, None, :, None, :]
    ).reshape(384, 512)


def shifted(array, axis, by):
    peers = lax.axis_size(axis)
    return lax.ppermute(array, axis, [(i, (i + by) % peers) for i in range(peers)])


def local(fine_coeffs, fine_slot, neighbours, filter_matrix, kernel_ops):
    row_count = lax.axis_size("row")
    held_boxes, volume = fine_coeffs.shape
    par_row = neighbours.shape[0]
    source_count = held_boxes // 8
    capacity = 2
    col_index = lax.axis_index("col")
    weights = prepare(filter_matrix, kernel_ops)
    dest_row = fine_slot // (8 * par_row)
    item = jnp.arange(held_boxes)
    earlier = (dest_row[None, :] == dest_row[:, None]) & (item[None, :] < item[:, None])
    slot_index = dest_row * capacity + jnp.sum(earlier.astype(jnp.int32), axis=1)
    packer = jnp.arange(row_count * capacity)[:, None] == slot_index[None, :]
    send_blocks = jnp.dot(packer.astype(f32), fine_coeffs, precision=exact_mode)
    send_ids = jnp.max(jnp.where(packer, fine_slot[None, :], -1), axis=1)
    a2a = functools.partial(
        lax.all_to_all, axis_name="row", split_axis=0, concat_axis=0, tiled=True
    )
    got_blocks = a2a(send_blocks.reshape(row_count, capacity, volume))
    got_ids = a2a(send_ids.reshape(row_count, capacity)).reshape(-1)
    child_pos = got_ids % held_boxes
    picker = (
        (child_pos[None, :] == jnp.arange(held_boxes)[:, None]) & (got_ids[None, :] >= 0)
    ).astype(f32)
    children = jnp.dot(picker, got_blocks.reshape(-1, volume), precision=exact_mode)
    boxes = children.reshape(source_count, 2, 2, 2, 16, 16, 16)
    own = jnp.transpose(boxes, (1, 4, 2, 5, 0, 3, 6)).reshape(1024, 64)
    below, above = shifted(own, "row", 1), shifted(own, "row", -1)
    part, centre = convolve(own, below, above, weights, selection(neighbours, col_index))
    part = part.reshape(4, 1024, 2, 64).transpose(0, 2, 1, 3).reshape(8, 1024, 64)
    arrived = lax.all_to_all(part, "col", split_axis=0, concat_axis=0, tiled=True)
    applied = centre[:, :64] + arrived.sum(axis=0)
    result = applied.reshape(2, 16, 2, 16, source_count, 2, 16)
    result = jnp.transpose(result, (4, 2, 0, 5, 3, 1, 6)).reshape(held_boxes, volume)
    back = jnp.einsum("ab,ac->bc", picker, result, precision=exact_mode)
    returned = a2a(back.reshape(row_count, capacity, volume))
    return jnp.einsum(
        "ab,ac->bc", packer.astype(f32), returned.reshape(-1, volume), precision=exact_mode
    )


def solution(mesh):
    in_specs = (P(("row", "col"), None), P(("row", "col")), P("row", None), P(), P())
    out_specs = P(("row", "col"), None)
    return jax.shard_map(local, mesh=mesh, in_specs=in_specs, out_specs=out_specs, check_vma=False)
```

```python
import functools

import jax
import jax.numpy as jnp
from jax import lax
from jax.experimental import pallas as pl
from jax.experimental.pallas import tpu as pltpu
from jax.sharding import PartitionSpec as P

exact_mode = lax.Precision.HIGHEST
f32, bf16 = jnp.float32, jnp.bfloat16
TERMS, N, PAIRS = 20, 32, 10


def split(x):
    hi = x.astype(bf16)
    return hi, (x - hi.astype(f32)).astype(bf16)


def dot(a, b):
    return jnp.dot(a, b, preferred_element_type=f32)


def dot_t(a, b):
    return lax.dot_general(a, b, (((1,), (1,)), ((), ())), preferred_element_type=f32)


def packed_rows(x):
    hi, lo = split(x)
    return jnp.concatenate([hi, lo, hi], axis=1)


def low_half(rows):
    return lax.broadcasted_iota(jnp.int32, (rows, 128), 1) < 64


def centre_pass(xk, wz, wy, wx, t_hi, t_lo, ys, out):
    mask = low_half(N)

    def pair(mp, carry):
        weights = wz[pl.ds(pl.multiple_of(mp * 128, 128), 128), 0:192]
        for q in range(4):
            z = dot_t(xk[q * 256 : (q + 1) * 256, :], weights)
            hi, lo = split(z)
            t_hi[q * 256 : (q + 1) * 256, 0:128] = hi
            t_lo[q * 256 : (q + 1) * 256, 0:128] = lo
        left = jnp.concatenate([wy[mp * 2, 0:N, 0:96], wy[mp * 2 + 1, 0:N, 0:96]], axis=0)

        def line(i8, carry):
            for k in range(8):
                i = i8 * 8 + k
                at = pl.ds(pl.multiple_of(i * N, N), N)
                hi, lo = t_hi[at, 0:128], t_lo[at, 0:128]
                y = dot(left, jnp.concatenate([hi, lo, hi], axis=0))
                ys[pl.ds(mp * N + i, N, stride=PAIRS * N), :] = jnp.where(mask, y[:N], y[N:])
            return carry

        return lax.fori_loop(0, N // 8, line, carry)

    lax.fori_loop(0, PAIRS, pair, 0)

    def column(b, carry):
        at = pl.ds(pl.multiple_of(b * PAIRS * N, PAIRS * N), PAIRS * N)
        hi, lo = split(ys[at, :])
        first = dot(wx[:, 0:320], hi)
        r = first[:64] + first[64:] + dot(wx[0:64, 0:320], lo)
        out[pl.ds(pl.multiple_of(b * N, N), N), :] = r[:N] + pltpu.roll(r[N:], 64, 1)
        return carry

    lax.fori_loop(0, N, column, 0, unroll=2)


def sides_pass(xkb, xka, wzb, wza, wy, wx, wx0, t_hi, t_lo, ya, yb, yc, out):
    mask = low_half(N)

    def pair(mp, carry):
        for xk, wz, base in ((xkb, wzb, 0), (xka, wza, 128)):
            weights = wz[pl.ds(pl.multiple_of(mp * 256, 256), 256), 0:192]
            for q in range(4):
                z = dot_t(xk[q * 256 : (q + 1) * 256, :], weights)
                hi, lo = split(z)
                for odd in range(2):
                    t_hi[odd * 1024 + q * 256 : odd * 1024 + (q + 1) * 256, base : base + 128] = hi[
                        :, odd * 128 : (odd + 1) * 128
                    ]
                    t_lo[odd * 1024 + q * 256 : odd * 1024 + (q + 1) * 256, base : base + 128] = lo[
                        :, odd * 128 : (odd + 1) * 128
                    ]
        for odd in range(2):
            m = mp * 2 + odd
            left = wy[m, :, 0:96]

            def line(i8, carry, odd=odd, m=m, left=left):
                for k in range(8):
                    i = i8 * 8 + k
                    at = pl.ds(pl.multiple_of(odd * 1024 + i * N, N), N)
                    hi, lo = t_hi[at, :], t_lo[at, :]
                    y = dot(left, jnp.concatenate([hi, lo, hi], axis=0))
                    to = pl.ds(m * N + i, N, stride=TERMS * N)
                    ya[to, :] = y[:N, :128]
                    yb[to, :] = y[:N, 128:]
                    yc[to, :] = jnp.where(mask, y[N : 2 * N, :128], y[2 * N :, 128:])
                return carry

            lax.fori_loop(0, N // 8, line, 0)
        return carry

    lax.fori_loop(0, PAIRS, pair, 0)

    def column(b, carry):
        at = pl.ds(pl.multiple_of(b * TERMS * N, TERMS * N), TERMS * N)
        rows = pl.ds(pl.multiple_of(b * N, N), N)
        hi, lo = split(ya[at, :])
        first = dot(wx[0:128, :], hi)
        r = first[:64] + first[64:128] + dot(wx[0:64, :], lo)
        out[rows, 0:128] = jnp.where(mask, r[:N], r[N:])
        hi, lo = split(yb[at, :])
        first = dot(wx[128:256, :], hi)
        r = first[:64] + first[64:128] + dot(wx[128:192, :], lo)
        out[rows, 128:256] = jnp.where(mask, r[:N], r[N:])
        hi, lo = split(yc[at, :])
        first = dot(wx0[...], hi)
        out[rows, 256:384] = first[:N] + first[N:] + dot(wx0[0:N, :], lo)
        return carry

    lax.fori_loop(0, N, column, 0)


def kernel(xo, xb, xa, wzo, wzb, wza, wys, wxo, wxs, wx0, sel, part, centre,
           xk, xkb, t_hi, t_lo, yo, ya, yb, yc, terms):
    xk[...] = packed_rows(xo[...])
    centre_pass(xk, wzo, wys, wxo, t_hi, t_lo, yo, centre)
    xk[...] = packed_rows(xa[...])
    xkb[...] = packed_rows(xb[...])
    sides_pass(xkb, xk, wzb, wza, wys, wxs, wx0, t_hi, t_lo, ya, yb, yc, terms)
    for q in range(4):
        rows = slice(q * 256, (q + 1) * 256)
        hi, lo = split(terms[rows, :])
        summed = dot(hi, sel[...]) + dot(lo, sel[...])
        for y in range(4):
            part[y, rows, :] = summed[:, y * 128 : (y + 1) * 128]


def convolve(xo, xb, xa, weights, sel):
    vm = pl.BlockSpec(memory_space=pltpu.VMEM)
    operands = (xo, xb, xa, *weights, sel)
    return pl.pallas_call(
        kernel,
        out_shape=(
            jax.ShapeDtypeStruct((4, 1024, 128), f32),
            jax.ShapeDtypeStruct((1024, 128), f32),
        ),
        in_specs=[vm] * len(operands),
        out_specs=(vm, vm),
        scratch_shapes=[
            pltpu.VMEM((1024, 192), bf16),
            pltpu.VMEM((1024, 192), bf16),
            pltpu.VMEM((2048, 256), bf16),
            pltpu.VMEM((2048, 256), bf16),
            pltpu.VMEM((N * PAIRS * N, 128), f32),
            pltpu.VMEM((N * TERMS * N, 128), f32),
            pltpu.VMEM((N * TERMS * N, 128), f32),
            pltpu.VMEM((N * TERMS * N, 128), f32),
            pltpu.VMEM((1024, 384), f32),
        ],
        compiler_params=pltpu.CompilerParams(vmem_limit_bytes=60 * 2**20),
    )(*operands)


def take(array, axis, places):
    return jnp.stack([lax.index_in_dim(array, k, axis, False) for k in places], axis)


def fold_kernel(f, hx, ht, wzo, wzb, wza, wys, wxo, wxs, wx0, k_hi, k_lo, folded, mats):
    def row(a, carry):
        hi, lo = split(hx[pl.ds(a, 1), :] * ht[...])
        at = pl.ds(pl.multiple_of(a * N, N), N)
        k_hi[at, :] = hi
        k_lo[at, :] = lo
        return carry

    lax.fori_loop(0, N, row, 0)
    f_hi, f_lo = split(f[...])
    for n in range(4):
        at = slice(n * 256, (n + 1) * 256)
        folded[:, at] = dot(f_hi, k_hi[:, at]) + dot(f_lo, k_hi[:, at]) + dot(f_hi, k_lo[:, at])
    for g in range(8):
        piece = folded[:, g * 128 : (g + 1) * 128]
        for k in range(4):
            turned = piece if k == 0 else pltpu.roll(piece, 128 - 32 * k, 1)
            mats[pl.ds(4 * g + k, 192, stride=N), :] = turned
    mask = lax.broadcasted_iota(jnp.int32, (N, 128), 1) < N

    def matrix(m, axis, offset):
        start = (m * 9 + axis * 3 + offset) * N
        v = mats[pl.ds(start if isinstance(m, int) else pl.multiple_of(start, N), N), :]
        return jnp.where(mask, v, 0.0)

    def parts(v):
        hi = v.astype(bf16).astype(f32)
        return hi, v - hi

    def term(m, carry):
        for t, offset in enumerate((1, 2, 0)):
            hi, lo = parts(matrix(m, 1, offset))
            wys[m, t * N : (t + 1) * N, :] = (hi + pltpu.roll(hi, 32, 1) + pltpu.roll(lo, 64, 1)).astype(bf16)
        for offset, places in ((0, ((wza, 0),)), (1, ((wzo, 0), (wzb, 0), (wza, 64))), (2, ((wzb, 64),))):
            hi, lo = parts(matrix(m, 2, offset))
            first = hi + pltpu.roll(hi, 64, 1)
            for ref, base in places:
                start = m * (64 if ref is wzo else 128) + base
                for p in range(2):
                    at = pl.ds(pl.multiple_of(start + p * N, N), N)
                    ref[at, 0:128] = (pltpu.roll(first, 32, 1) if p else first).astype(bf16)
                    ref[at, 128:256] = (pltpu.roll(lo, 32, 1) if p else lo).astype(bf16)
        return carry

    lax.fori_loop(0, TERMS, term, 0)

    def wide(terms, offset):
        total = None
        for k, m in enumerate(terms):
            v = matrix(m, 0, offset)
            v = pltpu.roll(v, 32 * k, 1) if k else v
            total = v if total is None else total + v
        return split(total)

    for g in range(5):
        at = slice(g * 128, (g + 1) * 128)
        for offset, places in ((2, ((wxs, 0, 64),)), (1, ((wxs, 32, 96), (wxs, 128, 192), (wx0, 0, 32))), (0, ((wxs, 160, 224),))):
            hi, lo = wide(range(4 * g, 4 * g + 4), offset)
            for ref, high_at, low_at in places:
                ref[high_at : high_at + N, at] = hi
                ref[low_at : low_at + N, at] = lo
    for g in range(3):
        at = slice(g * 128, (g + 1) * 128)
        for odd in range(2):
            hi, lo = wide([2 * mp + odd for mp in range(4 * g, min(4 * g + 4, PAIRS))], 1)
            wxo[odd * N : (odd + 1) * N, at] = hi
            wxo[64 + odd * N : 64 + (odd + 1) * N, at] = lo


def prepare(filter_matrix, kernel_ops):
    f = jnp.pad(kernel_ops.reshape(TERMS * 9, N * N), ((0, 12), (0, 0)))
    hx = jnp.repeat(filter_matrix, N, axis=1)
    ht = jnp.tile(filter_matrix, (1, N))
    vm = pl.BlockSpec(memory_space=pltpu.VMEM)
    shapes = ((1280, 256), (2560, 256), (2560, 256), (TERMS, 96, 128), (128, 384), (256, 640), (64, 640))
    return pl.pallas_call(
        fold_kernel,
        out_shape=tuple(jax.ShapeDtypeStruct(shape, bf16) for shape in shapes),
        in_specs=[vm] * 3,
        out_specs=(vm,) * len(shapes),
        scratch_shapes=[
            pltpu.VMEM((1024, 1024), bf16),
            pltpu.VMEM((1024, 1024), bf16),
            pltpu.VMEM((192, 1024), f32),
            pltpu.VMEM((192 * N, 128), f32),
        ],
        compiler_params=pltpu.CompilerParams(vmem_limit_bytes=40 * 2**20),
    )(f, hx, ht)


MESH = pl.DeviceIdType.MESH
Y, CORES, ROWS = 4, 2, 16


def return_kernel(part, centre, held, slot, out, from_core, pair_sum, from_y, total, from_half,
                  applied, boxes, leaving, back, s1, r1, s2, r2, s3, r3, s4, r4):
    row, col = lax.axis_index("row"), lax.axis_index("col")
    y, core = col // CORES, col % CORES
    sibling = y * CORES + (1 - core)
    peers = [(row, sibling)]
    peers += [(row, (y + 1 + d) % Y * CORES + core) for d in range(Y - 1)]
    peers += [((row + d) % ROWS, col) for d in range(1, ROWS)]
    barrier = pltpu.get_barrier_semaphore()
    for peer in peers:
        pl.semaphore_signal(barrier, inc=1, device_id=peer, device_id_type=MESH)
    pl.semaphore_wait(barrier, len(peers))
    mine = pl.ds(pl.multiple_of(core * 512, 512), 512)
    other = pl.ds(pl.multiple_of((1 - core) * 512, 512), 512)

    def send(src, dst, s, r, peer):
        copy = pltpu.make_async_remote_copy(
            src_ref=src, dst_ref=dst, send_sem=s, recv_sem=r, device_id=peer, device_id_type=MESH
        )
        copy.start()
        return copy

    order = [(y + 1 + d) % Y for d in range(Y)]
    first = [
        send(part.at[to, other], from_core.at[d], s1.at[d], r1.at[d], (row, sibling))
        for d, to in enumerate(order)
    ]
    second = []
    for d, to in enumerate(order):
        first[d].wait_recv()
        if d < Y - 1:
            pair_sum[d] = part[to, mine, :] + from_core[d]
            second.append(
                send(pair_sum.at[d], from_y.at[d], s2.at[d], r2.at[d], (row, to * CORES + core))
            )
        else:
            total[...] = part[to, mine, :] + from_core[d]
    for copy in second:
        copy.wait_recv()
    total[...] = total[...] + from_y[0] + from_y[1] + from_y[2]
    third = send(total, from_half, s3, r3, (row, sibling))

    def own_lanes(v):
        return jnp.where(core == 1, pltpu.roll(v, 64, 1), v)

    applied[mine, :] = own_lanes(total[...]) + centre[mine, :]
    third.wait_recv()
    applied[other, :] = own_lanes(from_half[...]) + centre[other, :]
    lanes = lax.broadcasted_iota(jnp.int32, (16, 128), 1) // 16
    for ox in range(2):
        for oy in range(2):
            for jh in range(2):
                lines = [
                    applied[pl.ds((oy * 16 + jh * 8 + j) * N + ox * 16, 16), :] for j in range(8)
                ]
                for p in range(2):
                    for oz in range(2):
                        base = p * 32 + oz * 16
                        box = None
                        for j in range(8):
                            shift = (16 * j - base) % 128
                            v = pltpu.roll(lines[j], shift, 1) if shift else lines[j]
                            box = v if box is None else jnp.where(lanes == j, v, box)
                        boxes[p * 8 + ox * 4 + oy * 2 + oz, pl.ds(jh, 16, stride=2), :] = box
    fourth = []
    for d in range(1, ROWS):
        to = (row + d) % ROWS
        for s in range(2):
            leaving[d * 2 + s] = boxes[held[to * 2 + s]]
        fourth.append(
            send(
                leaving.at[pl.ds(d * 2, 2)],
                back.at[pl.ds(row * 2, 2)],
                s4.at[d],
                r4.at[d],
                (to, col),
            )
        )
    for s in range(2):
        back[row * 2 + s] = boxes[held[row * 2 + s]]
    for copy in fourth:
        copy.wait_recv()
    for q in range(16):
        out[q] = back[slot[q]]
    for copy in first + second + [third] + fourth:
        copy.wait_send()


def gather_back(part, centre, held, slot):
    vm = pl.BlockSpec(memory_space=pltpu.VMEM)
    sm = pl.BlockSpec(memory_space=pltpu.SMEM)
    sems = [pltpu.SemaphoreType.DMA((n,)) for n in (4, 4, 3, 3)]
    sems += [pltpu.SemaphoreType.DMA, pltpu.SemaphoreType.DMA]
    sems += [pltpu.SemaphoreType.DMA((ROWS,)), pltpu.SemaphoreType.DMA((ROWS,))]
    return pl.pallas_call(
        return_kernel,
        out_shape=jax.ShapeDtypeStruct((16, 32, 128), f32),
        in_specs=[vm, vm, sm, sm],
        out_specs=vm,
        scratch_shapes=[
            pltpu.VMEM((4, 512, 128), f32),
            pltpu.VMEM((3, 512, 128), f32),
            pltpu.VMEM((3, 512, 128), f32),
            pltpu.VMEM((512, 128), f32),
            pltpu.VMEM((512, 128), f32),
            pltpu.VMEM((1024, 128), f32),
            pltpu.VMEM((16, 32, 128), f32),
            pltpu.VMEM((32, 32, 128), f32),
            pltpu.VMEM((32, 32, 128), f32),
        ]
        + sems,
        compiler_params=pltpu.CompilerParams(
            collective_id=2, has_side_effects=True, vmem_limit_bytes=32 * 2**20
        ),
    )(part, centre, held, slot)


def selection(neighbours, col_index):
    order = (1, 5, 4, 0, 3, 2)
    sender = take(neighbours, 1, order)
    within = sender % 16 - col_index * 2
    hit = (sender >= 0)[:, :, None] & (within[:, :, None] == jnp.arange(2)[None, None, :])
    hit = jnp.transpose(hit, (1, 2, 0)).astype(bf16)
    return (
        hit[:, :, None, :, None] * jnp.eye(N, dtype=bf16)[None, None, :, None, :]
    ).reshape(384, 512)


def shifted(array, axis, by):
    peers = lax.axis_size(axis)
    return lax.ppermute(array, axis, [(i, (i + by) % peers) for i in range(peers)])


def local(fine_coeffs, fine_slot, neighbours, filter_matrix, kernel_ops):
    row_count = lax.axis_size("row")
    held_boxes, volume = fine_coeffs.shape
    par_row = neighbours.shape[0]
    source_count = held_boxes // 8
    capacity = 2
    col_index = lax.axis_index("col")
    weights = prepare(filter_matrix, kernel_ops)
    dest_row = fine_slot // (8 * par_row)
    item = jnp.arange(held_boxes)
    earlier = (dest_row[None, :] == dest_row[:, None]) & (item[None, :] < item[:, None])
    slot_index = dest_row * capacity + jnp.sum(earlier.astype(jnp.int32), axis=1)
    packer = jnp.arange(row_count * capacity)[:, None] == slot_index[None, :]
    send_blocks = jnp.dot(packer.astype(f32), fine_coeffs, precision=exact_mode)
    send_ids = jnp.max(jnp.where(packer, fine_slot[None, :], -1), axis=1)
    a2a = functools.partial(
        lax.all_to_all, axis_name="row", split_axis=0, concat_axis=0, tiled=True
    )
    got_blocks = a2a(send_blocks.reshape(row_count, capacity, volume))
    got_ids = a2a(send_ids.reshape(row_count, capacity)).reshape(-1)
    child_pos = got_ids % held_boxes
    picker = (
        (child_pos[None, :] == jnp.arange(held_boxes)[:, None]) & (got_ids[None, :] >= 0)
    ).astype(f32)
    children = jnp.dot(picker, got_blocks.reshape(-1, volume), precision=exact_mode)
    boxes = children.reshape(source_count, 2, 2, 2, 16, 16, 16)
    own = jnp.transpose(boxes, (1, 4, 2, 5, 0, 3, 6)).reshape(1024, 64)
    below, above = shifted(own, "row", 1), shifted(own, "row", -1)
    part, centre = convolve(own, below, above, weights, selection(neighbours, col_index))
    held = jnp.where(got_ids >= 0, child_pos, 0)
    return gather_back(part, centre, held, slot_index).reshape(held_boxes, volume)


def solution(mesh):
    in_specs = (P(("row", "col"), None), P(("row", "col")), P("row", None), P(), P())
    out_specs = P(("row", "col"), None)
    return jax.shard_map(local, mesh=mesh, in_specs=in_specs, out_specs=out_specs, check_vma=False)
```

```python
import jax
import jax.numpy as jnp
from jax import lax
from jax.experimental import pallas as pl
from jax.experimental.pallas import tpu as pltpu
from jax.sharding import PartitionSpec as P

f32, bf16 = jnp.float32, jnp.bfloat16
TERMS, N, PAIRS = 20, 32, 10
SIDE_LINE, OWN_LINE = TERMS * N + 8, PAIRS * N + 8


def split(x):
    hi = x.astype(bf16)
    return hi, (x - hi.astype(f32)).astype(bf16)


def dot(a, b):
    return jnp.dot(a, b, preferred_element_type=f32)


def dot_t(a, b):
    return lax.dot_general(a, b, (((1,), (1,)), ((), ())), preferred_element_type=f32)


def low_half(rows):
    return lax.broadcasted_iota(jnp.int32, (rows, 128), 1) < 64


def centre_pass(xk, wz, wy, wx, t_hi, t_lo, ys, out):
    mask = low_half(N)

    def pair(mp, carry):
        weights = wz[pl.ds(pl.multiple_of(mp * 128, 128), 128), 0:192]
        for q in range(4):
            z = dot_t(xk[q * 256 : (q + 1) * 256, 0:192], weights)
            hi, lo = split(z)
            t_hi[q * 256 : (q + 1) * 256, 0:128] = hi
            t_lo[q * 256 : (q + 1) * 256, 0:128] = lo
        left = jnp.concatenate([wy[mp * 2, 0:N, 0:96], wy[mp * 2 + 1, 0:N, 0:96]], axis=0)

        for i in range(N):
            at = slice(i * N, (i + 1) * N)
            hi, lo = t_hi[at, 0:128], t_lo[at, 0:128]
            y = dot(left, jnp.concatenate([hi, lo, hi], axis=0))
            ys[pl.ds(mp * N + i, N, stride=OWN_LINE), :] = jnp.where(mask, y[:N], y[N:])
        return carry

    lax.fori_loop(0, PAIRS, pair, 0)

    def column(b, carry):
        at = pl.ds(pl.multiple_of(b * OWN_LINE, 8), PAIRS * N)
        hi, lo = split(ys[at, :])
        first = dot(wx[:, 0:320], hi)
        r = first[:64] + first[64:] + dot(wx[0:64, 0:320], lo)
        out[pl.ds(pl.multiple_of(b * N, N), N), :] = r[:N] + pltpu.roll(r[N:], 64, 1)
        return carry

    lax.fori_loop(0, N, column, 0, unroll=4)


def sides_pass(xkb, xka, wzb, wza, wy, wx, wx0, t_hi, t_lo, ya, yb, yc, out):
    mask = low_half(N)

    def pair(mp, carry):
        for xk, wz, base in ((xkb, wzb, 0), (xka, wza, 128)):
            weights = wz[pl.ds(pl.multiple_of(mp * 256, 256), 256), 0:192]
            for q in range(4):
                z = dot_t(xk[q * 256 : (q + 1) * 256, 0:192], weights)
                hi, lo = split(z)
                for odd in range(2):
                    t_hi[odd * 1024 + q * 256 : odd * 1024 + (q + 1) * 256, base : base + 128] = hi[
                        :, odd * 128 : (odd + 1) * 128
                    ]
                    t_lo[odd * 1024 + q * 256 : odd * 1024 + (q + 1) * 256, base : base + 128] = lo[
                        :, odd * 128 : (odd + 1) * 128
                    ]
        for odd in range(2):
            m = mp * 2 + odd
            left = wy[m, :, 0:96]

            for i in range(N):
                at = slice(odd * 1024 + i * N, odd * 1024 + (i + 1) * N)
                hi, lo = t_hi[at, :], t_lo[at, :]
                y = dot(left, jnp.concatenate([hi, lo, hi], axis=0))
                to = pl.ds(m * N + i, N, stride=SIDE_LINE)
                ya[to, :] = y[:N, :128]
                yb[to, :] = y[:N, 128:]
                yc[to, :] = jnp.where(mask, y[N : 2 * N, :128], y[2 * N :, 128:])
        return carry

    lax.fori_loop(0, PAIRS, pair, 0)

    def column(b, carry):
        at = pl.ds(pl.multiple_of(b * SIDE_LINE, 8), TERMS * N)
        rows = pl.ds(pl.multiple_of(b * N, N), N)
        hi, lo = split(ya[at, :])
        first = dot(wx[0:128, :], hi)
        r = first[:64] + first[64:128] + dot(wx[0:64, :], lo)
        out[rows, 0:128] = jnp.where(mask, r[:N], r[N:])
        hi, lo = split(yb[at, :])
        first = dot(wx[128:256, :], hi)
        r = first[:64] + first[64:128] + dot(wx[128:192, :], lo)
        out[rows, 128:256] = jnp.where(mask, r[:N], r[N:])
        hi, lo = split(yc[at, :])
        first = dot(wx0[...], hi)
        out[rows, 256:384] = first[:N] + first[N:] + dot(wx0[0:N, :], lo)
        return carry

    lax.fori_loop(0, N, column, 0, unroll=4)


def kernel(xs, wzo, wzb, wza, wys, wxo, wxs, wx0, sel, part, centre,
           t_hi, t_lo, yo, ya, yb, yc, terms):
    centre_pass(xs.at[0], wzo, wys, wxo, t_hi, t_lo, yo, centre)
    sides_pass(xs.at[1], xs.at[2], wzb, wza, wys, wxs, wx0, t_hi, t_lo, ya, yb, yc, terms)
    for q in range(4):
        rows = slice(q * 256, (q + 1) * 256)
        hi, lo = split(terms[rows, :])
        summed = dot(hi, sel[...]) + dot(lo, sel[...])
        for y in range(4):
            part[y, rows, :] = summed[:, y * 128 : (y + 1) * 128]


def convolve(xs, weights, sel):
    vm = pl.BlockSpec(memory_space=pltpu.VMEM)
    operands = (xs, *weights, sel)
    return pl.pallas_call(
        kernel,
        out_shape=(
            jax.ShapeDtypeStruct((4, 1024, 128), f32),
            jax.ShapeDtypeStruct((1024, 128), f32),
        ),
        in_specs=[vm] * len(operands),
        out_specs=(vm, vm),
        scratch_shapes=[
            pltpu.VMEM((2048, 256), bf16),
            pltpu.VMEM((2048, 256), bf16),
            pltpu.VMEM((N * OWN_LINE, 128), f32),
            pltpu.VMEM((N * SIDE_LINE, 128), f32),
            pltpu.VMEM((N * SIDE_LINE, 128), f32),
            pltpu.VMEM((N * SIDE_LINE, 128), f32),
            pltpu.VMEM((1024, 384), f32),
        ],
        compiler_params=pltpu.CompilerParams(vmem_limit_bytes=60 * 2**20),
    )(*operands)


def take(array, axis, places):
    return jnp.stack([lax.index_in_dim(array, k, axis, False) for k in places], axis)


def fold(f, hx, ht, wzo, wzb, wza, wys, wxo, wxs, wx0, k_hi, k_lo, folded, mats):
    def row(a, carry):
        hi, lo = split(hx[pl.ds(a, 1), :] * ht[...])
        at = pl.ds(pl.multiple_of(a * N, N), N)
        k_hi[at, :] = hi
        k_lo[at, :] = lo
        return carry

    lax.fori_loop(0, N, row, 0)
    f_hi, f_lo = split(f[...])
    for n in range(4):
        at = slice(n * 256, (n + 1) * 256)
        folded[:, at] = dot(f_hi, k_hi[:, at]) + dot(f_lo, k_hi[:, at]) + dot(f_hi, k_lo[:, at])
    for g in range(8):
        piece = folded[:, g * 128 : (g + 1) * 128]
        for k in range(4):
            turned = piece if k == 0 else pltpu.roll(piece, 128 - 32 * k, 1)
            mats[pl.ds(4 * g + k, 192, stride=N), :] = turned
    mask = lax.broadcasted_iota(jnp.int32, (N, 128), 1) < N

    def matrix(m, axis, offset):
        start = (m * 9 + axis * 3 + offset) * N
        v = mats[pl.ds(start if isinstance(m, int) else pl.multiple_of(start, N), N), :]
        return jnp.where(mask, v, 0.0)

    def parts(v):
        hi = v.astype(bf16).astype(f32)
        return hi, v - hi

    def term(m, carry):
        for t, offset in enumerate((1, 2, 0)):
            hi, lo = parts(matrix(m, 1, offset))
            wys[m, t * N : (t + 1) * N, :] = (hi + pltpu.roll(hi, 32, 1) + pltpu.roll(lo, 64, 1)).astype(bf16)
        for offset, places in ((0, ((wza, 0),)), (1, ((wzo, 0), (wzb, 0), (wza, 64))), (2, ((wzb, 64),))):
            hi, lo = parts(matrix(m, 2, offset))
            first = hi + pltpu.roll(hi, 64, 1)
            for ref, base in places:
                start = m * (64 if ref is wzo else 128) + base
                for p in range(2):
                    at = pl.ds(pl.multiple_of(start + p * N, N), N)
                    ref[at, 0:128] = (pltpu.roll(first, 32, 1) if p else first).astype(bf16)
                    ref[at, 128:256] = (pltpu.roll(lo, 32, 1) if p else lo).astype(bf16)
        return carry

    lax.fori_loop(0, TERMS, term, 0)

    def wide(terms, offset):
        total = None
        for k, m in enumerate(terms):
            v = matrix(m, 0, offset)
            v = pltpu.roll(v, 32 * k, 1) if k else v
            total = v if total is None else total + v
        return split(total)

    for g in range(5):
        at = slice(g * 128, (g + 1) * 128)
        for offset, places in ((2, ((wxs, 0, 64),)), (1, ((wxs, 32, 96), (wxs, 128, 192), (wx0, 0, 32))), (0, ((wxs, 160, 224),))):
            hi, lo = wide(range(4 * g, 4 * g + 4), offset)
            for ref, high_at, low_at in places:
                ref[high_at : high_at + N, at] = hi
                ref[low_at : low_at + N, at] = lo
    for g in range(3):
        at = slice(g * 128, (g + 1) * 128)
        for odd in range(2):
            hi, lo = wide([2 * mp + odd for mp in range(4 * g, min(4 * g + 4, PAIRS))], 1)
            wxo[odd * N : (odd + 1) * N, at] = hi
            wxo[64 + odd * N : 64 + (odd + 1) * N, at] = lo


MESH = pl.DeviceIdType.MESH
Y, CORES, ROWS = 4, 2, 16


def start_copy(src, dst, s, r, peer):
    copy = pltpu.make_async_remote_copy(
        src_ref=src, dst_ref=dst, send_sem=s, recv_sem=r, device_id=peer, device_id_type=MESH
    )
    copy.start()
    return copy


def greet(peers):
    barrier = pltpu.get_barrier_semaphore()
    for peer in peers:
        pl.semaphore_signal(barrier, inc=1, device_id=peer, device_id_type=MESH)
    pl.semaphore_wait(barrier, len(peers))


BOX_LINE = N + 8


def lay_out(boxes, lines, xs):
    piece = lax.broadcasted_iota(jnp.int32, (16, 128), 1) // 16

    def octant(at, carry):
        ox, oy, jh = at // 4, at // 2 % 2, at % 2
        rows = [boxes[p * 8 + ox * 4 + oy * 2 + oz, pl.ds(jh, 16, stride=2), :] for p in range(2) for oz in range(2)]
        for j in range(8):
            x = None
            for k in range(4):
                shift = (16 * (k - j)) % 128
                v = pltpu.roll(rows[k], shift, 1) if shift else rows[k]
                x = v if x is None else jnp.where(piece == k, v, x)
            lines[pl.ds(ox * 16 * BOX_LINE + oy * 16 + jh * 8 + j, 16, stride=BOX_LINE), :] = x
        return carry

    lax.fori_loop(0, 8, octant, 0)
    mask = low_half(N)

    def line(i, carry):
        v = lines[pl.ds(pl.multiple_of(i * BOX_LINE, 8), N), :]
        hi = v.astype(bf16).astype(f32)
        at = pl.ds(pl.multiple_of(i * N, N), N)
        xs[at, 0:128] = jnp.where(mask, hi, pltpu.roll(v - hi, 64, 1)).astype(bf16)
        xs[at, 128:256] = v.astype(bf16)
        return carry

    lax.fori_loop(0, N, line, 0, unroll=4)


def exchange_kernel(fine, tags, source, f, hx, ht, xs, came_from, wzo, wzb, wza, wys, wxo, wxs, wx0,
                    k_hi, k_lo, folded, mats, leaving, arrived, boxes, lines, s1, r1, s2, r2):
    row, col = lax.axis_index("row"), lax.axis_index("col")
    greet([((row + d) % ROWS, col) for d in range(1, ROWS)])
    copies = []
    for d in list(range(1, ROWS)) + [0]:
        to = (row + d) % ROWS
        target = arrived.at[row] if d == 0 else leaving.at[d]
        target[0:32, :] = fine[source[2 * to]]
        target[32:64, :] = fine[source[2 * to + 1]]
        target[64:72, :] = tags[to]
        if d:
            copies.append(start_copy(leaving.at[d], arrived.at[row], s1.at[d], r1.at[d], (to, col)))
    fold(f, hx, ht, wzo, wzb, wza, wys, wxo, wxs, wx0, k_hi, k_lo, folded, mats)
    for copy in copies:
        copy.wait_recv()

    def place(at, carry):
        wanted = at.astype(f32)
        total = [jnp.zeros((8, 128), f32)] * 4
        for k in range(ROWS):
            for s in range(2):
                hit = jnp.broadcast_to(arrived[k, 64 + s : 65 + s, :], (8, 128)) == wanted
                for c in range(4):
                    start = s * 32 + c * 8
                    total[c] = jnp.where(hit, arrived[k, start : start + 8, :], total[c])
        for c in range(4):
            boxes[0, at, c * 8 : (c + 1) * 8, :] = total[c]
        return carry

    lax.fori_loop(0, 16, place, 0)
    up, down = (row + 1) % ROWS, (row + ROWS - 1) % ROWS
    hops = [
        start_copy(boxes.at[0], boxes.at[1], s2.at[0], r2.at[0], (up, col)),
        start_copy(boxes.at[0], boxes.at[2], s2.at[1], r2.at[1], (down, col)),
    ]
    for k in range(ROWS):
        came_from[k] = arrived[k, 64:72, :]
    lay_out(boxes.at[0], lines, xs.at[0])
    for hop, k in zip(hops, (1, 2)):
        hop.wait_recv()
        lay_out(boxes.at[k], lines, xs.at[k])
    for copy in copies + hops:
        copy.wait_send()


def exchange(fine, tags, source, filter_matrix, kernel_ops):
    f = jnp.pad(kernel_ops.reshape(TERMS * 9, N * N), ((0, 12), (0, 0)))
    hx = jnp.repeat(filter_matrix, N, axis=1)
    ht = jnp.tile(filter_matrix, (1, N))
    vm = pl.BlockSpec(memory_space=pltpu.VMEM)
    sm = pl.BlockSpec(memory_space=pltpu.SMEM)
    shapes = ((1280, 256), (2560, 256), (2560, 256), (TERMS, 96, 128), (128, 384), (256, 640), (64, 640))
    shapes = tuple(jax.ShapeDtypeStruct(shape, bf16) for shape in shapes)
    outs = (jax.ShapeDtypeStruct((3, 1024, 256), bf16), jax.ShapeDtypeStruct((16, 8, 128), f32)) + shapes
    return pl.pallas_call(
        exchange_kernel,
        out_shape=outs,
        in_specs=[vm, vm, sm, vm, vm, vm],
        out_specs=(vm,) * len(outs),
        scratch_shapes=[
            pltpu.VMEM((1024, 1024), bf16),
            pltpu.VMEM((1024, 1024), bf16),
            pltpu.VMEM((192, 1024), f32),
            pltpu.VMEM((192 * N, 128), f32),
            pltpu.VMEM((16, 72, 128), f32),
            pltpu.VMEM((16, 72, 128), f32),
            pltpu.VMEM((3, 16, 32, 128), f32),
            pltpu.VMEM((N * BOX_LINE, 128), f32),
            pltpu.SemaphoreType.DMA((ROWS,)),
            pltpu.SemaphoreType.DMA((ROWS,)),
            pltpu.SemaphoreType.DMA((2,)),
            pltpu.SemaphoreType.DMA((2,)),
        ],
        compiler_params=pltpu.CompilerParams(
            collective_id=1, has_side_effects=True, vmem_limit_bytes=40 * 2**20
        ),
    )(fine, tags, source, f, hx, ht)


def return_kernel(part, centre, held, slot, out, from_core, pair_sum, from_y, total, from_half,
                  applied, boxes, leaving, back, s1, r1, s2, r2, s3, r3, s4, r4):
    row, col = lax.axis_index("row"), lax.axis_index("col")
    y, core = col // CORES, col % CORES
    sibling = y * CORES + (1 - core)
    peers = [(row, sibling)]
    peers += [(row, (y + 1 + d) % Y * CORES + core) for d in range(Y - 1)]
    peers += [((row + d) % ROWS, col) for d in range(1, ROWS)]
    greet(peers)
    mine = pl.ds(pl.multiple_of(core * 512, 512), 512)
    other = pl.ds(pl.multiple_of((1 - core) * 512, 512), 512)

    order = [(y + 1 + d) % Y for d in range(Y)]
    first = [
        start_copy(part.at[to, other], from_core.at[d], s1.at[d], r1.at[d], (row, sibling))
        for d, to in enumerate(order)
    ]
    second = []
    for d, to in enumerate(order):
        first[d].wait_recv()
        if d < Y - 1:
            pair_sum[d] = part[to, mine, :] + from_core[d]
            second.append(
                start_copy(pair_sum.at[d], from_y.at[d], s2.at[d], r2.at[d], (row, to * CORES + core))
            )
        else:
            total[...] = part[to, mine, :] + from_core[d]
    for copy in second:
        copy.wait_recv()
    total[...] = total[...] + from_y[0] + from_y[1] + from_y[2]
    third = start_copy(total, from_half, s3, r3, (row, sibling))

    def own_lanes(v):
        return jnp.where(core == 1, pltpu.roll(v, 64, 1), v)

    applied[mine, :] = own_lanes(total[...]) + centre[mine, :]
    third.wait_recv()
    applied[other, :] = own_lanes(from_half[...]) + centre[other, :]
    lanes = lax.broadcasted_iota(jnp.int32, (16, 128), 1) // 16
    for ox in range(2):
        for oy in range(2):
            for jh in range(2):
                lines = [
                    applied[pl.ds((oy * 16 + jh * 8 + j) * N + ox * 16, 16), :] for j in range(8)
                ]
                for p in range(2):
                    for oz in range(2):
                        base = p * 32 + oz * 16
                        box = None
                        for j in range(8):
                            shift = (16 * j - base) % 128
                            v = pltpu.roll(lines[j], shift, 1) if shift else lines[j]
                            box = v if box is None else jnp.where(lanes == j, v, box)
                        boxes[p * 8 + ox * 4 + oy * 2 + oz, pl.ds(jh, 16, stride=2), :] = box
    fourth = []
    for d in range(1, ROWS):
        to = (row + d) % ROWS
        for s in range(2):
            leaving[d * 2 + s] = boxes[held[to * 2 + s]]
        fourth.append(
            start_copy(
                leaving.at[pl.ds(d * 2, 2)],
                back.at[pl.ds(row * 2, 2)],
                s4.at[d],
                r4.at[d],
                (to, col),
            )
        )
    for s in range(2):
        back[row * 2 + s] = boxes[held[row * 2 + s]]
    for copy in fourth:
        copy.wait_recv()
    for q in range(16):
        out[q] = back[slot[q]]
    for copy in first + second + [third] + fourth:
        copy.wait_send()


def gather_back(part, centre, held, slot):
    vm = pl.BlockSpec(memory_space=pltpu.VMEM)
    sm = pl.BlockSpec(memory_space=pltpu.SMEM)
    sems = [pltpu.SemaphoreType.DMA((n,)) for n in (4, 4, 3, 3)]
    sems += [pltpu.SemaphoreType.DMA, pltpu.SemaphoreType.DMA]
    sems += [pltpu.SemaphoreType.DMA((ROWS,)), pltpu.SemaphoreType.DMA((ROWS,))]
    return pl.pallas_call(
        return_kernel,
        out_shape=jax.ShapeDtypeStruct((16, 32, 128), f32),
        in_specs=[vm, vm, sm, sm],
        out_specs=vm,
        scratch_shapes=[
            pltpu.VMEM((4, 512, 128), f32),
            pltpu.VMEM((3, 512, 128), f32),
            pltpu.VMEM((3, 512, 128), f32),
            pltpu.VMEM((512, 128), f32),
            pltpu.VMEM((512, 128), f32),
            pltpu.VMEM((1024, 128), f32),
            pltpu.VMEM((16, 32, 128), f32),
            pltpu.VMEM((32, 32, 128), f32),
            pltpu.VMEM((32, 32, 128), f32),
        ]
        + sems,
        compiler_params=pltpu.CompilerParams(
            collective_id=2, has_side_effects=True, vmem_limit_bytes=32 * 2**20
        ),
    )(part, centre, held, slot)


def selection(neighbours, col_index):
    order = (1, 5, 4, 0, 3, 2)
    sender = take(neighbours, 1, order)
    within = sender % 16 - col_index * 2
    hit = (sender >= 0)[:, :, None] & (within[:, :, None] == jnp.arange(2)[None, None, :])
    hit = jnp.transpose(hit, (1, 2, 0)).astype(bf16)
    return (
        hit[:, :, None, :, None] * jnp.eye(N, dtype=bf16)[None, None, :, None, :]
    ).reshape(384, 512)


def local(fine_coeffs, fine_slot, neighbours, filter_matrix, kernel_ops):
    held_boxes, volume = fine_coeffs.shape
    dest_row = fine_slot // 128
    item = jnp.arange(held_boxes)
    earlier = (dest_row[None, :] == dest_row[:, None]) & (item[None, :] < item[:, None])
    slot_index = dest_row * 2 + jnp.sum(earlier.astype(jnp.int32), axis=1)
    packer = jnp.arange(2 * ROWS)[:, None] == slot_index[None, :]
    source = jnp.sum(jnp.where(packer, item[None, :], 0), axis=1)
    places = jnp.max(jnp.where(packer, fine_slot[None, :] % 16, -1), axis=1).astype(f32)
    tags = jnp.broadcast_to(places.reshape(ROWS, 2, 1), (ROWS, 2, 128))
    tags = jnp.pad(tags, ((0, 0), (0, 6), (0, 0)))
    boxes = fine_coeffs.reshape(held_boxes, 32, 128)
    xs, came_from, *weights = exchange(boxes, tags, source, filter_matrix, kernel_ops)
    part, centre = convolve(xs, weights, selection(neighbours, lax.axis_index("col")))
    held = jnp.maximum(came_from[:, 0:2, 0].reshape(2 * ROWS).astype(jnp.int32), 0)
    return gather_back(part, centre, held, slot_index).reshape(held_boxes, volume)


def solution(mesh):
    in_specs = (P(("row", "col"), None), P(("row", "col")), P("row", None), P(), P())
    out_specs = P(("row", "col"), None)
    return jax.shard_map(local, mesh=mesh, in_specs=in_specs, out_specs=out_specs, check_vma=False)
```

```python
import jax
import jax.numpy as jnp
from jax import lax
from jax.experimental import pallas as pl
from jax.experimental.pallas import tpu as pltpu
from jax.sharding import PartitionSpec as P

f32, bf16 = jnp.float32, jnp.bfloat16
TERMS, N, PAIRS = 20, 32, 10
SIDE_LINE, OWN_LINE, MAT_LINE = TERMS * N + 8, PAIRS * N + 8, N + 8


def split(x):
    hi = x.astype(bf16)
    return hi, (x - hi.astype(f32)).astype(bf16)


def dot(a, b):
    return jnp.dot(a, b, preferred_element_type=f32)


def dot_t(a, b):
    return lax.dot_general(a, b, (((1,), (1,)), ((), ())), preferred_element_type=f32)


def low_half(rows):
    return lax.broadcasted_iota(jnp.int32, (rows, 128), 1) < 64


def centre_pass(xk, wz, wy, wx, t_hi, t_lo, ys, out):
    mask = low_half(N)

    def pair(mp, carry):
        weights = wz[pl.ds(pl.multiple_of(mp * 128, 128), 128), 0:192]
        for q in range(4):
            z = dot_t(xk[q * 256 : (q + 1) * 256, 0:192], weights)
            hi, lo = split(z)
            t_hi[q * 256 : (q + 1) * 256, 0:128] = hi
            t_lo[q * 256 : (q + 1) * 256, 0:128] = lo
        left = jnp.concatenate([wy[mp * 2, 0:N, 0:96], wy[mp * 2 + 1, 0:N, 0:96]], axis=0)

        for i in range(N):
            at = slice(i * N, (i + 1) * N)
            hi, lo = t_hi[at, 0:128], t_lo[at, 0:128]
            y = dot(left, jnp.concatenate([hi, lo, hi], axis=0))
            ys[pl.ds(mp * N + i, N, stride=OWN_LINE), :] = jnp.where(mask, y[:N], y[N:])
        return carry

    lax.fori_loop(0, PAIRS, pair, 0)

    def column(b, carry):
        at = pl.ds(pl.multiple_of(b * OWN_LINE, 8), PAIRS * N)
        hi, lo = split(ys[at, :])
        first = dot(wx[:, 0:320], hi)
        r = first[:64] + first[64:] + dot(wx[0:64, 0:320], lo)
        out[pl.ds(pl.multiple_of(b * N, N), N), :] = r[:N] + pltpu.roll(r[N:], 64, 1)
        return carry

    lax.fori_loop(0, N, column, 0, unroll=4)


def sides_lines(xkb, xka, wzb, wza, wy, t_hi, t_lo, ya, yb, yc):
    mask = low_half(N)

    def pair(mp, carry):
        for xk, wz, base in ((xkb, wzb, 0), (xka, wza, 128)):
            weights = wz[pl.ds(pl.multiple_of(mp * 256, 256), 256), 0:192]
            for q in range(4):
                z = dot_t(xk[q * 256 : (q + 1) * 256, 0:192], weights)
                hi, lo = split(z)
                for odd in range(2):
                    t_hi[odd * 1024 + q * 256 : odd * 1024 + (q + 1) * 256, base : base + 128] = hi[
                        :, odd * 128 : (odd + 1) * 128
                    ]
                    t_lo[odd * 1024 + q * 256 : odd * 1024 + (q + 1) * 256, base : base + 128] = lo[
                        :, odd * 128 : (odd + 1) * 128
                    ]
        for odd in range(2):
            m = mp * 2 + odd
            left = wy[m, :, 0:96]

            for i in range(N):
                at = slice(odd * 1024 + i * N, odd * 1024 + (i + 1) * N)
                hi, lo = t_hi[at, :], t_lo[at, :]
                y = dot(left, jnp.concatenate([hi, lo, hi], axis=0))
                to = pl.ds(m * N + i, N, stride=SIDE_LINE)
                ya[to, :] = y[:N, :128]
                yb[to, :] = y[:N, 128:]
                yc[to, :] = jnp.where(mask, y[N : 2 * N, :128], y[2 * N :, 128:])
        return carry

    lax.fori_loop(0, PAIRS, pair, 0)


def sides_columns(first_b, wx, wx0, ya, yb, yc, out):
    mask = low_half(N)

    def column(k, carry):
        at = pl.ds(pl.multiple_of((first_b + k) * SIDE_LINE, 8), TERMS * N)
        rows = pl.ds(pl.multiple_of(k * N, N), N)
        hi, lo = split(ya[at, :])
        first = dot(wx[0:128, :], hi)
        r = first[:64] + first[64:128] + dot(wx[0:64, :], lo)
        out[rows, 0:128] = jnp.where(mask, r[:N], r[N:])
        hi, lo = split(yb[at, :])
        first = dot(wx[128:256, :], hi)
        r = first[:64] + first[64:128] + dot(wx[128:192, :], lo)
        out[rows, 128:256] = jnp.where(mask, r[:N], r[N:])
        hi, lo = split(yc[at, :])
        first = dot(wx0[...], hi)
        out[rows, 256:384] = first[:N] + first[N:] + dot(wx0[0:N, :], lo)
        return carry

    lax.fori_loop(0, 8, column, 0, unroll=4)


def fold(f, hx, ht, folded, kron, mats):
    def row(a, carry):
        wide = hx[pl.ds(a, 1), :]
        for g in range(8):
            at = pl.ds(pl.multiple_of(g * 1024 + a * N, N), N)
            kron[at, :] = wide[:, g * 128 : (g + 1) * 128] * ht[...]
        return carry

    lax.fori_loop(0, N, row, 0, unroll=4)
    f_hi, f_lo = split(f[...])
    for n in range(4):
        left, right = split(kron[2048 * n : 2048 * n + 1024, :]), split(kron[2048 * n + 1024 : 2048 * n + 2048, :])
        hi, lo = jnp.concatenate([left[0], right[0]], axis=1), jnp.concatenate([left[1], right[1]], axis=1)
        folded[:, n * 256 : (n + 1) * 256] = dot(f_hi, hi) + dot(f_lo, hi) + dot(f_hi, lo)
    for g in range(8):
        piece = folded[:, g * 128 : (g + 1) * 128]
        for k in range(4):
            turned = piece if k == 0 else pltpu.roll(piece, 128 - 32 * k, 1)
            mats[pl.ds(4 * g + k, 192, stride=MAT_LINE), :] = turned


def pack(mats, wzo, wzb, wza, wys, wxo, wxs, wx0):
    mask = lax.broadcasted_iota(jnp.int32, (N, 128), 1) < N

    def matrix(m, axis, offset):
        start = (m * 9 + axis * 3 + offset) * MAT_LINE
        v = mats[pl.ds(start if isinstance(m, int) else pl.multiple_of(start, 8), N), :]
        return jnp.where(mask, v, 0.0)

    def parts(v):
        hi = v.astype(bf16).astype(f32)
        return hi, v - hi

    def term(m, carry):
        for t, offset in enumerate((1, 2, 0)):
            hi, lo = parts(matrix(m, 1, offset))
            wys[m, t * N : (t + 1) * N, :] = (hi + pltpu.roll(hi, 32, 1) + pltpu.roll(lo, 64, 1)).astype(bf16)
        for offset, places in ((0, ((wza, 0),)), (1, ((wzo, 0), (wzb, 0), (wza, 64))), (2, ((wzb, 64),))):
            hi, lo = parts(matrix(m, 2, offset))
            first = hi + pltpu.roll(hi, 64, 1)
            for ref, base in places:
                start = m * (64 if ref is wzo else 128) + base
                for p in range(2):
                    at = pl.ds(pl.multiple_of(start + p * N, N), N)
                    ref[at, 0:128] = (pltpu.roll(first, 32, 1) if p else first).astype(bf16)
                    ref[at, 128:256] = (pltpu.roll(lo, 32, 1) if p else lo).astype(bf16)
        return carry

    lax.fori_loop(0, TERMS, term, 0)

    def wide(terms, offset):
        total = None
        for k, m in enumerate(terms):
            v = matrix(m, 0, offset)
            v = pltpu.roll(v, 32 * k, 1) if k else v
            total = v if total is None else total + v
        return split(total)

    for g in range(5):
        at = slice(g * 128, (g + 1) * 128)
        for offset, places in ((2, ((wxs, 0, 64),)), (1, ((wxs, 32, 96), (wxs, 128, 192), (wx0, 0, 32))), (0, ((wxs, 160, 224),))):
            hi, lo = wide(range(4 * g, 4 * g + 4), offset)
            for ref, high_at, low_at in places:
                ref[high_at : high_at + N, at] = hi
                ref[low_at : low_at + N, at] = lo
    for g in range(3):
        at = slice(g * 128, (g + 1) * 128)
        for odd in range(2):
            hi, lo = wide([2 * mp + odd for mp in range(4 * g, min(4 * g + 4, PAIRS))], 1)
            wxo[odd * N : (odd + 1) * N, at] = hi
            wxo[64 + odd * N : 64 + (odd + 1) * N, at] = lo


MESH = pl.DeviceIdType.MESH
Y, CORES, ROWS = 4, 2, 16


def start_copy(src, dst, s, r, peer):
    copy = pltpu.make_async_remote_copy(
        src_ref=src, dst_ref=dst, send_sem=s, recv_sem=r, device_id=peer, device_id_type=MESH
    )
    copy.start()
    return copy


def greet(peers):
    barrier = pltpu.get_barrier_semaphore()
    for peer in peers:
        pl.semaphore_signal(barrier, inc=1, device_id=peer, device_id_type=MESH)
    pl.semaphore_wait(barrier, len(peers))


BOX_LINE = N + 8


def lay_out(boxes, lines, xs):
    piece = lax.broadcasted_iota(jnp.int32, (16, 128), 1) // 16

    def octant(at, carry):
        ox, oy, jh = at // 4, at // 2 % 2, at % 2
        rows = [boxes[p * 8 + ox * 4 + oy * 2 + oz, pl.ds(jh, 16, stride=2), :] for p in range(2) for oz in range(2)]
        for j in range(8):
            x = None
            for k in range(4):
                shift = (16 * (k - j)) % 128
                v = pltpu.roll(rows[k], shift, 1) if shift else rows[k]
                x = v if x is None else jnp.where(piece == k, v, x)
            lines[pl.ds(ox * 16 * BOX_LINE + oy * 16 + jh * 8 + j, 16, stride=BOX_LINE), :] = x
        return carry

    lax.fori_loop(0, 8, octant, 0)
    mask = low_half(N)

    def line(i, carry):
        v = lines[pl.ds(pl.multiple_of(i * BOX_LINE, 8), N), :]
        hi = v.astype(bf16).astype(f32)
        at = pl.ds(pl.multiple_of(i * N, N), N)
        xs[at, 0:128] = jnp.where(mask, hi, pltpu.roll(v - hi, 64, 1)).astype(bf16)
        xs[at, 128:256] = v.astype(bf16)
        return carry

    lax.fori_loop(0, N, line, 0, unroll=4)


def own_lanes(v, core):
    return jnp.where(core == 1, pltpu.roll(v, 64, 1), v)


def lay_back(applied, boxes):
    piece = lax.broadcasted_iota(jnp.int32, (16, 128), 1) // 16

    def octants(at, carry):
        ox, oy, jh = at // 4, at // 2 % 2, at % 2
        start = (oy * 16 + jh * 8) * N + ox * 16
        lines = [applied[pl.ds(pl.multiple_of(start + j * N, 16), 16), :] for j in range(8)]
        for p in range(2):
            for oz in range(2):
                box = None
                for j in range(8):
                    shift = (16 * j - p * 32 - oz * 16) % 128
                    v = pltpu.roll(lines[j], shift, 1) if shift else lines[j]
                    box = v if box is None else jnp.where(piece == j, v, box)
                boxes[p * 8 + ox * 4 + oy * 2 + oz, pl.ds(jh, 16, stride=2), :] = box
        return carry

    lax.fori_loop(0, 8, octants, 0)


def convolve_kernel(fine, tags, source, slot, f, hx, ht, hit, out,
                    wzo, wzb, wza, wys, wxo, wxs, wx0, sel, folded, leaving, arrived, boxes, lines, xs,
                    t_hi, t_lo, ya, yb, yc, terms, part, centre, from_core, pair_sum, from_y, total,
                    from_half, returned, back, s1, r1, s2, r2, s3, r3, s4, r4, s5, r5, s6, r6):
    row, col = lax.axis_index("row"), lax.axis_index("col")
    y, core = col // CORES, col % CORES
    sibling = (row, y * CORES + (1 - core))
    across = [(row, (y + 1 + d) % Y * CORES + core) for d in range(Y - 1)]
    greet([sibling] + across + [((row + d) % ROWS, col) for d in range(1, ROWS)])

    arrivals = []
    for d in list(range(1, ROWS)) + [0]:
        to = (row + d) % ROWS
        target = arrived.at[row] if d == 0 else leaving.at[d]
        target[0:32, :] = fine[source[2 * to]]
        target[32:64, :] = fine[source[2 * to + 1]]
        target[64:72, :] = tags[to]
        if d:
            arrivals.append(start_copy(leaving.at[d], arrived.at[row], s1.at[d], r1.at[d], (to, col)))
    fold(f, hx, ht, folded, yb, ya)
    for copy in arrivals:
        copy.wait_recv()

    def place(at, carry):
        wanted = at.astype(f32)
        total = [jnp.zeros((8, 128), f32)] * 4
        for k in range(ROWS):
            for s in range(2):
                hit = jnp.broadcast_to(arrived[k, 64 + s : 65 + s, :], (8, 128)) == wanted
                for c in range(4):
                    start = s * 32 + c * 8
                    total[c] = jnp.where(hit, arrived[k, start : start + 8, :], total[c])
        for c in range(4):
            boxes[0, at, c * 8 : (c + 1) * 8, :] = total[c]
        return carry

    lax.fori_loop(0, 16, place, 0)

    hops = [
        start_copy(boxes.at[0], boxes.at[1], s2.at[0], r2.at[0], ((row + 1) % ROWS, col)),
        start_copy(boxes.at[0], boxes.at[2], s2.at[1], r2.at[1], ((row + ROWS - 1) % ROWS, col)),
    ]
    pack(ya, wzo, wzb, wza, wys, wxo, wxs, wx0)
    same = lax.broadcasted_iota(jnp.int32, (N, 512), 1) % N == lax.broadcasted_iota(jnp.int32, (N, 512), 0)
    for k in range(12):
        sel[k * N : (k + 1) * N, :] = jnp.where(same, hit[k : k + 1, :], 0.0).astype(bf16)
    lay_out(boxes.at[0], lines, xs.at[0])
    for hop, k in zip(hops, (1, 2)):
        hop.wait_recv()
        lay_out(boxes.at[k], lines, xs.at[k])

    sides_lines(xs.at[1], xs.at[2], wzb, wza, wys, t_hi, t_lo, ya, yb, yc)
    mine = pl.ds(pl.multiple_of(core * 128, 128), 128)
    other = pl.ds(pl.multiple_of((1 - core) * 128, 128), 128)
    pairs, sums = [], []

    def over_pair(c):
        pairs[c].wait_recv()
        for d in range(Y):
            to = (y + 1 + d) % Y
            v = part[c, to, mine, :] + from_core[c, to]
            if d < Y - 1:
                pair_sum[c, d] = v
                k = c * (Y - 1) + d
                sums.append(start_copy(pair_sum.at[c, d], from_y.at[c, d], s4.at[k], r4.at[k], across[d]))
            else:
                total[c] = v

    for c in range(4):
        sides_columns(8 * c, wxs, wx0, ya, yb, yc, terms)
        hi, lo = split(terms[...])
        summed = dot(hi, sel[...]) + dot(lo, sel[...])
        for k in range(Y):
            part[c, k] = summed[:, k * 128 : (k + 1) * 128]
        pairs.append(start_copy(part.at[c, :, other], from_core.at[c], s3.at[c], r3.at[c], sibling))
        if c:
            over_pair(c - 1)
    over_pair(3)
    centre_pass(xs.at[0], wzo, wys, wxo, t_hi, t_lo, ya, centre)
    halves = []
    for c in range(4):
        for d in range(Y - 1):
            sums[c * (Y - 1) + d].wait_recv()
        total[c] = total[c] + from_y[c, 0] + from_y[c, 1] + from_y[c, 2]
        halves.append(start_copy(total.at[c], from_half.at[c], s5.at[c], r5.at[c], sibling))
    for c in range(4):
        at = pl.ds(pl.multiple_of(c * 256 + core * 128, 128), 128)
        centre[at, :] = centre[at, :] + own_lanes(total[c], core)
    for c in range(4):
        halves[c].wait_recv()
        at = pl.ds(pl.multiple_of(c * 256 + (1 - core) * 128, 128), 128)
        centre[at, :] = centre[at, :] + own_lanes(from_half[c], core)

    result = boxes.at[0]
    for hop in hops:
        hop.wait_send()
    lay_back(centre, result)

    def give_back(d, carry):
        to = (row + d) % ROWS
        for s in range(2):
            place = jnp.broadcast_to(arrived[to, pl.ds(64 + s, 1), :], (8, 128))
            hit = [place == float(k) for k in range(16)]
            for c in range(4):
                rows = slice(c * 8, (c + 1) * 8)
                v = result[0, rows, :]
                for k in range(1, 16):
                    v = jnp.where(hit[k], result[k, rows, :], v)
                returned[d * 2 + s, rows, :] = v
        return carry

    lax.fori_loop(0, ROWS, give_back, 0)
    returns = []
    for d in range(1, ROWS):
        src, dst = returned.at[pl.ds(2 * d, 2)], back.at[pl.ds(row * 2, 2)]
        returns.append(start_copy(src, dst, s6.at[d], r6.at[d], ((row + d) % ROWS, col)))
    for s in range(2):
        back[row * 2 + s] = returned[s]
    for copy in returns:
        copy.wait_recv()
    for q in range(16):
        out[q] = back[slot[q]]
    for copy in arrivals + pairs + sums + halves + returns:
        copy.wait_send()


def convolve(fine, tags, source, slot, filter_matrix, kernel_ops, hit):
    f = jnp.pad(kernel_ops.reshape(TERMS * 9, N * N), ((0, 12), (0, 0)))
    hx = jnp.repeat(filter_matrix, N, axis=1)
    ht = jnp.tile(filter_matrix, (1, 4))
    vm = pl.BlockSpec(memory_space=pltpu.VMEM)
    sm = pl.BlockSpec(memory_space=pltpu.SMEM)
    low = ((1280, 256), (2560, 256), (2560, 256), (TERMS, 96, 128), (128, 384), (256, 640), (64, 640), (384, 512))
    scratch = [pltpu.VMEM(shape, bf16) for shape in low]
    scratch += [pltpu.VMEM(shape, f32) for shape in ((192, 1024), (16, 72, 128), (16, 72, 128), (3, 16, 32, 128), (N * BOX_LINE, 128))]
    scratch += [pltpu.VMEM(shape, bf16) for shape in ((3, 1024, 256), (2048, 256), (2048, 256))]
    scratch += [pltpu.VMEM((N * SIDE_LINE, 128), f32)] * 3
    scratch += [
        pltpu.VMEM(shape, f32)
        for shape in (
            (256, 384), (4, 4, 256, 128), (1024, 128), (4, 4, 128, 128), (4, 3, 128, 128), (4, 3, 128, 128),
            (4, 128, 128), (4, 128, 128), (32, 32, 128), (32, 32, 128),
        )
    ]
    scratch += [pltpu.SemaphoreType.DMA((n,)) for n in (16, 16, 2, 2, 4, 4, 12, 12, 4, 4, 16, 16)]
    return pl.pallas_call(
        convolve_kernel,
        out_shape=jax.ShapeDtypeStruct((16, 32, 128), f32),
        in_specs=[vm, vm, sm, sm, vm, vm, vm, vm],
        out_specs=vm,
        scratch_shapes=scratch,
        compiler_params=pltpu.CompilerParams(
            collective_id=1, has_side_effects=True, vmem_limit_bytes=60 * 2**20
        ),
    )(fine, tags, source, slot, f, hx, ht, hit)


def hits(neighbours, col_index):
    order = (1, 5, 4, 0, 3, 2)
    sender = jnp.stack([neighbours[:, k] for k in order for p in range(2)])
    parent = (jnp.arange(12) % 2)[:, None] + col_index * 2
    hit = ((sender >= 0) & (sender % 16 == parent)).astype(f32)
    return jnp.repeat(hit, N, axis=1)


def local(fine_coeffs, fine_slot, neighbours, filter_matrix, kernel_ops):
    held_boxes, volume = fine_coeffs.shape
    dest_row = fine_slot // 128
    item = jnp.arange(held_boxes)
    earlier = (dest_row[None, :] == dest_row[:, None]) & (item[None, :] < item[:, None])
    slot_index = dest_row * 2 + jnp.sum(earlier.astype(jnp.int32), axis=1)
    packer = jnp.arange(2 * ROWS)[:, None] == slot_index[None, :]
    source = jnp.sum(jnp.where(packer, item[None, :], 0), axis=1)
    places = jnp.max(jnp.where(packer, fine_slot[None, :] % 16, -1), axis=1).astype(f32)
    tags = jnp.broadcast_to(places.reshape(ROWS, 2, 1), (ROWS, 2, 128))
    tags = jnp.pad(tags, ((0, 0), (0, 6), (0, 0)))
    boxes = fine_coeffs.reshape(held_boxes, 32, 128)
    hit = hits(neighbours, lax.axis_index("col"))
    out = convolve(boxes, tags, source, slot_index, filter_matrix, kernel_ops, hit)
    return out.reshape(held_boxes, volume)


def solution(mesh):
    in_specs = (P(("row", "col"), None), P(("row", "col")), P("row", None), P(), P())
    out_specs = P(("row", "col"), None)
    return jax.shard_map(local, mesh=mesh, in_specs=in_specs, out_specs=out_specs, check_vma=False)
```

```python
import jax
import jax.numpy as jnp
from jax import lax
from jax.experimental import pallas as pl
from jax.experimental.pallas import tpu as pltpu
from jax.sharding import PartitionSpec as P

f32, bf16 = jnp.float32, jnp.bfloat16
TERMS, N, PAIRS = 20, 32, 10
SIDE_LINE, OWN_LINE, MAT_LINE = TERMS * N + 8, PAIRS * N + 8, N + 8


def split(x):
    hi = x.astype(bf16)
    return hi, (x - hi.astype(f32)).astype(bf16)


def dot(a, b):
    return jnp.dot(a, b, preferred_element_type=f32)


def dot_t(a, b):
    return lax.dot_general(a, b, (((1,), (1,)), ((), ())), preferred_element_type=f32)


def low_half(rows):
    return lax.broadcasted_iota(jnp.int32, (rows, 128), 1) < 64


def centre_pass(xk, wz, wy, wx, t_hi, t_lo, ys, out):
    mask = low_half(N)

    def pair(mp, carry):
        weights = wz[pl.ds(pl.multiple_of(mp * 128, 128), 128), 0:192]
        for q in range(4):
            z = dot_t(xk[q * 256 : (q + 1) * 256, 0:192], weights)
            hi, lo = split(z)
            t_hi[q * 256 : (q + 1) * 256, 0:128] = hi
            t_lo[q * 256 : (q + 1) * 256, 0:128] = lo
        left = jnp.concatenate([wy[mp * 2, 0:N, 0:96], wy[mp * 2 + 1, 0:N, 0:96]], axis=0)

        for i in range(N):
            at = slice(i * N, (i + 1) * N)
            hi, lo = t_hi[at, 0:128], t_lo[at, 0:128]
            y = dot(left, jnp.concatenate([hi, lo, hi], axis=0))
            ys[pl.ds(mp * N + i, N, stride=OWN_LINE), :] = jnp.where(mask, y[:N], y[N:])
        return carry

    lax.fori_loop(0, PAIRS, pair, 0)

    def column(b, carry):
        at = pl.ds(pl.multiple_of(b * OWN_LINE, 8), PAIRS * N)
        hi, lo = split(ys[at, :])
        first = dot(wx[:, 0:320], hi)
        r = first[:64] + first[64:] + dot(wx[0:64, 0:320], lo)
        out[pl.ds(pl.multiple_of(b * N, N), N), :] = r[:N] + pltpu.roll(r[N:], 64, 1)
        return carry

    lax.fori_loop(0, N, column, 0, unroll=4)


def sides_lines(xkb, xka, wzb, wza, wy, t_hi, t_lo, ya, yb, yc):
    mask = low_half(N)

    def pair(mp, carry):
        for xk, wz, base in ((xkb, wzb, 0), (xka, wza, 128)):
            weights = wz[pl.ds(pl.multiple_of(mp * 256, 256), 256), 0:192]
            for q in range(4):
                z = dot_t(xk[q * 256 : (q + 1) * 256, 0:192], weights)
                hi, lo = split(z)
                for odd in range(2):
                    t_hi[odd * 1024 + q * 256 : odd * 1024 + (q + 1) * 256, base : base + 128] = hi[
                        :, odd * 128 : (odd + 1) * 128
                    ]
                    t_lo[odd * 1024 + q * 256 : odd * 1024 + (q + 1) * 256, base : base + 128] = lo[
                        :, odd * 128 : (odd + 1) * 128
                    ]
        for odd in range(2):
            m = mp * 2 + odd
            left = wy[m, :, 0:96]

            for i in range(N):
                at = slice(odd * 1024 + i * N, odd * 1024 + (i + 1) * N)
                hi, lo = t_hi[at, :], t_lo[at, :]
                y = dot(left, jnp.concatenate([hi, lo, hi], axis=0))
                to = pl.ds(m * N + i, N, stride=SIDE_LINE)
                ya[to, :] = y[:N, :128]
                yb[to, :] = y[:N, 128:]
                yc[to, :] = jnp.where(mask, y[N : 2 * N, :128], y[2 * N :, 128:])
        return carry

    lax.fori_loop(0, PAIRS, pair, 0)


def sides_columns(first_b, wx, wx0, ya, yb, yc, out):
    mask = low_half(N)

    def column(k, carry):
        at = pl.ds(pl.multiple_of((first_b + k) * SIDE_LINE, 8), TERMS * N)
        rows = pl.ds(pl.multiple_of(k * N, N), N)
        hi, lo = split(ya[at, :])
        first = dot(wx[0:128, :], hi)
        r = first[:64] + first[64:128] + dot(wx[0:64, :], lo)
        out[rows, 0:128] = jnp.where(mask, r[:N], r[N:])
        hi, lo = split(yb[at, :])
        first = dot(wx[128:256, :], hi)
        r = first[:64] + first[64:128] + dot(wx[128:192, :], lo)
        out[rows, 128:256] = jnp.where(mask, r[:N], r[N:])
        hi, lo = split(yc[at, :])
        first = dot(wx0[...], hi)
        out[rows, 256:384] = first[:N] + first[N:] + dot(wx0[0:N, :], lo)
        return carry

    lax.fori_loop(0, 8, column, 0, unroll=4)


def spread(h, lanes, pick):
    shape = (N, lanes)
    chosen = pick(lax.broadcasted_iota(jnp.int32, shape, 1)) == lax.broadcasted_iota(jnp.int32, shape, 0)
    chosen = jnp.where(chosen, 1.0, 0.0).astype(bf16)
    hi = split(h)[0]
    mid, low = split(h - hi.astype(f32))
    return dot(hi, chosen) + (dot(mid, chosen) + dot(low, chosen))


def fold(ops, h, f, hx, ht, folded, kron, mats):
    for k in range(9):
        f[k * 24 : k * 24 + TERMS, :] = ops[k // 3, k % 3]
        f[k * 24 + TERMS : (k + 1) * 24, :] = jnp.zeros((4, 1024), f32)
    hx[...] = spread(h[...], 1024, lambda lane: lane // N)
    ht[...] = spread(h[...], 128, lambda lane: lane % N)

    def row(a, carry):
        wide = hx[pl.ds(a, 1), :]
        for g in range(8):
            at = pl.ds(pl.multiple_of(g * 1024 + a * N, N), N)
            kron[at, :] = wide[:, g * 128 : (g + 1) * 128] * ht[...]
        return carry

    lax.fori_loop(0, N, row, 0, unroll=4)
    f_hi, f_lo = split(f[...])
    for n in range(4):
        left, right = split(kron[2048 * n : 2048 * n + 1024, :]), split(kron[2048 * n + 1024 : 2048 * n + 2048, :])
        hi, lo = jnp.concatenate([left[0], right[0]], axis=1), jnp.concatenate([left[1], right[1]], axis=1)
        folded[:, n * 256 : (n + 1) * 256] = dot(f_hi, hi) + dot(f_lo, hi) + dot(f_hi, lo)
    for g in range(8):
        piece = folded[:, g * 128 : (g + 1) * 128]
        for k in range(4):
            turned = piece if k == 0 else pltpu.roll(piece, 128 - 32 * k, 1)
            mats[pl.ds(4 * g + k, 216, stride=MAT_LINE), :] = turned


def pack(mats, wzo, wzb, wza, wys, wxo, wxs, wx0):
    mask = lax.broadcasted_iota(jnp.int32, (N, 128), 1) < N

    def matrix(m, axis, offset):
        start = ((axis * 3 + offset) * 24 + m) * MAT_LINE
        v = mats[pl.ds(start if isinstance(m, int) else pl.multiple_of(start, 8), N), :]
        return jnp.where(mask, v, 0.0)

    def parts(v):
        hi = v.astype(bf16).astype(f32)
        return hi, v - hi

    def term(m, carry):
        for t, offset in enumerate((1, 2, 0)):
            hi, lo = parts(matrix(m, 1, offset))
            wys[m, t * N : (t + 1) * N, :] = (hi + pltpu.roll(hi, 32, 1) + pltpu.roll(lo, 64, 1)).astype(bf16)
        for offset, places in ((0, ((wza, 0),)), (1, ((wzo, 0), (wzb, 0), (wza, 64))), (2, ((wzb, 64),))):
            hi, lo = parts(matrix(m, 2, offset))
            first = hi + pltpu.roll(hi, 64, 1)
            for ref, base in places:
                start = m * (64 if ref is wzo else 128) + base
                for p in range(2):
                    at = pl.ds(pl.multiple_of(start + p * N, N), N)
                    ref[at, 0:128] = (pltpu.roll(first, 32, 1) if p else first).astype(bf16)
                    ref[at, 128:256] = (pltpu.roll(lo, 32, 1) if p else lo).astype(bf16)
        return carry

    lax.fori_loop(0, TERMS, term, 0)

    def wide(terms, offset):
        total = None
        for k, m in enumerate(terms):
            v = matrix(m, 0, offset)
            v = pltpu.roll(v, 32 * k, 1) if k else v
            total = v if total is None else total + v
        return split(total)

    for g in range(5):
        at = slice(g * 128, (g + 1) * 128)
        for offset, places in ((2, ((wxs, 0, 64),)), (1, ((wxs, 32, 96), (wxs, 128, 192), (wx0, 0, 32))), (0, ((wxs, 160, 224),))):
            hi, lo = wide(range(4 * g, 4 * g + 4), offset)
            for ref, high_at, low_at in places:
                ref[high_at : high_at + N, at] = hi
                ref[low_at : low_at + N, at] = lo
    for g in range(3):
        at = slice(g * 128, (g + 1) * 128)
        for odd in range(2):
            hi, lo = wide([2 * mp + odd for mp in range(4 * g, min(4 * g + 4, PAIRS))], 1)
            wxo[odd * N : (odd + 1) * N, at] = hi
            wxo[64 + odd * N : 64 + (odd + 1) * N, at] = lo


MESH = pl.DeviceIdType.MESH
Y, CORES, ROWS = 4, 2, 16


def start_copy(src, dst, s, r, peer):
    copy = pltpu.make_async_remote_copy(
        src_ref=src, dst_ref=dst, send_sem=s, recv_sem=r, device_id=peer, device_id_type=MESH
    )
    copy.start()
    return copy


def greet(peers):
    barrier = pltpu.get_barrier_semaphore()
    for peer in peers:
        pl.semaphore_signal(barrier, inc=1, device_id=peer, device_id_type=MESH)
    pl.semaphore_wait(barrier, len(peers))


BOX_LINE = N + 8


def lay_out(boxes, lines, xs):
    piece = lax.broadcasted_iota(jnp.int32, (16, 128), 1) // 16

    def octant(at, carry):
        ox, oy, jh = at // 4, at // 2 % 2, at % 2
        rows = [boxes[p * 8 + ox * 4 + oy * 2 + oz, pl.ds(jh, 16, stride=2), :] for p in range(2) for oz in range(2)]
        for j in range(8):
            x = None
            for k in range(4):
                shift = (16 * (k - j)) % 128
                v = pltpu.roll(rows[k], shift, 1) if shift else rows[k]
                x = v if x is None else jnp.where(piece == k, v, x)
            lines[pl.ds(ox * 16 * BOX_LINE + oy * 16 + jh * 8 + j, 16, stride=BOX_LINE), :] = x
        return carry

    lax.fori_loop(0, 8, octant, 0)
    mask = low_half(N)

    def line(i, carry):
        v = lines[pl.ds(pl.multiple_of(i * BOX_LINE, 8), N), :]
        hi = v.astype(bf16).astype(f32)
        at = pl.ds(pl.multiple_of(i * N, N), N)
        xs[at, 0:128] = jnp.where(mask, hi, pltpu.roll(v - hi, 64, 1)).astype(bf16)
        xs[at, 128:256] = v.astype(bf16)
        return carry

    lax.fori_loop(0, N, line, 0, unroll=4)


def lay_back(applied, boxes):
    piece = lax.broadcasted_iota(jnp.int32, (16, 128), 1) // 16

    def octants(at, carry):
        ox, oy, jh = at // 4, at // 2 % 2, at % 2
        start = (oy * 16 + jh * 8) * N + ox * 16
        lines = [applied[pl.ds(pl.multiple_of(start + j * N, 16), 16), :] for j in range(8)]
        for p in range(2):
            for oz in range(2):
                box = None
                for j in range(8):
                    shift = (16 * j - p * 32 - oz * 16) % 128
                    v = pltpu.roll(lines[j], shift, 1) if shift else lines[j]
                    box = v if box is None else jnp.where(piece == j, v, box)
                boxes[p * 8 + ox * 4 + oy * 2 + oz, pl.ds(jh, 16, stride=2), :] = box
        return carry

    lax.fori_loop(0, 8, octants, 0)


def choose(neighbours, col, sel):
    lane = lax.broadcasted_iota(jnp.int32, (N, 128), 1)
    same = lane % N == lax.broadcasted_iota(jnp.int32, (N, 128), 0)
    for d, k in enumerate((1, 5, 4, 0, 3, 2)):
        for g in range(4):
            held = None
            for n in range(4):
                sender = neighbours[k, (g % 2 * 2 + n // 2) * 4 + g // 2 * 2 + n % 2]
                v = jnp.where(sender >= 0, sender % 16 - 2 * col, -1)
                held = v if held is None else jnp.where(lane // N == n, v, held)
            for p in range(2):
                at = slice((d * 2 + p) * N, (d * 2 + p + 1) * N)
                sel[at, g * 128 : (g + 1) * 128] = jnp.where(same & (held == p), 1.0, 0.0).astype(bf16)


def convolve_kernel(fine, slot, neighbours, ops, h, out, own, f, hx, ht,
                    wzo, wzb, wza, wys, wxo, wxs, wx0, sel, folded, leaving, arrived, boxes, lines, xs,
                    t_hi, t_lo, ya, yb, yc, terms, part, centre, from_core, pair_sum, from_y, total,
                    returned, back, s1, r1, s2, r2, s3, r3, s4, r4, s6, r6):
    row, col = lax.axis_index("row"), lax.axis_index("col")
    y, core = col // CORES, col % CORES
    sibling = (row, y * CORES + (1 - core))
    across = [(row, (y + 1 + d) % Y * CORES + core) for d in range(Y - 1)]
    greet([sibling] + across + [((row + d) % ROWS, col) for d in range(1, ROWS)])

    for q in range(16):
        own[q] = fine[pl.ds(q // 8 * 256 + q % 8, N, stride=8), :]
    slots = [slot[q] for q in range(16)]
    dest = [v // 128 for v in slots]
    first_row = lax.broadcasted_iota(jnp.int32, (8, 128), 0) == 0
    arrivals = []
    for d in list(range(1, ROWS)) + [0]:
        to = (row + d) % ROWS
        target = arrived.at[row] if d == 0 else leaving.at[d]
        first, last = jnp.int32(16), jnp.int32(-1)
        for q in range(16):
            here = dest[q] == to
            first = jnp.minimum(first, jnp.where(here, q, 16))
            last = jnp.maximum(last, jnp.where(here, q, -1))
        tag = []
        for k, q in enumerate((jnp.minimum(first, 15), jnp.maximum(last, 0))):
            target[k * N : (k + 1) * N, :] = own[q]
            tag.append(jnp.where(last >= 0, slot[q] % 16, -1).astype(f32))
        target[64:72, :] = jnp.where(first_row, tag[0], tag[1])
        if d:
            arrivals.append(start_copy(leaving.at[d], arrived.at[row], s1.at[d], r1.at[d], (to, col)))
    fold(ops, h, f, hx, ht, folded, yb, ya)
    for copy in arrivals:
        copy.wait_recv()

    def place(at, carry):
        wanted = at.astype(f32)
        total = [jnp.zeros((8, 128), f32)] * 4
        for k in range(ROWS):
            for s in range(2):
                hit = jnp.broadcast_to(arrived[k, 64 + s : 65 + s, :], (8, 128)) == wanted
                for c in range(4):
                    start = s * 32 + c * 8
                    total[c] = jnp.where(hit, arrived[k, start : start + 8, :], total[c])
        for c in range(4):
            boxes[0, at, c * 8 : (c + 1) * 8, :] = total[c]
        return carry

    lax.fori_loop(0, 16, place, 0)

    hops = [
        start_copy(boxes.at[0], boxes.at[1], s2.at[0], r2.at[0], ((row + 1) % ROWS, col)),
        start_copy(boxes.at[0], boxes.at[2], s2.at[1], r2.at[1], ((row + ROWS - 1) % ROWS, col)),
    ]
    pack(ya, wzo, wzb, wza, wys, wxo, wxs, wx0)
    choose(neighbours, col, sel)
    lay_out(boxes.at[0], lines, xs.at[0])
    for hop, k in zip(hops, (1, 2)):
        hop.wait_recv()
        lay_out(boxes.at[k], lines, xs.at[k])

    sides_lines(xs.at[1], xs.at[2], wzb, wza, wys, t_hi, t_lo, ya, yb, yc)
    pairs, sums = [], []
    mask = low_half(128)

    def over_pair(c):
        pairs[c].wait_recv()
        for d in range(Y):
            to = (y + 1 + d) % Y
            v = part[c, core, to // 2] + from_core[c, to // 2]
            odd = to % 2 == 1
            low = jnp.where(odd, pltpu.roll(v[:128], 64, 1), v[:128])
            high = jnp.where(odd, v[128:], pltpu.roll(v[128:], 64, 1))
            v = jnp.where(mask, low, high)
            if d < Y - 1:
                pair_sum[c, d] = v
                k = c * (Y - 1) + d
                sums.append(start_copy(pair_sum.at[c, d], from_y.at[c, d], s4.at[k], r4.at[k], across[d]))
            else:
                total[c] = v

    for c in range(4):
        sides_columns(8 * c, wxs, wx0, ya, yb, yc, terms)
        hi, lo = split(terms[...])
        summed = dot(hi, sel[...]) + dot(lo, sel[...])
        for k in range(Y):
            part[c, k // 2, k % 2] = summed[:, k * 128 : (k + 1) * 128]
        pairs.append(start_copy(part.at[c, 1 - core], from_core.at[c], s3.at[c], r3.at[c], sibling))
        if c:
            over_pair(c - 1)
    over_pair(3)
    centre_pass(xs.at[0], wzo, wys, wxo, t_hi, t_lo, ya, centre)
    for c in range(4):
        for d in range(Y - 1):
            sums[c * (Y - 1) + d].wait_recv()
        v = total[c] + from_y[c, 0] + from_y[c, 1] + from_y[c, 2]
        at = slice(c * 256, c * 256 + 128)
        centre[at, :] = centre[at, :] + v
        at = slice(c * 256 + 128, c * 256 + 256)
        centre[at, :] = centre[at, :] + pltpu.roll(v, 64, 1)

    result = boxes.at[0]
    for hop in hops:
        hop.wait_send()
    lay_back(centre, result)

    def give_back(d, carry):
        to = (row + d) % ROWS
        for s in range(2):
            place = jnp.broadcast_to(arrived[to, pl.ds(64 + s, 1), :], (8, 128))
            hit = [place == float(k) for k in range(16)]
            for c in range(4):
                rows = slice(c * 8, (c + 1) * 8)
                v = result[0, rows, :]
                for k in range(1, 16):
                    v = jnp.where(hit[k], result[k, rows, :], v)
                returned[d * 2 + s, rows, :] = v
        return carry

    lax.fori_loop(0, ROWS, give_back, 0)
    returns = []
    for d in range(1, ROWS):
        src, dst = returned.at[pl.ds(2 * d, 2)], back.at[pl.ds(row * 2, 2)]
        returns.append(start_copy(src, dst, s6.at[d], r6.at[d], ((row + d) % ROWS, col)))
    for s in range(2):
        back[row * 2 + s] = returned[s]
    for copy in returns:
        copy.wait_recv()
    for q in range(16):
        earlier = jnp.int32(0)
        for k in range(q):
            earlier = jnp.where(dest[k] == dest[q], 1, earlier)
        out[pl.ds(q // 8 * 256 + q % 8, N, stride=8), :] = back[2 * dest[q] + earlier]
    for copy in arrivals + pairs + sums + returns:
        copy.wait_send()


def convolve(fine, slot, neighbours, kernel_ops, filter_matrix):
    vm = pl.BlockSpec(memory_space=pltpu.VMEM)
    sm = pl.BlockSpec(memory_space=pltpu.SMEM)
    low = ((1280, 256), (2560, 256), (2560, 256), (TERMS, 96, 128), (128, 384), (256, 640), (64, 640), (384, 512))
    scratch = [pltpu.VMEM(shape, f32) for shape in ((16, 32, 128), (216, 1024), (32, 1024), (32, 128))]
    scratch += [pltpu.VMEM(shape, bf16) for shape in low]
    scratch += [pltpu.VMEM(shape, f32) for shape in ((216, 1024), (16, 72, 128), (16, 72, 128), (3, 16, 32, 128), (N * BOX_LINE, 128))]
    scratch += [pltpu.VMEM(shape, bf16) for shape in ((3, 1024, 256), (2048, 256), (2048, 256))]
    scratch += [pltpu.VMEM((N * SIDE_LINE, 128), f32)] * 3
    scratch += [
        pltpu.VMEM(shape, f32)
        for shape in (
            (256, 384), (4, 2, 2, 256, 128), (1024, 128), (4, 2, 256, 128), (4, 3, 128, 128), (4, 3, 128, 128),
            (4, 128, 128), (32, 32, 128), (32, 32, 128),
        )
    ]
    scratch += [pltpu.SemaphoreType.DMA((n,)) for n in (16, 16, 2, 2, 4, 4, 12, 12, 16, 16)]
    return pl.pallas_call(
        convolve_kernel,
        out_shape=jax.ShapeDtypeStruct((512, 128), f32),
        in_specs=[vm, sm, sm, vm, vm],
        out_specs=vm,
        scratch_shapes=scratch,
        compiler_params=pltpu.CompilerParams(
            collective_id=1, has_side_effects=True, vmem_limit_bytes=60 * 2**20
        ),
    )(fine, slot, neighbours, kernel_ops, filter_matrix)


def local(fine_coeffs, fine_slot, neighbours, filter_matrix, kernel_ops):
    held_boxes, volume = fine_coeffs.shape
    boxes = jnp.transpose(fine_coeffs.reshape(2, 8, 32, 128), (0, 2, 1, 3)).reshape(512, 128)
    out = convolve(boxes, fine_slot, neighbours.T, jnp.transpose(kernel_ops, (1, 2, 0, 3)), filter_matrix)
    return jnp.transpose(out.reshape(2, 32, 8, 128), (0, 2, 1, 3)).reshape(held_boxes, volume)


def solution(mesh):
    in_specs = (P(("row", "col"), None), P(("row", "col")), P("row", None), P(), P())
    out_specs = P(("row", "col"), None)
    return jax.shard_map(local, mesh=mesh, in_specs=in_specs, out_specs=out_specs, check_vma=False)
```

```python
import jax
import jax.numpy as jnp
from jax import lax
from jax.experimental import pallas as pl
from jax.experimental.pallas import tpu as pltpu
from jax.sharding import PartitionSpec as P

f32, bf16 = jnp.float32, jnp.bfloat16
TERMS, N, PAIRS = 20, 32, 10
SIDE_LINE, OWN_LINE, MAT_LINE = TERMS * N + 8, PAIRS * N + 8, N + 8


def split(x):
    hi = x.astype(bf16)
    return hi, (x - hi.astype(f32)).astype(bf16)


def dot(a, b):
    return jnp.dot(a, b, preferred_element_type=f32)


def dot_t(a, b):
    return lax.dot_general(a, b, (((1,), (1,)), ((), ())), preferred_element_type=f32)


def low_half(rows):
    return lax.broadcasted_iota(jnp.int32, (rows, 128), 1) < 64


def centre_pass(xk, wz, wy, wx, t_hi, t_lo, ys, out):
    mask = low_half(N)

    def pair(mp, carry):
        weights = wz[pl.ds(pl.multiple_of(mp * 128, 128), 128), 0:192]
        for q in range(4):
            z = dot_t(xk[q * 256 : (q + 1) * 256, 0:192], weights)
            hi, lo = split(z)
            t_hi[q * 256 : (q + 1) * 256, 0:128] = hi
            t_lo[q * 256 : (q + 1) * 256, 0:128] = lo
        left = jnp.concatenate([wy[mp * 2, 0:N, 0:96], wy[mp * 2 + 1, 0:N, 0:96]], axis=0)

        for i in range(N):
            at = slice(i * N, (i + 1) * N)
            hi, lo = t_hi[at, 0:128], t_lo[at, 0:128]
            y = dot(left, jnp.concatenate([hi, lo, hi], axis=0))
            ys[pl.ds(mp * N + i, N, stride=OWN_LINE), :] = jnp.where(mask, y[:N], y[N:])
        return carry

    lax.fori_loop(0, PAIRS, pair, 0)

    def column(b, carry):
        at = pl.ds(pl.multiple_of(b * OWN_LINE, 8), PAIRS * N)
        hi, lo = split(ys[at, :])
        first = dot(wx[:, 0:320], hi)
        r = first[:64] + first[64:] + dot(wx[0:64, 0:320], lo)
        out[pl.ds(pl.multiple_of(b * N, N), N), :] = r[:N] + pltpu.roll(r[N:], 64, 1)
        return carry

    lax.fori_loop(0, N, column, 0, unroll=4)


def sides_lines(xkb, xka, wzb, wza, wy, t_hi, t_lo, ya, yb, yc):
    mask = low_half(N)

    def pair(mp, carry):
        for xk, wz, base in ((xkb, wzb, 0), (xka, wza, 128)):
            weights = wz[pl.ds(pl.multiple_of(mp * 256, 256), 256), 0:192]
            for q in range(4):
                z = dot_t(xk[q * 256 : (q + 1) * 256, 0:192], weights)
                hi, lo = split(z)
                for odd in range(2):
                    t_hi[odd * 1024 + q * 256 : odd * 1024 + (q + 1) * 256, base : base + 128] = hi[
                        :, odd * 128 : (odd + 1) * 128
                    ]
                    t_lo[odd * 1024 + q * 256 : odd * 1024 + (q + 1) * 256, base : base + 128] = lo[
                        :, odd * 128 : (odd + 1) * 128
                    ]
        for odd in range(2):
            m = mp * 2 + odd
            left = wy[m, :, 0:96]

            for i in range(N):
                at = slice(odd * 1024 + i * N, odd * 1024 + (i + 1) * N)
                hi, lo = t_hi[at, :], t_lo[at, :]
                y = dot(left, jnp.concatenate([hi, lo, hi], axis=0))
                to = pl.ds(m * N + i, N, stride=SIDE_LINE)
                ya[to, :] = y[:N, :128]
                yb[to, :] = y[:N, 128:]
                yc[to, :] = jnp.where(mask, y[N : 2 * N, :128], y[2 * N :, 128:])
        return carry

    lax.fori_loop(0, PAIRS, pair, 0)


def sides_columns(first_b, wx, wx0, ya, yb, yc, out):
    mask = low_half(N)

    def column(k, carry):
        at = pl.ds(pl.multiple_of((first_b + k) * SIDE_LINE, 8), TERMS * N)
        rows = pl.ds(pl.multiple_of(k * N, N), N)
        hi, lo = split(ya[at, :])
        first = dot(wx[0:128, :], hi)
        r = first[:64] + first[64:128] + dot(wx[0:64, :], lo)
        out[rows, 0:128] = jnp.where(mask, r[:N], r[N:])
        hi, lo = split(yb[at, :])
        first = dot(wx[128:256, :], hi)
        r = first[:64] + first[64:128] + dot(wx[128:192, :], lo)
        out[rows, 128:256] = jnp.where(mask, r[:N], r[N:])
        hi, lo = split(yc[at, :])
        first = dot(wx0[...], hi)
        out[rows, 256:384] = first[:N] + first[N:] + dot(wx0[0:N, :], lo)
        return carry

    lax.fori_loop(0, 8, column, 0, unroll=4)


def spread(h, lanes, pick):
    shape = (N, lanes)
    chosen = pick(lax.broadcasted_iota(jnp.int32, shape, 1)) == lax.broadcasted_iota(jnp.int32, shape, 0)
    chosen = jnp.where(chosen, 1.0, 0.0).astype(bf16)
    hi = split(h)[0]
    mid, low = split(h - hi.astype(f32))
    return dot(hi, chosen) + (dot(mid, chosen) + dot(low, chosen))


def fold(ops, h, f, hx, ht, folded, kron, mats):
    for k in range(9):
        f[k * 24 : k * 24 + TERMS, :] = ops[k // 3, k % 3]
        f[k * 24 + TERMS : (k + 1) * 24, :] = jnp.zeros((4, 1024), f32)
    hx[...] = spread(h[...], 1024, lambda lane: lane // N)
    ht[...] = spread(h[...], 128, lambda lane: lane % N)

    def row(a, carry):
        wide = hx[pl.ds(a, 1), :]
        for g in range(8):
            at = pl.ds(pl.multiple_of(g * 1024 + a * N, N), N)
            kron[at, :] = wide[:, g * 128 : (g + 1) * 128] * ht[...]
        return carry

    lax.fori_loop(0, N, row, 0, unroll=4)
    f_hi, f_lo = split(f[...])
    for n in range(4):
        left, right = split(kron[2048 * n : 2048 * n + 1024, :]), split(kron[2048 * n + 1024 : 2048 * n + 2048, :])
        hi, lo = jnp.concatenate([left[0], right[0]], axis=1), jnp.concatenate([left[1], right[1]], axis=1)
        folded[:, n * 256 : (n + 1) * 256] = dot(f_hi, hi) + dot(f_lo, hi) + dot(f_hi, lo)
    for g in range(8):
        piece = folded[:, g * 128 : (g + 1) * 128]
        for k in range(4):
            turned = piece if k == 0 else pltpu.roll(piece, 128 - 32 * k, 1)
            mats[pl.ds(4 * g + k, 216, stride=MAT_LINE), :] = turned


def pack(mats, wzo, wzb, wza, wys, wxo, wxs, wx0):
    mask = lax.broadcasted_iota(jnp.int32, (N, 128), 1) < N

    def matrix(m, axis, offset):
        start = ((axis * 3 + offset) * 24 + m) * MAT_LINE
        v = mats[pl.ds(start if isinstance(m, int) else pl.multiple_of(start, 8), N), :]
        return jnp.where(mask, v, 0.0)

    def parts(v):
        hi = v.astype(bf16).astype(f32)
        return hi, v - hi

    def term(m, carry):
        for t, offset in enumerate((1, 2, 0)):
            hi, lo = parts(matrix(m, 1, offset))
            wys[m, t * N : (t + 1) * N, :] = (hi + pltpu.roll(hi, 32, 1) + pltpu.roll(lo, 64, 1)).astype(bf16)
        for offset, places in ((0, ((wza, 0),)), (1, ((wzo, 0), (wzb, 0), (wza, 64))), (2, ((wzb, 64),))):
            hi, lo = parts(matrix(m, 2, offset))
            first = hi + pltpu.roll(hi, 64, 1)
            for ref, base in places:
                start = m * (64 if ref is wzo else 128) + base
                for p in range(2):
                    at = pl.ds(pl.multiple_of(start + p * N, N), N)
                    ref[at, 0:128] = (pltpu.roll(first, 32, 1) if p else first).astype(bf16)
                    ref[at, 128:256] = (pltpu.roll(lo, 32, 1) if p else lo).astype(bf16)
        return carry

    lax.fori_loop(0, TERMS, term, 0)

    def wide(terms, offset):
        total = None
        for k, m in enumerate(terms):
            v = matrix(m, 0, offset)
            v = pltpu.roll(v, 32 * k, 1) if k else v
            total = v if total is None else total + v
        return split(total)

    for g in range(5):
        at = slice(g * 128, (g + 1) * 128)
        for offset, places in ((2, ((wxs, 0, 64),)), (1, ((wxs, 32, 96), (wxs, 128, 192), (wx0, 0, 32))), (0, ((wxs, 160, 224),))):
            hi, lo = wide(range(4 * g, 4 * g + 4), offset)
            for ref, high_at, low_at in places:
                ref[high_at : high_at + N, at] = hi
                ref[low_at : low_at + N, at] = lo
    for g in range(3):
        at = slice(g * 128, (g + 1) * 128)
        for odd in range(2):
            hi, lo = wide([2 * mp + odd for mp in range(4 * g, min(4 * g + 4, PAIRS))], 1)
            wxo[odd * N : (odd + 1) * N, at] = hi
            wxo[64 + odd * N : 64 + (odd + 1) * N, at] = lo


MESH = pl.DeviceIdType.MESH
Y, CORES, ROWS = 4, 2, 16


def start_copy(src, dst, s, r, peer):
    copy = pltpu.make_async_remote_copy(
        src_ref=src, dst_ref=dst, send_sem=s, recv_sem=r, device_id=peer, device_id_type=MESH
    )
    copy.start()
    return copy


BOX_LINE = N + 8


def lay_out(boxes, lines, xs):
    piece = lax.broadcasted_iota(jnp.int32, (16, 128), 1) // 16

    def octant(at, carry):
        ox, oy, jh = at // 4, at // 2 % 2, at % 2
        rows = [boxes[p * 8 + ox * 4 + oy * 2 + oz, pl.ds(jh, 16, stride=2), :] for p in range(2) for oz in range(2)]
        for j in range(8):
            x = None
            for k in range(4):
                shift = (16 * (k - j)) % 128
                v = pltpu.roll(rows[k], shift, 1) if shift else rows[k]
                x = v if x is None else jnp.where(piece == k, v, x)
            lines[pl.ds(ox * 16 * BOX_LINE + oy * 16 + jh * 8 + j, 16, stride=BOX_LINE), :] = x
        return carry

    lax.fori_loop(0, 8, octant, 0, unroll=4)
    mask = low_half(N)

    def line(i, carry):
        v = lines[pl.ds(pl.multiple_of(i * BOX_LINE, 8), N), :]
        hi = v.astype(bf16).astype(f32)
        at = pl.ds(pl.multiple_of(i * N, N), N)
        xs[at, 0:128] = jnp.where(mask, hi, pltpu.roll(v - hi, 64, 1)).astype(bf16)
        xs[at, 128:256] = v.astype(bf16)
        return carry

    lax.fori_loop(0, N, line, 0, unroll=8)


def lay_back(applied, boxes):
    piece = lax.broadcasted_iota(jnp.int32, (16, 128), 1) // 16

    def octants(at, carry):
        ox, oy, jh = at // 4, at // 2 % 2, at % 2
        start = (oy * 16 + jh * 8) * N + ox * 16
        lines = [applied[pl.ds(pl.multiple_of(start + j * N, 16), 16), :] for j in range(8)]
        for p in range(2):
            for oz in range(2):
                box = None
                for j in range(8):
                    shift = (16 * j - p * 32 - oz * 16) % 128
                    v = pltpu.roll(lines[j], shift, 1) if shift else lines[j]
                    box = v if box is None else jnp.where(piece == j, v, box)
                boxes[p * 8 + ox * 4 + oy * 2 + oz, pl.ds(jh, 16, stride=2), :] = box
        return carry

    lax.fori_loop(0, 8, octants, 0, unroll=2)


def choose(neighbours, col, sel):
    lane = lax.broadcasted_iota(jnp.int32, (N, 128), 1)
    same = lane % N == lax.broadcasted_iota(jnp.int32, (N, 128), 0)
    for d, k in enumerate((1, 5, 4, 0, 3, 2)):
        for g in range(4):
            held = None
            for n in range(4):
                sender = neighbours[k, (g % 2 * 2 + n // 2) * 4 + g // 2 * 2 + n % 2]
                v = jnp.where(sender >= 0, sender % 16 - 2 * col, -1)
                held = v if held is None else jnp.where(lane // N == n, v, held)
            for p in range(2):
                at = slice((d * 2 + p) * N, (d * 2 + p + 1) * N)
                sel[at, g * 128 : (g + 1) * 128] = jnp.where(same & (held == p), 1.0, 0.0).astype(bf16)


def convolve_kernel(fine, slot, neighbours, ops, h, out, own, f, hx, ht,
                    wzo, wzb, wza, wys, wxo, wxs, wx0, sel, folded, leaving, arrived, boxes, lines, xs,
                    t_hi, t_lo, ya, yb, yc, terms, part, centre, from_core, pair_sum, from_y, total,
                    returned, back, s1, r1, s2, r2, s3, r3, s4, r4, s6, r6):
    row, col = lax.axis_index("row"), lax.axis_index("col")
    y, core = col // CORES, col % CORES
    sibling = (row, y * CORES + (1 - core))
    across = [(row, (y + 1 + d) % Y * CORES + core) for d in range(Y - 1)]
    peers = [sibling] + across + [((row + d) % ROWS, col) for d in range(1, ROWS)]
    barrier = pltpu.get_barrier_semaphore()
    for peer in peers:
        pl.semaphore_signal(barrier, inc=1, device_id=peer, device_id_type=MESH)

    for q in range(16):
        own[q] = fine[pl.ds(q // 8 * 256 + q % 8, N, stride=8), :]
    slots = [slot[q] for q in range(16)]
    dest = [v // 128 for v in slots]
    first_row = lax.broadcasted_iota(jnp.int32, (8, 128), 0) == 0
    for d in range(ROWS):
        to = (row + d) % ROWS
        target = arrived.at[row] if d == 0 else leaving.at[d]
        first, last = jnp.int32(16), jnp.int32(-1)
        for q in range(16):
            here = dest[q] == to
            first = jnp.minimum(first, jnp.where(here, q, 16))
            last = jnp.maximum(last, jnp.where(here, q, -1))
        tag = []
        for k, q in enumerate((jnp.minimum(first, 15), jnp.maximum(last, 0))):
            target[k * N : (k + 1) * N, :] = own[q]
            tag.append(jnp.where(last >= 0, slot[q] % 16, -1).astype(f32))
        target[64:72, :] = jnp.where(first_row, tag[0], tag[1])
    fold(ops, h, f, hx, ht, folded, yb, ya)
    pack(ya, wzo, wzb, wza, wys, wxo, wxs, wx0)
    choose(neighbours, col, sel)
    pl.semaphore_wait(barrier, len(peers))

    arrivals = [
        start_copy(leaving.at[d], arrived.at[row], s1.at[d], r1.at[d], ((row + d) % ROWS, col))
        for d in range(1, ROWS)
    ]
    for copy in arrivals:
        copy.wait_recv()

    def place(group, carry):
        total = [[jnp.zeros((8, 128), f32)] * 4 for n in range(4)]
        for k in range(ROWS):
            for s in range(2):
                tag = jnp.broadcast_to(arrived[k, 64 + s : 65 + s, :], (8, 128))
                data = [arrived[k, s * 32 + c * 8 : s * 32 + c * 8 + 8, :] for c in range(4)]
                for n in range(4):
                    hit = tag == (group * 4 + n).astype(f32)
                    total[n] = [jnp.where(hit, data[c], total[n][c]) for c in range(4)]
        for n in range(4):
            for c in range(4):
                boxes[0, group * 4 + n, c * 8 : (c + 1) * 8, :] = total[n][c]
        return carry

    hops = []
    for p in range(2):
        lax.fori_loop(2 * p, 2 * p + 2, place, 0)
        for k, to in ((1, (row + 1) % ROWS), (2, (row + ROWS - 1) % ROWS)):
            at, n = pl.ds(8 * p, 8), 2 * p + k - 1
            hops.append(start_copy(boxes.at[0, at], boxes.at[k, at], s2.at[n], r2.at[n], (to, col)))
    lay_out(boxes.at[0], lines, xs.at[0])
    for k in (1, 2):
        hops[k - 1].wait_recv()
        hops[k + 1].wait_recv()
        lay_out(boxes.at[k], lines, xs.at[k])

    sides_lines(xs.at[1], xs.at[2], wzb, wza, wys, t_hi, t_lo, ya, yb, yc)
    pairs, sums = [], []
    mask = low_half(128)

    def over_pair(c):
        pairs[c].wait_recv()
        for d in range(Y):
            to = (y + 1 + d) % Y
            v = part[c, core, to // 2] + from_core[c, to // 2]
            odd = to % 2 == 1
            low = jnp.where(odd, pltpu.roll(v[:128], 64, 1), v[:128])
            high = jnp.where(odd, v[128:], pltpu.roll(v[128:], 64, 1))
            v = jnp.where(mask, low, high)
            if d < Y - 1:
                pair_sum[c, d] = v
                k = c * (Y - 1) + d
                sums.append(start_copy(pair_sum.at[c, d], from_y.at[c, d], s4.at[k], r4.at[k], across[d]))
            else:
                total[c] = v

    for c in range(4):
        sides_columns(8 * c, wxs, wx0, ya, yb, yc, terms)
        hi, lo = split(terms[...])
        summed = dot(hi, sel[...]) + dot(lo, sel[...])
        for k in range(Y):
            part[c, k // 2, k % 2] = summed[:, k * 128 : (k + 1) * 128]
        pairs.append(start_copy(part.at[c, 1 - core], from_core.at[c], s3.at[c], r3.at[c], sibling))
        if c:
            over_pair(c - 1)
    over_pair(3)
    centre_pass(xs.at[0], wzo, wys, wxo, t_hi, t_lo, ya, centre)
    for c in range(4):
        for d in range(Y - 1):
            sums[c * (Y - 1) + d].wait_recv()
        v = total[c] + from_y[c, 0] + from_y[c, 1] + from_y[c, 2]
        at = slice(c * 256, c * 256 + 128)
        centre[at, :] = centre[at, :] + v
        at = slice(c * 256 + 128, c * 256 + 256)
        centre[at, :] = centre[at, :] + pltpu.roll(v, 64, 1)

    result = boxes.at[0]
    for hop in hops:
        hop.wait_send()
    lay_back(centre, result)

    def give_back(d, carry):
        to = (row + d) % ROWS
        hit = []
        for s in range(2):
            tag = jnp.broadcast_to(arrived[to, 64 + s : 65 + s, :], (8, 128))
            hit.append([tag == float(k) for k in range(16)])
        for c in range(4):
            rows = slice(c * 8, (c + 1) * 8)
            v = [result[0, rows, :]] * 2
            for k in range(1, 16):
                box = result[k, rows, :]
                v = [jnp.where(hit[s][k], box, v[s]) for s in range(2)]
            for s in range(2):
                returned[d * 2 + s, rows, :] = v[s]
        return carry

    returns = []
    for first in range(1, ROWS, 3):
        lax.fori_loop(first, first + 3, give_back, 0)
        for d in range(first, first + 3):
            src, dst = returned.at[pl.ds(2 * d, 2)], back.at[pl.ds(row * 2, 2)]
            returns.append(start_copy(src, dst, s6.at[d], r6.at[d], ((row + d) % ROWS, col)))
    give_back(0, 0)
    for s in range(2):
        back[row * 2 + s] = returned[s]
    for copy in returns:
        copy.wait_recv()
    for q in range(16):
        earlier = jnp.int32(0)
        for k in range(q):
            earlier = jnp.where(dest[k] == dest[q], 1, earlier)
        out[pl.ds(q // 8 * 256 + q % 8, N, stride=8), :] = back[2 * dest[q] + earlier]
    for copy in arrivals + pairs + sums + returns:
        copy.wait_send()


def convolve(fine, slot, neighbours, kernel_ops, filter_matrix):
    vm = pl.BlockSpec(memory_space=pltpu.VMEM)
    sm = pl.BlockSpec(memory_space=pltpu.SMEM)
    low = ((1280, 256), (2560, 256), (2560, 256), (TERMS, 96, 128), (128, 384), (256, 640), (64, 640), (384, 512))
    scratch = [pltpu.VMEM(shape, f32) for shape in ((16, 32, 128), (216, 1024), (32, 1024), (32, 128))]
    scratch += [pltpu.VMEM(shape, bf16) for shape in low]
    scratch += [pltpu.VMEM(shape, f32) for shape in ((216, 1024), (16, 72, 128), (16, 72, 128), (3, 16, 32, 128), (N * BOX_LINE, 128))]
    scratch += [pltpu.VMEM(shape, bf16) for shape in ((3, 1024, 256), (2048, 256), (2048, 256))]
    scratch += [pltpu.VMEM((N * SIDE_LINE, 128), f32)] * 3
    scratch += [
        pltpu.VMEM(shape, f32)
        for shape in (
            (256, 384), (4, 2, 2, 256, 128), (1024, 128), (4, 2, 256, 128), (4, 3, 128, 128), (4, 3, 128, 128),
            (4, 128, 128), (32, 32, 128), (32, 32, 128),
        )
    ]
    scratch += [pltpu.SemaphoreType.DMA((n,)) for n in (16, 16, 4, 4, 4, 4, 12, 12, 16, 16)]
    return pl.pallas_call(
        convolve_kernel,
        out_shape=jax.ShapeDtypeStruct((512, 128), f32),
        in_specs=[vm, sm, sm, vm, vm],
        out_specs=vm,
        scratch_shapes=scratch,
        compiler_params=pltpu.CompilerParams(
            collective_id=1, has_side_effects=True, vmem_limit_bytes=60 * 2**20
        ),
    )(fine, slot, neighbours, kernel_ops, filter_matrix)


def local(fine_coeffs, fine_slot, neighbours, filter_matrix, kernel_ops):
    held_boxes, volume = fine_coeffs.shape
    boxes = jnp.transpose(fine_coeffs.reshape(2, 8, 32, 128), (0, 2, 1, 3)).reshape(512, 128)
    out = convolve(boxes, fine_slot, neighbours.T, jnp.transpose(kernel_ops, (1, 2, 0, 3)), filter_matrix)
    return jnp.transpose(out.reshape(2, 32, 8, 128), (0, 2, 1, 3)).reshape(held_boxes, volume)


def solution(mesh):
    in_specs = (P(("row", "col"), None), P(("row", "col")), P("row", None), P(), P())
    out_specs = P(("row", "col"), None)
    return jax.shard_map(local, mesh=mesh, in_specs=in_specs, out_specs=out_specs, check_vma=False)
```

```python
import jax
import jax.numpy as jnp
from jax import lax
from jax.experimental import pallas as pl
from jax.experimental.pallas import tpu as pltpu
from jax.sharding import PartitionSpec as P

f32, bf16 = jnp.float32, jnp.bfloat16
TERMS, N, PAIRS = 20, 32, 10
SIDE_LINE, OWN_LINE, MAT_LINE = TERMS * N + 8, PAIRS * N + 8, N + 8


def split(x):
    hi = x.astype(bf16)
    return hi, (x - hi.astype(f32)).astype(bf16)


def dot(a, b):
    return jnp.dot(a, b, preferred_element_type=f32)


def dot_t(a, b):
    return lax.dot_general(a, b, (((1,), (1,)), ((), ())), preferred_element_type=f32)


def low_half(rows):
    return lax.broadcasted_iota(jnp.int32, (rows, 128), 1) < 64


def centre_lines(xk, wz, wy, t_hi, t_lo, ys):
    mask = low_half(N)

    def pair(mp, carry):
        weights = wz[pl.ds(pl.multiple_of(mp * 128, 128), 128), 0:192]
        for q in range(4):
            z = dot_t(xk[q * 256 : (q + 1) * 256, 0:192], weights)
            hi, lo = split(z)
            t_hi[q * 256 : (q + 1) * 256, 0:128] = hi
            t_lo[q * 256 : (q + 1) * 256, 0:128] = lo
        left = jnp.concatenate([wy[mp * 2, 0:N, 0:96], wy[mp * 2 + 1, 0:N, 0:96]], axis=0)

        for i in range(N):
            at = slice(i * N, (i + 1) * N)
            hi, lo = t_hi[at, 0:128], t_lo[at, 0:128]
            y = dot(left, jnp.concatenate([hi, lo, hi], axis=0))
            ys[pl.ds(mp * N + i, N, stride=OWN_LINE), :] = jnp.where(mask, y[:N], y[N:])
        return carry

    lax.fori_loop(0, PAIRS, pair, 0)


def centre_columns(wx, ys, out):
    def column(b, carry):
        at = pl.ds(pl.multiple_of(b * OWN_LINE, 8), PAIRS * N)
        hi, lo = split(ys[at, :])
        first = dot(wx[:, 0:320], hi)
        r = first[:64] + first[64:] + dot(wx[0:64, 0:320], lo)
        out[pl.ds(pl.multiple_of(b * N, N), N), :] = r[:N] + pltpu.roll(r[N:], 64, 1)
        return carry

    lax.fori_loop(0, N, column, 0, unroll=4)


def sides_lines(xkb, xka, wzb, wza, wy, t_hi, t_lo, ya, yb, yc):
    mask = low_half(N)

    def pair(mp, carry):
        for xk, wz, base in ((xkb, wzb, 0), (xka, wza, 128)):
            weights = wz[pl.ds(pl.multiple_of(mp * 256, 256), 256), 0:192]
            for q in range(4):
                z = dot_t(xk[q * 256 : (q + 1) * 256, 0:192], weights)
                hi, lo = split(z)
                for odd in range(2):
                    t_hi[odd * 1024 + q * 256 : odd * 1024 + (q + 1) * 256, base : base + 128] = hi[
                        :, odd * 128 : (odd + 1) * 128
                    ]
                    t_lo[odd * 1024 + q * 256 : odd * 1024 + (q + 1) * 256, base : base + 128] = lo[
                        :, odd * 128 : (odd + 1) * 128
                    ]
        for odd in range(2):
            m = mp * 2 + odd
            left = wy[m, :, 0:96]

            for i in range(N):
                at = slice(odd * 1024 + i * N, odd * 1024 + (i + 1) * N)
                hi, lo = t_hi[at, :], t_lo[at, :]
                y = dot(left, jnp.concatenate([hi, lo, hi], axis=0))
                to = pl.ds(m * N + i, N, stride=SIDE_LINE)
                ya[to, :] = y[:N, :128]
                yb[to, :] = y[:N, 128:]
                yc[to, :] = jnp.where(mask, y[N : 2 * N, :128], y[2 * N :, 128:])
        return carry

    lax.fori_loop(0, PAIRS, pair, 0)


def sides_columns(first_b, wx, wx0, ya, yb, yc, out):
    mask = low_half(N)

    def column(k, carry):
        at = pl.ds(pl.multiple_of((first_b + k) * SIDE_LINE, 8), TERMS * N)
        rows = pl.ds(pl.multiple_of(k * N, N), N)
        hi, lo = split(ya[at, :])
        first = dot(wx[0:128, :], hi)
        r = first[:64] + first[64:128] + dot(wx[0:64, :], lo)
        out[rows, 0:128] = jnp.where(mask, r[:N], r[N:])
        hi, lo = split(yb[at, :])
        first = dot(wx[128:256, :], hi)
        r = first[:64] + first[64:128] + dot(wx[128:192, :], lo)
        out[rows, 128:256] = jnp.where(mask, r[:N], r[N:])
        hi, lo = split(yc[at, :])
        first = dot(wx0[...], hi)
        out[rows, 256:384] = first[:N] + first[N:] + dot(wx0[0:N, :], lo)
        return carry

    lax.fori_loop(0, 8, column, 0, unroll=4)


def spread(h, lanes, pick):
    shape = (N, lanes)
    chosen = pick(lax.broadcasted_iota(jnp.int32, shape, 1)) == lax.broadcasted_iota(jnp.int32, shape, 0)
    chosen = jnp.where(chosen, 1.0, 0.0).astype(bf16)
    hi = split(h)[0]
    mid, low = split(h - hi.astype(f32))
    return dot(hi, chosen) + (dot(mid, chosen) + dot(low, chosen))


def fold(ops, h, f, hx, ht, folded, kron, mats):
    for k in range(9):
        f[k * 24 : k * 24 + TERMS, :] = ops[k // 3, k % 3]
        f[k * 24 + TERMS : (k + 1) * 24, :] = jnp.zeros((4, 1024), f32)
    hx[...] = spread(h[...], 1024, lambda lane: lane // N)
    ht[...] = spread(h[...], 128, lambda lane: lane % N)

    def row(a, carry):
        wide = hx[pl.ds(a, 1), :]
        for g in range(8):
            at = pl.ds(pl.multiple_of(g * 1024 + a * N, N), N)
            kron[at, :] = wide[:, g * 128 : (g + 1) * 128] * ht[...]
        return carry

    lax.fori_loop(0, N, row, 0, unroll=4)
    f_hi, f_lo = split(f[...])
    for n in range(4):
        left, right = split(kron[2048 * n : 2048 * n + 1024, :]), split(kron[2048 * n + 1024 : 2048 * n + 2048, :])
        hi, lo = jnp.concatenate([left[0], right[0]], axis=1), jnp.concatenate([left[1], right[1]], axis=1)
        folded[:, n * 256 : (n + 1) * 256] = dot(f_hi, hi) + dot(f_lo, hi) + dot(f_hi, lo)
    for g in range(8):
        piece = folded[:, g * 128 : (g + 1) * 128]
        for k in range(4):
            turned = piece if k == 0 else pltpu.roll(piece, 128 - 32 * k, 1)
            mats[pl.ds(4 * g + k, 216, stride=MAT_LINE), :] = turned


def pack(mats, wzo, wzb, wza, wys, wxo, wxs, wx0):
    mask = lax.broadcasted_iota(jnp.int32, (N, 128), 1) < N

    def matrix(m, axis, offset):
        start = ((axis * 3 + offset) * 24 + m) * MAT_LINE
        v = mats[pl.ds(start if isinstance(m, int) else pl.multiple_of(start, 8), N), :]
        return jnp.where(mask, v, 0.0)

    def parts(v):
        hi = v.astype(bf16).astype(f32)
        return hi, v - hi

    def term(m, carry):
        for t, offset in enumerate((1, 2, 0)):
            hi, lo = parts(matrix(m, 1, offset))
            wys[m, t * N : (t + 1) * N, :] = (hi + pltpu.roll(hi, 32, 1) + pltpu.roll(lo, 64, 1)).astype(bf16)
        for offset, places in ((0, ((wza, 0),)), (1, ((wzo, 0), (wzb, 0), (wza, 64))), (2, ((wzb, 64),))):
            hi, lo = parts(matrix(m, 2, offset))
            first = hi + pltpu.roll(hi, 64, 1)
            for ref, base in places:
                start = m * (64 if ref is wzo else 128) + base
                for p in range(2):
                    at = pl.ds(pl.multiple_of(start + p * N, N), N)
                    ref[at, 0:128] = (pltpu.roll(first, 32, 1) if p else first).astype(bf16)
                    ref[at, 128:256] = (pltpu.roll(lo, 32, 1) if p else lo).astype(bf16)
        return carry

    lax.fori_loop(0, TERMS, term, 0)

    def wide(terms, offset):
        total = None
        for k, m in enumerate(terms):
            v = matrix(m, 0, offset)
            v = pltpu.roll(v, 32 * k, 1) if k else v
            total = v if total is None else total + v
        return split(total)

    for g in range(5):
        at = slice(g * 128, (g + 1) * 128)
        for offset, places in ((2, ((wxs, 0, 64),)), (1, ((wxs, 32, 96), (wxs, 128, 192), (wx0, 0, 32))), (0, ((wxs, 160, 224),))):
            hi, lo = wide(range(4 * g, 4 * g + 4), offset)
            for ref, high_at, low_at in places:
                ref[high_at : high_at + N, at] = hi
                ref[low_at : low_at + N, at] = lo
    for g in range(3):
        at = slice(g * 128, (g + 1) * 128)
        for odd in range(2):
            hi, lo = wide([2 * mp + odd for mp in range(4 * g, min(4 * g + 4, PAIRS))], 1)
            wxo[odd * N : (odd + 1) * N, at] = hi
            wxo[64 + odd * N : 64 + (odd + 1) * N, at] = lo


MESH = pl.DeviceIdType.MESH
Y, CORES, ROWS = 4, 2, 16


def start_copy(src, dst, s, r, peer):
    copy = pltpu.make_async_remote_copy(
        src_ref=src, dst_ref=dst, send_sem=s, recv_sem=r, device_id=peer, device_id_type=MESH
    )
    copy.start()
    return copy


BOX_LINE = N + 8


def lay_out(boxes, lines, xs):
    piece = lax.broadcasted_iota(jnp.int32, (16, 128), 1) // 16

    def octant(at, carry):
        ox, oy, jh = at // 4, at // 2 % 2, at % 2
        rows = [boxes[p * 8 + ox * 4 + oy * 2 + oz, pl.ds(jh, 16, stride=2), :] for p in range(2) for oz in range(2)]
        for j in range(8):
            x = None
            for k in range(4):
                shift = (16 * (k - j)) % 128
                v = pltpu.roll(rows[k], shift, 1) if shift else rows[k]
                x = v if x is None else jnp.where(piece == k, v, x)
            lines[pl.ds(ox * 16 * BOX_LINE + oy * 16 + jh * 8 + j, 16, stride=BOX_LINE), :] = x
        return carry

    lax.fori_loop(0, 8, octant, 0, unroll=4)
    mask = low_half(N)

    def line(i, carry):
        v = lines[pl.ds(pl.multiple_of(i * BOX_LINE, 8), N), :]
        hi = v.astype(bf16).astype(f32)
        at = pl.ds(pl.multiple_of(i * N, N), N)
        xs[at, 0:128] = jnp.where(mask, hi, pltpu.roll(v - hi, 64, 1)).astype(bf16)
        xs[at, 128:256] = v.astype(bf16)
        return carry

    lax.fori_loop(0, N, line, 0, unroll=8)


def lay_back(applied, boxes):
    piece = lax.broadcasted_iota(jnp.int32, (16, 128), 1) // 16

    def octants(at, carry):
        ox, oy, jh = at // 4, at // 2 % 2, at % 2
        start = (oy * 16 + jh * 8) * N + ox * 16
        lines = [applied[pl.ds(pl.multiple_of(start + j * N, 16), 16), :] for j in range(8)]
        for p in range(2):
            for oz in range(2):
                box = None
                for j in range(8):
                    shift = (16 * j - p * 32 - oz * 16) % 128
                    v = pltpu.roll(lines[j], shift, 1) if shift else lines[j]
                    box = v if box is None else jnp.where(piece == j, v, box)
                boxes[p * 8 + ox * 4 + oy * 2 + oz, pl.ds(jh, 16, stride=2), :] = box
        return carry

    lax.fori_loop(0, 8, octants, 0, unroll=2)


def choose(neighbours, col, sel):
    lane = lax.broadcasted_iota(jnp.int32, (N, 128), 1)
    same = lane % N == lax.broadcasted_iota(jnp.int32, (N, 128), 0)
    for d, k in enumerate((1, 5, 4, 0, 3, 2)):
        for g in range(4):
            held = None
            for n in range(4):
                sender = neighbours[k, (g % 2 * 2 + n // 2) * 4 + g // 2 * 2 + n % 2]
                v = jnp.where(sender >= 0, sender % 16 - 2 * col, -1)
                held = v if held is None else jnp.where(lane // N == n, v, held)
            for p in range(2):
                at = slice((d * 2 + p) * N, (d * 2 + p + 1) * N)
                sel[at, g * 128 : (g + 1) * 128] = jnp.where(same & (held == p), 1.0, 0.0).astype(bf16)


def convolve_kernel(fine, slot, neighbours, ops, h, out, own, f, hx, ht,
                    wzo, wzb, wza, wys, wxo, wxs, wx0, sel, folded, leaving, arrived, boxes, lines, xs,
                    t_hi, t_lo, ya, yb, yc, terms, part, centre, from_core, pair_sum, from_y, relay, passing, total,
                    returned, back, s1, r1, s2, r2, s3, r3, s4, r4, s6, r6):
    row, col = lax.axis_index("row"), lax.axis_index("col")
    y, core = col // CORES, col % CORES
    sibling = (row, y * CORES + (1 - core))
    across = [(row, (y + 1 + d) % Y * CORES + core) for d in range(Y - 1)]
    peers = [sibling] + across + [((row + d) % ROWS, col) for d in range(1, ROWS)]
    barrier = pltpu.get_barrier_semaphore()
    for peer in peers:
        pl.semaphore_signal(barrier, inc=1, device_id=peer, device_id_type=MESH)

    for q in range(16):
        own[q] = fine[pl.ds(q // 8 * 256 + q % 8, N, stride=8), :]
    slots = [slot[q] for q in range(16)]
    dest = [v // 128 for v in slots]
    first_row = lax.broadcasted_iota(jnp.int32, (8, 128), 0) == 0
    fold(ops, h, f, hx, ht, folded, yb, ya)
    pack(ya, wzo, wzb, wza, wys, wxo, wxs, wx0)
    choose(neighbours, col, sel)
    pl.semaphore_wait(barrier, len(peers))

    arrivals = []
    for d in list(range(1, ROWS)) + [0]:
        to = (row + d) % ROWS
        target = arrived.at[row] if d == 0 else leaving.at[d]
        first, last = jnp.int32(16), jnp.int32(-1)
        for q in range(16):
            here = dest[q] == to
            first = jnp.minimum(first, jnp.where(here, q, 16))
            last = jnp.maximum(last, jnp.where(here, q, -1))
        tag = []
        for k, q in enumerate((jnp.minimum(first, 15), jnp.maximum(last, 0))):
            target[k * N : (k + 1) * N, :] = own[q]
            tag.append(jnp.where(last >= 0, slot[q] % 16, -1).astype(f32))
        target[64:72, :] = jnp.where(first_row, tag[0], tag[1])
        if d:
            arrivals.append(start_copy(leaving.at[d], arrived.at[row], s1.at[d], r1.at[d], (to, col)))
    for copy in arrivals:
        copy.wait_recv()

    def place(group, carry):
        total = [[jnp.zeros((8, 128), f32)] * 4 for n in range(4)]
        for k in range(ROWS):
            for s in range(2):
                tag = jnp.broadcast_to(arrived[k, 64 + s : 65 + s, :], (8, 128))
                data = [arrived[k, s * 32 + c * 8 : s * 32 + c * 8 + 8, :] for c in range(4)]
                for n in range(4):
                    hit = tag == (group * 4 + n).astype(f32)
                    total[n] = [jnp.where(hit, data[c], total[n][c]) for c in range(4)]
        for n in range(4):
            for c in range(4):
                boxes[0, group * 4 + n, c * 8 : (c + 1) * 8, :] = total[n][c]
        return carry

    hops = []
    for p in range(2):
        lax.fori_loop(2 * p, 2 * p + 2, place, 0)
        for k, to in ((1, (row + 1) % ROWS), (2, (row + ROWS - 1) % ROWS)):
            at, n = pl.ds(8 * p, 8), 2 * p + k - 1
            hops.append(start_copy(boxes.at[0, at], boxes.at[k, at], s2.at[n], r2.at[n], (to, col)))
    lay_out(boxes.at[0], lines, xs.at[0])
    for k in (1, 2):
        hops[k - 1].wait_recv()
        hops[k + 1].wait_recv()
        lay_out(boxes.at[k], lines, xs.at[k])

    sides_lines(xs.at[1], xs.at[2], wzb, wza, wys, t_hi, t_lo, ya, yb, yc)
    pairs, sums = [], {}
    mask = low_half(128)

    def over_pair(c):
        pairs[c].wait_recv()
        for d in range(Y):
            to = (y + 1 + d) % Y
            v = part[c, core, to // 2] + from_core[c, to // 2]
            odd = to % 2 == 1
            low = jnp.where(odd, pltpu.roll(v[:128], 64, 1), v[:128])
            high = jnp.where(odd, v[128:], pltpu.roll(v[128:], 64, 1))
            v = jnp.where(mask, low, high)
            if d < Y - 1:
                pair_sum[c, d] = v
            else:
                total[c] = v
        up, down, halves = across[0], across[2], (slice(0, 64), slice(64, 128))
        for k, (d, half, to) in enumerate(((1, 0, up), (1, 1, down), (0, 1, up), (2, 0, down))):
            src = pair_sum.at[c, d, halves[half]]
            dst = relay.at[c, half] if d == 1 else from_y.at[c, d // 2, halves[half]]
            sums[c, k] = start_copy(src, dst, s4.at[c * 6 + k], r4.at[c * 6 + k], to)

    def relayed(c):
        up, down, halves = across[0], across[2], (slice(0, 64), slice(64, 128))
        for half, d, to in ((0, 0, up), (1, 2, down)):
            sums[c, half].wait_recv()
            passing[c, half] = pair_sum[c, d, halves[half]] + relay[c, half]
            k = c * 6 + 4 + half
            dst = from_y.at[c, d // 2, halves[half]]
            sums[c, 4 + half] = start_copy(passing.at[c, half], dst, s4.at[k], r4.at[k], to)

    for c in range(4):
        sides_columns(8 * c, wxs, wx0, ya, yb, yc, terms)
        hi, lo = split(terms[...])
        summed = dot(hi, sel[...]) + dot(lo, sel[...])
        for k in range(Y):
            part[c, k // 2, k % 2] = summed[:, k * 128 : (k + 1) * 128]
        pairs.append(start_copy(part.at[c, 1 - core], from_core.at[c], s3.at[c], r3.at[c], sibling))
        if c > 1:
            relayed(c - 2)
        if c:
            over_pair(c - 1)
    over_pair(3)
    relayed(2)
    centre_lines(xs.at[0], wzo, wys, t_hi, t_lo, ya)
    relayed(3)
    centre_columns(wxo, ya, centre)
    for c in range(4):
        for k in range(2, 6):
            sums[c, k].wait_recv()
        v = total[c] + from_y[c, 0] + from_y[c, 1]
        at = slice(c * 256, c * 256 + 128)
        centre[at, :] = centre[at, :] + v
        at = slice(c * 256 + 128, c * 256 + 256)
        centre[at, :] = centre[at, :] + pltpu.roll(v, 64, 1)

    result = boxes.at[0]
    for hop in hops:
        hop.wait_send()
    lay_back(centre, result)

    def give_back(d, carry):
        to = (row + d) % ROWS
        hit = []
        for s in range(2):
            tag = jnp.broadcast_to(arrived[to, 64 + s : 65 + s, :], (8, 128))
            hit.append([tag == float(k) for k in range(16)])
        for c in range(4):
            rows = slice(c * 8, (c + 1) * 8)
            v = [result[0, rows, :]] * 2
            for k in range(1, 16):
                box = result[k, rows, :]
                v = [jnp.where(hit[s][k], box, v[s]) for s in range(2)]
            for s in range(2):
                returned[d * 2 + s, rows, :] = v[s]
        return carry

    lax.fori_loop(0, ROWS, give_back, 0)
    returns = []
    for d in range(1, ROWS):
        src, dst = returned.at[pl.ds(2 * d, 2)], back.at[pl.ds(row * 2, 2)]
        returns.append(start_copy(src, dst, s6.at[d], r6.at[d], ((row + d) % ROWS, col)))
    for s in range(2):
        back[row * 2 + s] = returned[s]
    for copy in returns:
        copy.wait_recv()
    for q in range(16):
        earlier = jnp.int32(0)
        for k in range(q):
            earlier = jnp.where(dest[k] == dest[q], 1, earlier)
        out[pl.ds(q // 8 * 256 + q % 8, N, stride=8), :] = back[2 * dest[q] + earlier]
    for copy in arrivals + pairs + list(sums.values()) + returns:
        copy.wait_send()


def convolve(fine, slot, neighbours, kernel_ops, filter_matrix):
    vm = pl.BlockSpec(memory_space=pltpu.VMEM)
    sm = pl.BlockSpec(memory_space=pltpu.SMEM)
    low = ((1280, 256), (2560, 256), (2560, 256), (TERMS, 96, 128), (128, 384), (256, 640), (64, 640), (384, 512))
    scratch = [pltpu.VMEM(shape, f32) for shape in ((16, 32, 128), (216, 1024), (32, 1024), (32, 128))]
    scratch += [pltpu.VMEM(shape, bf16) for shape in low]
    scratch += [pltpu.VMEM(shape, f32) for shape in ((216, 1024), (16, 72, 128), (16, 72, 128), (3, 16, 32, 128), (N * BOX_LINE, 128))]
    scratch += [pltpu.VMEM(shape, bf16) for shape in ((3, 1024, 256), (2048, 256), (2048, 256))]
    scratch += [pltpu.VMEM((N * SIDE_LINE, 128), f32)] * 3
    scratch += [
        pltpu.VMEM(shape, f32)
        for shape in (
            (256, 384), (4, 2, 2, 256, 128), (1024, 128), (4, 2, 256, 128), (4, 3, 128, 128), (4, 2, 128, 128),
            (4, 2, 64, 128), (4, 2, 64, 128), (4, 128, 128), (32, 32, 128), (32, 32, 128),
        )
    ]
    scratch += [pltpu.SemaphoreType.DMA((n,)) for n in (16, 16, 4, 4, 4, 4, 24, 24, 16, 16)]
    return pl.pallas_call(
        convolve_kernel,
        out_shape=jax.ShapeDtypeStruct((512, 128), f32),
        in_specs=[vm, sm, sm, vm, vm],
        out_specs=vm,
        scratch_shapes=scratch,
        compiler_params=pltpu.CompilerParams(
            collective_id=1, has_side_effects=True, vmem_limit_bytes=60 * 2**20
        ),
    )(fine, slot, neighbours, kernel_ops, filter_matrix)


def local(fine_coeffs, fine_slot, neighbours, filter_matrix, kernel_ops):
    held_boxes, volume = fine_coeffs.shape
    boxes = jnp.transpose(fine_coeffs.reshape(2, 8, 32, 128), (0, 2, 1, 3)).reshape(512, 128)
    out = convolve(boxes, fine_slot, neighbours.T, jnp.transpose(kernel_ops, (1, 2, 0, 3)), filter_matrix)
    return jnp.transpose(out.reshape(2, 32, 8, 128), (0, 2, 1, 3)).reshape(held_boxes, volume)


def solution(mesh):
    in_specs = (P(("row", "col"), None), P(("row", "col")), P("row", None), P(), P())
    out_specs = P(("row", "col"), None)
    return jax.shard_map(local, mesh=mesh, in_specs=in_specs, out_specs=out_specs, check_vma=False)
```

```python
import jax
import jax.numpy as jnp
from jax import lax
from jax.experimental import pallas as pl
from jax.experimental.pallas import tpu as pltpu
from jax.sharding import PartitionSpec as P

f32, bf16 = jnp.float32, jnp.bfloat16
TERMS, N, PAIRS = 20, 32, 10
SIDE_LINE, OWN_LINE, MAT_LINE = TERMS * N + 8, PAIRS * N + 8, N + 8


def split(x):
    hi = x.astype(bf16)
    return hi, (x - hi.astype(f32)).astype(bf16)


def dot(a, b):
    return jnp.dot(a, b, preferred_element_type=f32)


def dot_t(a, b):
    return lax.dot_general(a, b, (((1,), (1,)), ((), ())), preferred_element_type=f32)


def low_half(rows):
    return lax.broadcasted_iota(jnp.int32, (rows, 128), 1) < 64


def centre_lines(xk, wz, wy, t_hi, t_lo, ys):
    mask = low_half(N)

    def pair(mp, carry):
        weights = wz[pl.ds(pl.multiple_of(mp * 128, 128), 128), 0:192]
        for q in range(4):
            z = dot_t(xk[q * 256 : (q + 1) * 256, 0:192], weights)
            hi, lo = split(z)
            t_hi[q * 256 : (q + 1) * 256, 0:128] = hi
            t_lo[q * 256 : (q + 1) * 256, 0:128] = lo
        left = jnp.concatenate([wy[mp * 2, 0:N, 0:96], wy[mp * 2 + 1, 0:N, 0:96]], axis=0)

        for i in range(N):
            at = slice(i * N, (i + 1) * N)
            hi, lo = t_hi[at, 0:128], t_lo[at, 0:128]
            y = dot(left, jnp.concatenate([hi, lo, hi], axis=0))
            ys[pl.ds(mp * N + i, N, stride=OWN_LINE), :] = jnp.where(mask, y[:N], y[N:])
        return carry

    lax.fori_loop(0, PAIRS, pair, 0)


def centre_columns(wx, ys, out):
    def column(b, carry):
        at = pl.ds(pl.multiple_of(b * OWN_LINE, 8), PAIRS * N)
        hi, lo = split(ys[at, :])
        first = dot(wx[:, 0:320], hi)
        r = first[:64] + first[64:] + dot(wx[0:64, 0:320], lo)
        out[pl.ds(pl.multiple_of(b * N, N), N), :] = r[:N] + pltpu.roll(r[N:], 64, 1)
        return carry

    lax.fori_loop(0, N, column, 0, unroll=4)


def sides_lines(xkb, xka, wzb, wza, wy, t_hi, t_lo, ya, yb, yc):
    mask = low_half(N)

    def pair(mp, carry):
        for xk, wz, base in ((xkb, wzb, 0), (xka, wza, 128)):
            weights = wz[pl.ds(pl.multiple_of(mp * 256, 256), 256), 0:192]
            for q in range(4):
                z = dot_t(xk[q * 256 : (q + 1) * 256, 0:192], weights)
                hi, lo = split(z)
                for odd in range(2):
                    t_hi[odd * 1024 + q * 256 : odd * 1024 + (q + 1) * 256, base : base + 128] = hi[
                        :, odd * 128 : (odd + 1) * 128
                    ]
                    t_lo[odd * 1024 + q * 256 : odd * 1024 + (q + 1) * 256, base : base + 128] = lo[
                        :, odd * 128 : (odd + 1) * 128
                    ]
        for odd in range(2):
            m = mp * 2 + odd
            left = wy[m, :, 0:96]

            for i in range(N):
                at = slice(odd * 1024 + i * N, odd * 1024 + (i + 1) * N)
                hi, lo = t_hi[at, :], t_lo[at, :]
                y = dot(left, jnp.concatenate([hi, lo, hi], axis=0))
                to = pl.ds(m * N + i, N, stride=SIDE_LINE)
                ya[to, :] = y[:N, :128]
                yb[to, :] = y[:N, 128:]
                yc[to, :] = jnp.where(mask, y[N : 2 * N, :128], y[2 * N :, 128:])
        return carry

    lax.fori_loop(0, PAIRS, pair, 0)


def sides_columns(first_b, wx, wx0, ya, yb, yc, out):
    mask = low_half(N)

    def column(k, carry):
        at = pl.ds(pl.multiple_of((first_b + k) * SIDE_LINE, 8), TERMS * N)
        rows = pl.ds(pl.multiple_of(k * N, N), N)
        hi, lo = split(ya[at, :])
        first = dot(wx[0:128, :], hi)
        r = first[:64] + first[64:128] + dot(wx[0:64, :], lo)
        out[rows, 0:128] = jnp.where(mask, r[:N], r[N:])
        hi, lo = split(yb[at, :])
        first = dot(wx[128:256, :], hi)
        r = first[:64] + first[64:128] + dot(wx[128:192, :], lo)
        out[rows, 128:256] = jnp.where(mask, r[:N], r[N:])
        hi, lo = split(yc[at, :])
        first = dot(wx0[...], hi)
        out[rows, 256:384] = first[:N] + first[N:] + dot(wx0[0:N, :], lo)
        return carry

    lax.fori_loop(0, 8, column, 0, unroll=4)


def spread(h, lanes, pick):
    shape = (N, lanes)
    chosen = pick(lax.broadcasted_iota(jnp.int32, shape, 1)) == lax.broadcasted_iota(jnp.int32, shape, 0)
    chosen = jnp.where(chosen, 1.0, 0.0).astype(bf16)
    hi = split(h)[0]
    mid, low = split(h - hi.astype(f32))
    return dot(hi, chosen) + (dot(mid, chosen) + dot(low, chosen))


def fold(ops, h, f, hx, ht, folded, kron, mats):
    for k in range(9):
        f[k * 24 : k * 24 + TERMS, :] = ops[k // 3, k % 3]
        f[k * 24 + TERMS : (k + 1) * 24, :] = jnp.zeros((4, 1024), f32)
    hx[...] = spread(h[...], 1024, lambda lane: lane // N)
    ht[...] = spread(h[...], 128, lambda lane: lane % N)

    def row(a, carry):
        wide = hx[pl.ds(a, 1), :]
        for g in range(8):
            at = pl.ds(pl.multiple_of(g * 1024 + a * N, N), N)
            kron[at, :] = wide[:, g * 128 : (g + 1) * 128] * ht[...]
        return carry

    lax.fori_loop(0, N, row, 0, unroll=4)
    f_hi, f_lo = split(f[...])
    for n in range(4):
        left, right = split(kron[2048 * n : 2048 * n + 1024, :]), split(kron[2048 * n + 1024 : 2048 * n + 2048, :])
        hi, lo = jnp.concatenate([left[0], right[0]], axis=1), jnp.concatenate([left[1], right[1]], axis=1)
        folded[:, n * 256 : (n + 1) * 256] = dot(f_hi, hi) + dot(f_lo, hi) + dot(f_hi, lo)
    for g in range(8):
        piece = folded[:, g * 128 : (g + 1) * 128]
        for k in range(4):
            turned = piece if k == 0 else pltpu.roll(piece, 128 - 32 * k, 1)
            mats[pl.ds(4 * g + k, 216, stride=MAT_LINE), :] = turned


def pack(mats, wzo, wzb, wza, wys, wxo, wxs, wx0):
    mask = lax.broadcasted_iota(jnp.int32, (N, 128), 1) < N

    def matrix(m, axis, offset):
        start = ((axis * 3 + offset) * 24 + m) * MAT_LINE
        v = mats[pl.ds(start if isinstance(m, int) else pl.multiple_of(start, 8), N), :]
        return jnp.where(mask, v, 0.0)

    def parts(v):
        hi = v.astype(bf16).astype(f32)
        return hi, v - hi

    def term(m, carry):
        for t, offset in enumerate((1, 2, 0)):
            hi, lo = parts(matrix(m, 1, offset))
            wys[m, t * N : (t + 1) * N, :] = (hi + pltpu.roll(hi, 32, 1) + pltpu.roll(lo, 64, 1)).astype(bf16)
        for offset, places in ((0, ((wza, 0),)), (1, ((wzo, 0), (wzb, 0), (wza, 64))), (2, ((wzb, 64),))):
            hi, lo = parts(matrix(m, 2, offset))
            first = hi + pltpu.roll(hi, 64, 1)
            for ref, base in places:
                start = m * (64 if ref is wzo else 128) + base
                for p in range(2):
                    at = pl.ds(pl.multiple_of(start + p * N, N), N)
                    ref[at, 0:128] = (pltpu.roll(first, 32, 1) if p else first).astype(bf16)
                    ref[at, 128:256] = (pltpu.roll(lo, 32, 1) if p else lo).astype(bf16)
        return carry

    lax.fori_loop(0, TERMS, term, 0)

    def wide(terms, offset):
        total = None
        for k, m in enumerate(terms):
            v = matrix(m, 0, offset)
            v = pltpu.roll(v, 32 * k, 1) if k else v
            total = v if total is None else total + v
        return split(total)

    for g in range(5):
        at = slice(g * 128, (g + 1) * 128)
        for offset, places in ((2, ((wxs, 0, 64),)), (1, ((wxs, 32, 96), (wxs, 128, 192), (wx0, 0, 32))), (0, ((wxs, 160, 224),))):
            hi, lo = wide(range(4 * g, 4 * g + 4), offset)
            for ref, high_at, low_at in places:
                ref[high_at : high_at + N, at] = hi
                ref[low_at : low_at + N, at] = lo
    for g in range(3):
        at = slice(g * 128, (g + 1) * 128)
        for odd in range(2):
            hi, lo = wide([2 * mp + odd for mp in range(4 * g, min(4 * g + 4, PAIRS))], 1)
            wxo[odd * N : (odd + 1) * N, at] = hi
            wxo[64 + odd * N : 64 + (odd + 1) * N, at] = lo


MESH = pl.DeviceIdType.MESH
Y, CORES, ROWS = 4, 2, 16


def start_copy(src, dst, s, r, peer):
    copy = pltpu.make_async_remote_copy(
        src_ref=src, dst_ref=dst, send_sem=s, recv_sem=r, device_id=peer, device_id_type=MESH
    )
    copy.start()
    return copy


BOX_LINE = N + 8


def lay_out(boxes, lines, xs):
    piece = lax.broadcasted_iota(jnp.int32, (16, 128), 1) // 16

    def octant(at, carry):
        ox, oy, jh = at // 4, at // 2 % 2, at % 2
        rows = [boxes[p * 8 + ox * 4 + oy * 2 + oz, pl.ds(jh, 16, stride=2), :] for p in range(2) for oz in range(2)]
        for j in range(8):
            x = None
            for k in range(4):
                shift = (16 * (k - j)) % 128
                v = pltpu.roll(rows[k], shift, 1) if shift else rows[k]
                x = v if x is None else jnp.where(piece == k, v, x)
            lines[pl.ds(ox * 16 * BOX_LINE + oy * 16 + jh * 8 + j, 16, stride=BOX_LINE), :] = x
        return carry

    lax.fori_loop(0, 8, octant, 0, unroll=4)
    mask = low_half(N)

    def line(i, carry):
        v = lines[pl.ds(pl.multiple_of(i * BOX_LINE, 8), N), :]
        hi = v.astype(bf16).astype(f32)
        at = pl.ds(pl.multiple_of(i * N, N), N)
        xs[at, 0:128] = jnp.where(mask, hi, pltpu.roll(v - hi, 64, 1)).astype(bf16)
        xs[at, 128:256] = v.astype(bf16)
        return carry

    lax.fori_loop(0, N, line, 0, unroll=8)


def lay_back(applied, boxes):
    piece = lax.broadcasted_iota(jnp.int32, (16, 128), 1) // 16

    def octants(at, carry):
        ox, oy, jh = at // 4, at // 2 % 2, at % 2
        start = (oy * 16 + jh * 8) * N + ox * 16
        lines = [applied[pl.ds(pl.multiple_of(start + j * N, 16), 16), :] for j in range(8)]
        for p in range(2):
            for oz in range(2):
                box = None
                for j in range(8):
                    shift = (16 * j - p * 32 - oz * 16) % 128
                    v = pltpu.roll(lines[j], shift, 1) if shift else lines[j]
                    box = v if box is None else jnp.where(piece == j, v, box)
                boxes[p * 8 + ox * 4 + oy * 2 + oz, pl.ds(jh, 16, stride=2), :] = box
        return carry

    lax.fori_loop(0, 8, octants, 0, unroll=2)


def choose(neighbours, col, sel):
    lane = lax.broadcasted_iota(jnp.int32, (N, 128), 1)
    same = lane % N == lax.broadcasted_iota(jnp.int32, (N, 128), 0)
    for d, k in enumerate((1, 5, 4, 0, 3, 2)):
        for g in range(4):
            held = None
            for n in range(4):
                sender = neighbours[k, (g % 2 * 2 + n // 2) * 4 + g // 2 * 2 + n % 2]
                v = jnp.where(sender >= 0, sender % 16 - 2 * col, -1)
                held = v if held is None else jnp.where(lane // N == n, v, held)
            for p in range(2):
                at = slice((d * 2 + p) * N, (d * 2 + p + 1) * N)
                sel[at, g * 128 : (g + 1) * 128] = jnp.where(same & (held == p), 1.0, 0.0).astype(bf16)


def convolve_kernel(fine, slot, neighbours, ops, h, out, own, f, hx, ht,
                    wzo, wzb, wza, wys, wxo, wxs, wx0, sel, folded, leaving, arrived, boxes, lines, xs,
                    t_hi, t_lo, ya, yb, yc, terms, part, centre, from_core, pair_sum, from_y, total,
                    returned, back, s1, r1, s2, r2, s3, r3, s4, r4, s6, r6):
    row, col = lax.axis_index("row"), lax.axis_index("col")
    y, core = col // CORES, col % CORES
    sibling = (row, y * CORES + (1 - core))
    across = [(row, (y + 1 + d) % Y * CORES + core) for d in range(Y - 1)]
    peers = [sibling] + across + [((row + d) % ROWS, col) for d in range(1, ROWS)]
    barrier = pltpu.get_barrier_semaphore()
    for peer in peers:
        pl.semaphore_signal(barrier, inc=1, device_id=peer, device_id_type=MESH)

    for q in range(16):
        own[q] = fine[pl.ds(q // 8 * 256 + q % 8, N, stride=8), :]
    slots = [slot[q] for q in range(16)]
    dest = [v // 128 for v in slots]
    first_row = lax.broadcasted_iota(jnp.int32, (8, 128), 0) == 0
    pl.semaphore_wait(barrier, len(peers))

    arrivals = []
    for d in list(range(1, ROWS)) + [0]:
        to = (row + d) % ROWS
        target = arrived.at[row] if d == 0 else leaving.at[d]
        first, last = jnp.int32(16), jnp.int32(-1)
        for q in range(16):
            here = dest[q] == to
            first = jnp.minimum(first, jnp.where(here, q, 16))
            last = jnp.maximum(last, jnp.where(here, q, -1))
        tag = []
        for k, q in enumerate((jnp.minimum(first, 15), jnp.maximum(last, 0))):
            target[k * N : (k + 1) * N, :] = own[q]
            tag.append(jnp.where(last >= 0, slot[q] % 16, -1).astype(f32))
        target[64:72, :] = jnp.where(first_row, tag[0], tag[1])
        if d:
            arrivals.append(start_copy(leaving.at[d], arrived.at[row], s1.at[d], r1.at[d], (to, col)))
    fold(ops, h, f, hx, ht, folded, yb, ya)
    pack(ya, wzo, wzb, wza, wys, wxo, wxs, wx0)
    choose(neighbours, col, sel)
    for copy in arrivals:
        copy.wait_recv()

    def place(group, carry):
        total = [[jnp.zeros((8, 128), f32)] * 4 for n in range(4)]
        for k in range(ROWS):
            for s in range(2):
                tag = jnp.broadcast_to(arrived[k, 64 + s : 65 + s, :], (8, 128))
                data = [arrived[k, s * 32 + c * 8 : s * 32 + c * 8 + 8, :] for c in range(4)]
                for n in range(4):
                    hit = tag == (group * 4 + n).astype(f32)
                    total[n] = [jnp.where(hit, data[c], total[n][c]) for c in range(4)]
        for n in range(4):
            for c in range(4):
                boxes[0, group * 4 + n, c * 8 : (c + 1) * 8, :] = total[n][c]
        return carry

    hops = []
    for p in range(2):
        lax.fori_loop(2 * p, 2 * p + 2, place, 0)
        for k, to in ((1, (row + 1) % ROWS), (2, (row + ROWS - 1) % ROWS)):
            at, n = pl.ds(8 * p, 8), 2 * p + k - 1
            hops.append(start_copy(boxes.at[0, at], boxes.at[k, at], s2.at[n], r2.at[n], (to, col)))
    lay_out(boxes.at[0], lines, xs.at[0])
    for k in (1, 2):
        hops[k - 1].wait_recv()
        hops[k + 1].wait_recv()
        lay_out(boxes.at[k], lines, xs.at[k])

    sides_lines(xs.at[1], xs.at[2], wzb, wza, wys, t_hi, t_lo, ya, yb, yc)
    pairs, sums = [], []
    mask = low_half(128)

    def over_pair(c):
        pairs[c].wait_recv()
        for d in range(Y):
            to = (y + 1 + d) % Y
            v = part[c, core, to // 2] + from_core[c, to // 2]
            odd = to % 2 == 1
            low = jnp.where(odd, pltpu.roll(v[:128], 64, 1), v[:128])
            high = jnp.where(odd, v[128:], pltpu.roll(v[128:], 64, 1))
            v = jnp.where(mask, low, high)
            if d < Y - 1:
                pair_sum[c, d] = v
                k = c * (Y - 1) + d
                sums.append(start_copy(pair_sum.at[c, d], from_y.at[c, d], s4.at[k], r4.at[k], across[d]))
            else:
                total[c] = v

    for c in range(4):
        sides_columns(8 * c, wxs, wx0, ya, yb, yc, terms)
        hi, lo = split(terms[...])
        summed = dot(hi, sel[...]) + dot(lo, sel[...])
        for k in range(Y):
            part[c, k // 2, k % 2] = summed[:, k * 128 : (k + 1) * 128]
        pairs.append(start_copy(part.at[c, 1 - core], from_core.at[c], s3.at[c], r3.at[c], sibling))
        if c:
            over_pair(c - 1)
    over_pair(3)
    centre_lines(xs.at[0], wzo, wys, t_hi, t_lo, ya)
    centre_columns(wxo, ya, centre)
    for c in range(4):
        for d in range(Y - 1):
            sums[c * (Y - 1) + d].wait_recv()
        v = total[c] + from_y[c, 0] + from_y[c, 1] + from_y[c, 2]
        at = slice(c * 256, c * 256 + 128)
        centre[at, :] = centre[at, :] + v
        at = slice(c * 256 + 128, c * 256 + 256)
        centre[at, :] = centre[at, :] + pltpu.roll(v, 64, 1)

    result = boxes.at[0]
    for hop in hops:
        hop.wait_send()
    lay_back(centre, result)

    def give_back(d, carry):
        to = (row + d) % ROWS
        hit = []
        for s in range(2):
            tag = jnp.broadcast_to(arrived[to, 64 + s : 65 + s, :], (8, 128))
            hit.append([tag == float(k) for k in range(16)])
        for c in range(4):
            rows = slice(c * 8, (c + 1) * 8)
            v = [result[0, rows, :]] * 2
            for k in range(1, 16):
                box = result[k, rows, :]
                v = [jnp.where(hit[s][k], box, v[s]) for s in range(2)]
            for s in range(2):
                returned[d * 2 + s, rows, :] = v[s]
        return carry

    lax.fori_loop(0, ROWS, give_back, 0)
    returns = []
    for d in range(1, ROWS):
        src, dst = returned.at[pl.ds(2 * d, 2)], back.at[pl.ds(row * 2, 2)]
        returns.append(start_copy(src, dst, s6.at[d], r6.at[d], ((row + d) % ROWS, col)))
    for s in range(2):
        back[row * 2 + s] = returned[s]
    for copy in returns:
        copy.wait_recv()
    for q in range(16):
        earlier = jnp.int32(0)
        for k in range(q):
            earlier = jnp.where(dest[k] == dest[q], 1, earlier)
        out[pl.ds(q // 8 * 256 + q % 8, N, stride=8), :] = back[2 * dest[q] + earlier]
    for copy in arrivals + pairs + sums + returns:
        copy.wait_send()


def convolve(fine, slot, neighbours, kernel_ops, filter_matrix):
    vm = pl.BlockSpec(memory_space=pltpu.VMEM)
    sm = pl.BlockSpec(memory_space=pltpu.SMEM)
    low = ((1280, 256), (2560, 256), (2560, 256), (TERMS, 96, 128), (128, 384), (256, 640), (64, 640), (384, 512))
    scratch = [pltpu.VMEM(shape, f32) for shape in ((16, 32, 128), (216, 1024), (32, 1024), (32, 128))]
    scratch += [pltpu.VMEM(shape, bf16) for shape in low]
    scratch += [pltpu.VMEM(shape, f32) for shape in ((216, 1024), (16, 72, 128), (16, 72, 128), (3, 16, 32, 128), (N * BOX_LINE, 128))]
    scratch += [pltpu.VMEM(shape, bf16) for shape in ((3, 1024, 256), (2048, 256), (2048, 256))]
    scratch += [pltpu.VMEM((N * SIDE_LINE, 128), f32)] * 3
    scratch += [
        pltpu.VMEM(shape, f32)
        for shape in (
            (256, 384), (4, 2, 2, 256, 128), (1024, 128), (4, 2, 256, 128), (4, 3, 128, 128), (4, 3, 128, 128),
            (4, 128, 128), (32, 32, 128), (32, 32, 128),
        )
    ]
    scratch += [pltpu.SemaphoreType.DMA((n,)) for n in (16, 16, 4, 4, 4, 4, 12, 12, 16, 16)]
    return pl.pallas_call(
        convolve_kernel,
        out_shape=jax.ShapeDtypeStruct((512, 128), f32),
        in_specs=[vm, sm, sm, vm, vm],
        out_specs=vm,
        scratch_shapes=scratch,
        compiler_params=pltpu.CompilerParams(
            collective_id=1, has_side_effects=True, vmem_limit_bytes=60 * 2**20
        ),
    )(fine, slot, neighbours, kernel_ops, filter_matrix)


def local(fine_coeffs, fine_slot, neighbours, filter_matrix, kernel_ops):
    held_boxes, volume = fine_coeffs.shape
    boxes = jnp.transpose(fine_coeffs.reshape(2, 8, 32, 128), (0, 2, 1, 3)).reshape(512, 128)
    out = convolve(boxes, fine_slot, neighbours.T, jnp.transpose(kernel_ops, (1, 2, 0, 3)), filter_matrix)
    return jnp.transpose(out.reshape(2, 32, 8, 128), (0, 2, 1, 3)).reshape(held_boxes, volume)


def solution(mesh):
    in_specs = (P(("row", "col"), None), P(("row", "col")), P("row", None), P(), P())
    out_specs = P(("row", "col"), None)
    return jax.shard_map(local, mesh=mesh, in_specs=in_specs, out_specs=out_specs, check_vma=False)
```

```python
import jax
import jax.numpy as jnp
from jax import lax
from jax.experimental import pallas as pl
from jax.experimental.pallas import tpu as pltpu
from jax.sharding import PartitionSpec as P

f32, bf16 = jnp.float32, jnp.bfloat16
TERMS, N, PAIRS = 20, 32, 10
SIDE_LINE, OWN_LINE, MAT_LINE = TERMS * N + 8, PAIRS * N + 8, N + 8


def split(x):
    hi = x.astype(bf16)
    return hi, (x - hi.astype(f32)).astype(bf16)


def dot(a, b):
    return jnp.dot(a, b, preferred_element_type=f32)


def dot_t(a, b):
    return lax.dot_general(a, b, (((1,), (1,)), ((), ())), preferred_element_type=f32)


def low_half(rows):
    return lax.broadcasted_iota(jnp.int32, (rows, 128), 1) < 64


def centre_lines(xk, wz, wy, t_hi, t_lo, ys):
    mask = low_half(N)

    def pair(mp, carry):
        weights = wz[pl.ds(pl.multiple_of(mp * 128, 128), 128), 0:192]
        for q in range(1):
            z = dot_t(xk[q * 1024 : (q + 1) * 1024, 0:192], weights)
            hi, lo = split(z)
            t_hi[q * 1024 : (q + 1) * 1024, 0:128] = hi
            t_lo[q * 1024 : (q + 1) * 1024, 0:128] = lo
        left = jnp.concatenate([wy[mp * 2, 0:N, 0:96], wy[mp * 2 + 1, 0:N, 0:96]], axis=0)

        for i in range(N):
            at = slice(i * N, (i + 1) * N)
            hi, lo = t_hi[at, 0:128], t_lo[at, 0:128]
            y = dot(left, jnp.concatenate([hi, lo, hi], axis=0))
            ys[pl.ds(mp * N + i, N, stride=OWN_LINE), :] = jnp.where(mask, y[:N], y[N:])
        return carry

    lax.fori_loop(0, PAIRS, pair, 0)


def centre_columns(wx, ys, out):
    def column(b, carry):
        at = pl.ds(pl.multiple_of(b * OWN_LINE, 8), PAIRS * N)
        hi, lo = split(ys[at, :])
        first = dot(wx[:, 0:320], hi)
        r = first[:64] + first[64:] + dot(wx[0:64, 0:320], lo)
        out[pl.ds(pl.multiple_of(b * N, N), N), :] = r[:N] + pltpu.roll(r[N:], 64, 1)
        return carry

    lax.fori_loop(0, N, column, 0, unroll=8)


def sides_lines(xkb, xka, wzb, wza, wy, t_hi, t_lo, ya, yb, yc):
    mask = low_half(N)

    def pair(mp, carry):
        for xk, wz, base in ((xkb, wzb, 0), (xka, wza, 128)):
            weights = wz[pl.ds(pl.multiple_of(mp * 256, 256), 256), 0:192]
            for q in range(1):
                z = dot_t(xk[q * 1024 : (q + 1) * 1024, 0:192], weights)
                hi, lo = split(z)
                for odd in range(2):
                    t_hi[odd * 1024 + q * 1024 : odd * 1024 + (q + 1) * 1024, base : base + 128] = hi[
                        :, odd * 128 : (odd + 1) * 128
                    ]
                    t_lo[odd * 1024 + q * 1024 : odd * 1024 + (q + 1) * 1024, base : base + 128] = lo[
                        :, odd * 128 : (odd + 1) * 128
                    ]
        for odd in range(2):
            m = mp * 2 + odd
            left = wy[m, :, 0:96]

            for i in range(N):
                at = slice(odd * 1024 + i * N, odd * 1024 + (i + 1) * N)
                hi, lo = t_hi[at, :], t_lo[at, :]
                y = dot(left, jnp.concatenate([hi, lo, hi], axis=0))
                to = pl.ds(m * N + i, N, stride=SIDE_LINE)
                ya[to, :] = y[:N, :128]
                yb[to, :] = y[:N, 128:]
                yc[to, :] = jnp.where(mask, y[N : 2 * N, :128], y[2 * N :, 128:])
        return carry

    lax.fori_loop(0, PAIRS, pair, 0)


def sides_columns(first_b, wx, wx0, ya, yb, yc, out):
    mask = low_half(N)

    def column(k, carry):
        at = pl.ds(pl.multiple_of((first_b + k) * SIDE_LINE, 8), TERMS * N)
        rows = pl.ds(pl.multiple_of(k * N, N), N)
        hi, lo = split(ya[at, :])
        first = dot(wx[0:128, :], hi)
        r = first[:64] + first[64:128] + dot(wx[0:64, :], lo)
        out[rows, 0:128] = jnp.where(mask, r[:N], r[N:])
        hi, lo = split(yb[at, :])
        first = dot(wx[128:256, :], hi)
        r = first[:64] + first[64:128] + dot(wx[128:192, :], lo)
        out[rows, 128:256] = jnp.where(mask, r[:N], r[N:])
        hi, lo = split(yc[at, :])
        first = dot(wx0[...], hi)
        out[rows, 256:384] = first[:N] + first[N:] + dot(wx0[0:N, :], lo)
        return carry

    lax.fori_loop(0, 8, column, 0, unroll=8)


def spread(h, lanes, pick):
    shape = (N, lanes)
    chosen = pick(lax.broadcasted_iota(jnp.int32, shape, 1)) == lax.broadcasted_iota(jnp.int32, shape, 0)
    chosen = jnp.where(chosen, 1.0, 0.0).astype(bf16)
    hi = split(h)[0]
    mid, low = split(h - hi.astype(f32))
    return dot(hi, chosen) + (dot(mid, chosen) + dot(low, chosen))


def fold(ops, h, f, hx, ht, folded, kron, mats):
    for k in range(9):
        f[k * 24 : k * 24 + TERMS, :] = ops[k // 3, k % 3]
        f[k * 24 + TERMS : (k + 1) * 24, :] = jnp.zeros((4, 1024), f32)
    hx[...] = spread(h[...], 1024, lambda lane: lane // N)
    ht[...] = spread(h[...], 128, lambda lane: lane % N)

    def row(a, carry):
        wide = hx[pl.ds(a, 1), :]
        for g in range(8):
            at = pl.ds(pl.multiple_of(g * 1024 + a * N, N), N)
            kron[at, :] = wide[:, g * 128 : (g + 1) * 128] * ht[...]
        return carry

    lax.fori_loop(0, N, row, 0, unroll=4)
    f_hi, f_lo = split(f[...])
    for n in range(4):
        left, right = split(kron[2048 * n : 2048 * n + 1024, :]), split(kron[2048 * n + 1024 : 2048 * n + 2048, :])
        hi, lo = jnp.concatenate([left[0], right[0]], axis=1), jnp.concatenate([left[1], right[1]], axis=1)
        folded[:, n * 256 : (n + 1) * 256] = dot(f_hi, hi) + dot(f_lo, hi) + dot(f_hi, lo)
    for g in range(8):
        piece = folded[:, g * 128 : (g + 1) * 128]
        for k in range(4):
            turned = piece if k == 0 else pltpu.roll(piece, 128 - 32 * k, 1)
            mats[pl.ds(4 * g + k, 216, stride=MAT_LINE), :] = turned


def pack(mats, wzo, wzb, wza, wys, wxo, wxs, wx0):
    mask = lax.broadcasted_iota(jnp.int32, (N, 128), 1) < N

    def matrix(m, axis, offset):
        start = ((axis * 3 + offset) * 24 + m) * MAT_LINE
        v = mats[pl.ds(start if isinstance(m, int) else pl.multiple_of(start, 8), N), :]
        return jnp.where(mask, v, 0.0)

    def parts(v):
        hi = v.astype(bf16).astype(f32)
        return hi, v - hi

    def term(m, carry):
        for t, offset in enumerate((1, 2, 0)):
            hi, lo = parts(matrix(m, 1, offset))
            wys[m, t * N : (t + 1) * N, :] = (hi + pltpu.roll(hi, 32, 1) + pltpu.roll(lo, 64, 1)).astype(bf16)
        for offset, places in ((0, ((wza, 0),)), (1, ((wzo, 0), (wzb, 0), (wza, 64))), (2, ((wzb, 64),))):
            hi, lo = parts(matrix(m, 2, offset))
            first = hi + pltpu.roll(hi, 64, 1)
            for ref, base in places:
                start = m * (64 if ref is wzo else 128) + base
                for p in range(2):
                    at = pl.ds(pl.multiple_of(start + p * N, N), N)
                    ref[at, 0:128] = (pltpu.roll(first, 32, 1) if p else first).astype(bf16)
                    ref[at, 128:256] = (pltpu.roll(lo, 32, 1) if p else lo).astype(bf16)
        return carry

    lax.fori_loop(0, TERMS, term, 0)

    def wide(terms, offset):
        total = None
        for k, m in enumerate(terms):
            v = matrix(m, 0, offset)
            v = pltpu.roll(v, 32 * k, 1) if k else v
            total = v if total is None else total + v
        return split(total)

    for g in range(5):
        at = slice(g * 128, (g + 1) * 128)
        for offset, places in ((2, ((wxs, 0, 64),)), (1, ((wxs, 32, 96), (wxs, 128, 192), (wx0, 0, 32))), (0, ((wxs, 160, 224),))):
            hi, lo = wide(range(4 * g, 4 * g + 4), offset)
            for ref, high_at, low_at in places:
                ref[high_at : high_at + N, at] = hi
                ref[low_at : low_at + N, at] = lo
    for g in range(3):
        at = slice(g * 128, (g + 1) * 128)
        for odd in range(2):
            hi, lo = wide([2 * mp + odd for mp in range(4 * g, min(4 * g + 4, PAIRS))], 1)
            wxo[odd * N : (odd + 1) * N, at] = hi
            wxo[64 + odd * N : 64 + (odd + 1) * N, at] = lo


MESH = pl.DeviceIdType.MESH
Y, CORES, ROWS = 4, 2, 16


def start_copy(src, dst, s, r, peer):
    copy = pltpu.make_async_remote_copy(
        src_ref=src, dst_ref=dst, send_sem=s, recv_sem=r, device_id=peer, device_id_type=MESH
    )
    copy.start()
    return copy


BOX_LINE = N + 8


def lay_out(boxes, lines, xs):
    piece = lax.broadcasted_iota(jnp.int32, (16, 128), 1) // 16

    def octant(at, carry):
        ox, oy, jh = at // 4, at // 2 % 2, at % 2
        rows = [boxes[p * 8 + ox * 4 + oy * 2 + oz, pl.ds(jh, 16, stride=2), :] for p in range(2) for oz in range(2)]
        for j in range(8):
            x = None
            for k in range(4):
                shift = (16 * (k - j)) % 128
                v = pltpu.roll(rows[k], shift, 1) if shift else rows[k]
                x = v if x is None else jnp.where(piece == k, v, x)
            lines[pl.ds(ox * 16 * BOX_LINE + oy * 16 + jh * 8 + j, 16, stride=BOX_LINE), :] = x
        return carry

    lax.fori_loop(0, 8, octant, 0, unroll=4)
    mask = low_half(N)

    def line(i, carry):
        v = lines[pl.ds(pl.multiple_of(i * BOX_LINE, 8), N), :]
        hi = v.astype(bf16).astype(f32)
        at = pl.ds(pl.multiple_of(i * N, N), N)
        xs[at, 0:128] = jnp.where(mask, hi, pltpu.roll(v - hi, 64, 1)).astype(bf16)
        xs[at, 128:256] = v.astype(bf16)
        return carry

    lax.fori_loop(0, N, line, 0, unroll=8)


def lay_back(applied, boxes):
    piece = lax.broadcasted_iota(jnp.int32, (16, 128), 1) // 16

    def octants(at, carry):
        ox, oy, jh = at // 4, at // 2 % 2, at % 2
        start = (oy * 16 + jh * 8) * N + ox * 16
        lines = [applied[pl.ds(pl.multiple_of(start + j * N, 16), 16), :] for j in range(8)]
        for p in range(2):
            for oz in range(2):
                box = None
                for j in range(8):
                    shift = (16 * j - p * 32 - oz * 16) % 128
                    v = pltpu.roll(lines[j], shift, 1) if shift else lines[j]
                    box = v if box is None else jnp.where(piece == j, v, box)
                boxes[p * 8 + ox * 4 + oy * 2 + oz, pl.ds(jh, 16, stride=2), :] = box
        return carry

    lax.fori_loop(0, 8, octants, 0, unroll=2)


def choose(neighbours, col, sel):
    lane = lax.broadcasted_iota(jnp.int32, (N, 128), 1)
    same = lane % N == lax.broadcasted_iota(jnp.int32, (N, 128), 0)
    for d, k in enumerate((1, 5, 4, 0, 3, 2)):
        for g in range(4):
            held = None
            for n in range(4):
                sender = neighbours[k, (g % 2 * 2 + n // 2) * 4 + g // 2 * 2 + n % 2]
                v = jnp.where(sender >= 0, sender % 16 - 2 * col, -1)
                held = v if held is None else jnp.where(lane // N == n, v, held)
            for p in range(2):
                at = slice((d * 2 + p) * N, (d * 2 + p + 1) * N)
                sel[at, g * 128 : (g + 1) * 128] = jnp.where(same & (held == p), 1.0, 0.0).astype(bf16)


def convolve_kernel(fine, slot, neighbours, ops, h, out, own, f, hx, ht,
                    wzo, wzb, wza, wys, wxo, wxs, wx0, sel, folded, leaving, arrived, boxes, lines, xs,
                    t_hi, t_lo, ya, yb, yc, terms, part, centre, from_core, pair_sum, from_y, total,
                    returned, back, s1, r1, s2, r2, s3, r3, s4, r4, s6, r6):
    row, col = lax.axis_index("row"), lax.axis_index("col")
    y, core = col // CORES, col % CORES
    sibling = (row, y * CORES + (1 - core))
    across = [(row, (y + 1 + d) % Y * CORES + core) for d in range(Y - 1)]
    peers = [sibling] + across + [((row + d) % ROWS, col) for d in range(1, ROWS)]
    barrier = pltpu.get_barrier_semaphore()
    for peer in peers:
        pl.semaphore_signal(barrier, inc=1, device_id=peer, device_id_type=MESH)

    for q in range(16):
        own[q] = fine[pl.ds(q // 8 * 256 + q % 8, N, stride=8), :]
    slots = [slot[q] for q in range(16)]
    dest = [v // 128 for v in slots]
    first_row = lax.broadcasted_iota(jnp.int32, (8, 128), 0) == 0
    pl.semaphore_wait(barrier, len(peers))

    arrivals = []
    for d in list(range(1, ROWS)) + [0]:
        to = (row + d) % ROWS
        target = arrived.at[row] if d == 0 else leaving.at[d]
        first, last = jnp.int32(16), jnp.int32(-1)
        for q in range(16):
            here = dest[q] == to
            first = jnp.minimum(first, jnp.where(here, q, 16))
            last = jnp.maximum(last, jnp.where(here, q, -1))
        tag = []
        for k, q in enumerate((jnp.minimum(first, 15), jnp.maximum(last, 0))):
            target[k * N : (k + 1) * N, :] = own[q]
            tag.append(jnp.where(last >= 0, slot[q] % 16, -1).astype(f32))
        target[64:72, :] = jnp.where(first_row, tag[0], tag[1])
        if d:
            arrivals.append(start_copy(leaving.at[d], arrived.at[row], s1.at[d], r1.at[d], (to, col)))
    fold(ops, h, f, hx, ht, folded, yb, ya)
    pack(ya, wzo, wzb, wza, wys, wxo, wxs, wx0)
    choose(neighbours, col, sel)
    for copy in arrivals:
        copy.wait_recv()

    def place(group, carry):
        total = [[jnp.zeros((8, 128), f32)] * 4 for n in range(4)]
        for k in range(ROWS):
            for s in range(2):
                tag = jnp.broadcast_to(arrived[k, 64 + s : 65 + s, :], (8, 128))
                data = [arrived[k, s * 32 + c * 8 : s * 32 + c * 8 + 8, :] for c in range(4)]
                for n in range(4):
                    hit = tag == (group * 4 + n).astype(f32)
                    total[n] = [jnp.where(hit, data[c], total[n][c]) for c in range(4)]
        for n in range(4):
            for c in range(4):
                boxes[0, group * 4 + n, c * 8 : (c + 1) * 8, :] = total[n][c]
        return carry

    hops = []
    for p in range(2):
        lax.fori_loop(2 * p, 2 * p + 2, place, 0)
        for k, to in ((1, (row + 1) % ROWS), (2, (row + ROWS - 1) % ROWS)):
            at, n = pl.ds(8 * p, 8), 2 * p + k - 1
            hops.append(start_copy(boxes.at[0, at], boxes.at[k, at], s2.at[n], r2.at[n], (to, col)))
    lay_out(boxes.at[0], lines, xs.at[0])
    for k in (1, 2):
        hops[k - 1].wait_recv()
        hops[k + 1].wait_recv()
        lay_out(boxes.at[k], lines, xs.at[k])

    sides_lines(xs.at[1], xs.at[2], wzb, wza, wys, t_hi, t_lo, ya, yb, yc)
    pairs, sums = [], []
    mask = low_half(128)

    def over_pair(c):
        pairs[c].wait_recv()
        for d in (1, 0, 2, 3):
            to = (y + 1 + d) % Y
            v = part[c, core, to // 2] + from_core[c, to // 2]
            odd = to % 2 == 1
            low = jnp.where(odd, pltpu.roll(v[:128], 64, 1), v[:128])
            high = jnp.where(odd, v[128:], pltpu.roll(v[128:], 64, 1))
            v = jnp.where(mask, low, high)
            if d < Y - 1:
                pair_sum[c, d] = v
                k = c * (Y - 1) + d
                sums.append(start_copy(pair_sum.at[c, d], from_y.at[c, d], s4.at[k], r4.at[k], across[d]))
            else:
                total[c] = v

    for c in range(4):
        sides_columns(8 * c, wxs, wx0, ya, yb, yc, terms)
        hi, lo = split(terms[...])
        summed = dot(hi, sel[...]) + dot(lo, sel[...])
        for k in range(Y):
            part[c, k // 2, k % 2] = summed[:, k * 128 : (k + 1) * 128]
        pairs.append(start_copy(part.at[c, 1 - core], from_core.at[c], s3.at[c], r3.at[c], sibling))
        if c:
            over_pair(c - 1)
    over_pair(3)
    centre_lines(xs.at[0], wzo, wys, t_hi, t_lo, ya)
    centre_columns(wxo, ya, centre)
    for c in range(4):
        for d in range(Y - 1):
            sums[c * (Y - 1) + d].wait_recv()
        v = total[c] + from_y[c, 0] + from_y[c, 1] + from_y[c, 2]
        at = slice(c * 256, c * 256 + 128)
        centre[at, :] = centre[at, :] + v
        at = slice(c * 256 + 128, c * 256 + 256)
        centre[at, :] = centre[at, :] + pltpu.roll(v, 64, 1)

    result = boxes.at[0]
    for hop in hops:
        hop.wait_send()
    lay_back(centre, result)

    def give_back(d, carry):
        to = (row + d) % ROWS
        hit = []
        for s in range(2):
            tag = jnp.broadcast_to(arrived[to, 64 + s : 65 + s, :], (8, 128))
            hit.append([tag == float(k) for k in range(16)])
        for c in range(4):
            rows = slice(c * 8, (c + 1) * 8)
            v = [result[0, rows, :]] * 2
            for k in range(1, 16):
                box = result[k, rows, :]
                v = [jnp.where(hit[s][k], box, v[s]) for s in range(2)]
            for s in range(2):
                returned[d * 2 + s, rows, :] = v[s]
        return carry

    lax.fori_loop(0, ROWS, give_back, 0)
    returns = []
    for d in range(1, ROWS):
        src, dst = returned.at[pl.ds(2 * d, 2)], back.at[pl.ds(row * 2, 2)]
        returns.append(start_copy(src, dst, s6.at[d], r6.at[d], ((row + d) % ROWS, col)))
    for s in range(2):
        back[row * 2 + s] = returned[s]
    for copy in returns:
        copy.wait_recv()
    for q in range(16):
        earlier = jnp.int32(0)
        for k in range(q):
            earlier = jnp.where(dest[k] == dest[q], 1, earlier)
        out[pl.ds(q // 8 * 256 + q % 8, N, stride=8), :] = back[2 * dest[q] + earlier]
    for copy in arrivals + pairs + sums + returns:
        copy.wait_send()


def convolve(fine, slot, neighbours, kernel_ops, filter_matrix):
    vm = pl.BlockSpec(memory_space=pltpu.VMEM)
    sm = pl.BlockSpec(memory_space=pltpu.SMEM)
    low = ((1280, 256), (2560, 256), (2560, 256), (TERMS, 96, 128), (128, 384), (256, 640), (64, 640), (384, 512))
    scratch = [pltpu.VMEM(shape, f32) for shape in ((16, 32, 128), (216, 1024), (32, 1024), (32, 128))]
    scratch += [pltpu.VMEM(shape, bf16) for shape in low]
    scratch += [pltpu.VMEM(shape, f32) for shape in ((216, 1024), (16, 72, 128), (16, 72, 128), (3, 16, 32, 128), (N * BOX_LINE, 128))]
    scratch += [pltpu.VMEM(shape, bf16) for shape in ((3, 1024, 256), (2048, 256), (2048, 256))]
    scratch += [pltpu.VMEM((N * SIDE_LINE, 128), f32)] * 3
    scratch += [
        pltpu.VMEM(shape, f32)
        for shape in (
            (256, 384), (4, 2, 2, 256, 128), (1024, 128), (4, 2, 256, 128), (4, 3, 128, 128), (4, 3, 128, 128),
            (4, 128, 128), (32, 32, 128), (32, 32, 128),
        )
    ]
    scratch += [pltpu.SemaphoreType.DMA((n,)) for n in (16, 16, 4, 4, 4, 4, 12, 12, 16, 16)]
    return pl.pallas_call(
        convolve_kernel,
        out_shape=jax.ShapeDtypeStruct((512, 128), f32),
        in_specs=[vm, sm, sm, vm, vm],
        out_specs=vm,
        scratch_shapes=scratch,
        compiler_params=pltpu.CompilerParams(
            collective_id=1, has_side_effects=True, vmem_limit_bytes=60 * 2**20
        ),
    )(fine, slot, neighbours, kernel_ops, filter_matrix)


def local(fine_coeffs, fine_slot, neighbours, filter_matrix, kernel_ops):
    held_boxes, volume = fine_coeffs.shape
    boxes = jnp.transpose(fine_coeffs.reshape(2, 8, 32, 128), (0, 2, 1, 3)).reshape(512, 128)
    out = convolve(boxes, fine_slot, neighbours.T, jnp.transpose(kernel_ops, (1, 2, 0, 3)), filter_matrix)
    return jnp.transpose(out.reshape(2, 32, 8, 128), (0, 2, 1, 3)).reshape(held_boxes, volume)


def solution(mesh):
    in_specs = (P(("row", "col"), None), P(("row", "col")), P("row", None), P(), P())
    out_specs = P(("row", "col"), None)
    return jax.shard_map(local, mesh=mesh, in_specs=in_specs, out_specs=out_specs, check_vma=False)
```

```python
import jax
import jax.numpy as jnp
from jax import lax
from jax.experimental import pallas as pl
from jax.experimental.pallas import tpu as pltpu
from jax.sharding import PartitionSpec as P

f32, bf16 = jnp.float32, jnp.bfloat16
TERMS, N, PAIRS = 20, 32, 10
SIDE_LINE, OWN_LINE, MAT_LINE = TERMS * N + 8, PAIRS * N + 8, N + 8


def split(x):
    hi = x.astype(bf16)
    return hi, (x - hi.astype(f32)).astype(bf16)


def dot(a, b):
    return jnp.dot(a, b, preferred_element_type=f32)


def dot_t(a, b):
    return lax.dot_general(a, b, (((1,), (1,)), ((), ())), preferred_element_type=f32)


def low_half(rows):
    return lax.broadcasted_iota(jnp.int32, (rows, 128), 1) < 64


def centre_lines(xk, wz, wy, t_hi, t_lo, ys):
    mask = low_half(N)

    def pair(mp, carry):
        weights = wz[pl.ds(pl.multiple_of(mp * 128, 128), 128), 0:192]
        for q in range(1):
            z = dot_t(xk[q * 1024 : (q + 1) * 1024, 0:192], weights)
            hi, lo = split(z)
            t_hi[q * 1024 : (q + 1) * 1024, 0:128] = hi
            t_lo[q * 1024 : (q + 1) * 1024, 0:128] = lo
        left = jnp.concatenate([wy[mp * 2, 0:N, 0:96], wy[mp * 2 + 1, 0:N, 0:96]], axis=0)

        for i in range(N):
            at = slice(i * N, (i + 1) * N)
            hi, lo = t_hi[at, 0:128], t_lo[at, 0:128]
            y = dot(left, jnp.concatenate([hi, lo, hi], axis=0))
            ys[pl.ds(mp * N + i, N, stride=OWN_LINE), :] = jnp.where(mask, y[:N], y[N:])
        return carry

    lax.fori_loop(0, PAIRS, pair, 0)


def centre_columns(wx, ys, out):
    def column(b, carry):
        at = pl.ds(pl.multiple_of(b * OWN_LINE, 8), PAIRS * N)
        hi, lo = split(ys[at, :])
        first = dot(wx[:, 0:320], hi)
        r = first[:64] + first[64:] + dot(wx[0:64, 0:320], lo)
        out[pl.ds(pl.multiple_of(b * N, N), N), :] = r[:N] + pltpu.roll(r[N:], 64, 1)
        return carry

    lax.fori_loop(0, N, column, 0, unroll=8)


def sides_lines(xkb, xka, wzb, wza, wy, t_hi, t_lo, ya, yb, yc):
    mask = low_half(N)

    def pair(mp, carry):
        for xk, wz, base in ((xkb, wzb, 0), (xka, wza, 128)):
            weights = wz[pl.ds(pl.multiple_of(mp * 256, 256), 256), 0:192]
            for q in range(1):
                z = dot_t(xk[q * 1024 : (q + 1) * 1024, 0:192], weights)
                hi, lo = split(z)
                for odd in range(2):
                    t_hi[odd * 1024 + q * 1024 : odd * 1024 + (q + 1) * 1024, base : base + 128] = hi[
                        :, odd * 128 : (odd + 1) * 128
                    ]
                    t_lo[odd * 1024 + q * 1024 : odd * 1024 + (q + 1) * 1024, base : base + 128] = lo[
                        :, odd * 128 : (odd + 1) * 128
                    ]
        for odd in range(2):
            m = mp * 2 + odd
            left = wy[m, :, 0:96]

            for i in range(N):
                at = slice(odd * 1024 + i * N, odd * 1024 + (i + 1) * N)
                hi, lo = t_hi[at, :], t_lo[at, :]
                y = dot(left, jnp.concatenate([hi, lo, hi], axis=0))
                to = pl.ds(m * N + i, N, stride=SIDE_LINE)
                ya[to, :] = y[:N, :128]
                yb[to, :] = y[:N, 128:]
                yc[to, :] = jnp.where(mask, y[N : 2 * N, :128], y[2 * N :, 128:])
        return carry

    lax.fori_loop(0, PAIRS, pair, 0)


def sides_columns(first_b, wx, wx0, ya, yb, yc, out):
    mask = low_half(N)

    def column(k, carry):
        at = pl.ds(pl.multiple_of((first_b + k) * SIDE_LINE, 8), TERMS * N)
        rows = pl.ds(pl.multiple_of(k * N, N), N)
        hi, lo = split(ya[at, :])
        first = dot(wx[0:128, :], hi)
        r = first[:64] + first[64:128] + dot(wx[0:64, :], lo)
        out[rows, 0:128] = jnp.where(mask, r[:N], r[N:])
        hi, lo = split(yb[at, :])
        first = dot(wx[128:256, :], hi)
        r = first[:64] + first[64:128] + dot(wx[128:192, :], lo)
        out[rows, 128:256] = jnp.where(mask, r[:N], r[N:])
        hi, lo = split(yc[at, :])
        first = dot(wx0[...], hi)
        out[rows, 256:384] = first[:N] + first[N:] + dot(wx0[0:N, :], lo)
        return carry

    lax.fori_loop(0, 8, column, 0, unroll=8)


def spread(h, lanes, pick):
    shape = (N, lanes)
    chosen = pick(lax.broadcasted_iota(jnp.int32, shape, 1)) == lax.broadcasted_iota(jnp.int32, shape, 0)
    chosen = jnp.where(chosen, 1.0, 0.0).astype(bf16)
    hi = split(h)[0]
    mid, low = split(h - hi.astype(f32))
    return dot(hi, chosen) + (dot(mid, chosen) + dot(low, chosen))


def fold(ops, h, f, hx, ht, folded, kron, mats):
    for k in range(9):
        f[k * 24 : k * 24 + TERMS, :] = ops[k // 3, k % 3]
        f[k * 24 + TERMS : (k + 1) * 24, :] = jnp.zeros((4, 1024), f32)
    hx[...] = spread(h[...], 1024, lambda lane: lane // N)
    ht[...] = spread(h[...], 128, lambda lane: lane % N)

    def row(a, carry):
        wide = hx[pl.ds(a, 1), :]
        for g in range(8):
            at = pl.ds(pl.multiple_of(g * 1024 + a * N, N), N)
            kron[at, :] = wide[:, g * 128 : (g + 1) * 128] * ht[...]
        return carry

    lax.fori_loop(0, N, row, 0, unroll=4)
    f_hi, f_lo = split(f[...])
    for n in range(4):
        left, right = split(kron[2048 * n : 2048 * n + 1024, :]), split(kron[2048 * n + 1024 : 2048 * n + 2048, :])
        hi, lo = jnp.concatenate([left[0], right[0]], axis=1), jnp.concatenate([left[1], right[1]], axis=1)
        folded[:, n * 256 : (n + 1) * 256] = dot(f_hi, hi) + dot(f_lo, hi) + dot(f_hi, lo)
    for g in range(8):
        piece = folded[:, g * 128 : (g + 1) * 128]
        for k in range(4):
            turned = piece if k == 0 else pltpu.roll(piece, 128 - 32 * k, 1)
            mats[pl.ds(4 * g + k, 216, stride=MAT_LINE), :] = turned


def pack(mats, wzo, wzb, wza, wys, wxo, wxs, wx0):
    mask = lax.broadcasted_iota(jnp.int32, (N, 128), 1) < N

    def matrix(m, axis, offset):
        start = ((axis * 3 + offset) * 24 + m) * MAT_LINE
        v = mats[pl.ds(start if isinstance(m, int) else pl.multiple_of(start, 8), N), :]
        return jnp.where(mask, v, 0.0)

    def parts(v):
        hi = v.astype(bf16).astype(f32)
        return hi, v - hi

    def term(m, carry):
        for t, offset in enumerate((1, 2, 0)):
            hi, lo = parts(matrix(m, 1, offset))
            wys[m, t * N : (t + 1) * N, :] = (hi + pltpu.roll(hi, 32, 1) + pltpu.roll(lo, 64, 1)).astype(bf16)
        for offset, places in ((0, ((wza, 0),)), (1, ((wzo, 0), (wzb, 0), (wza, 64))), (2, ((wzb, 64),))):
            hi, lo = parts(matrix(m, 2, offset))
            first = hi + pltpu.roll(hi, 64, 1)
            for ref, base in places:
                start = m * (64 if ref is wzo else 128) + base
                for p in range(2):
                    at = pl.ds(pl.multiple_of(start + p * N, N), N)
                    ref[at, 0:128] = (pltpu.roll(first, 32, 1) if p else first).astype(bf16)
                    ref[at, 128:256] = (pltpu.roll(lo, 32, 1) if p else lo).astype(bf16)
        return carry

    lax.fori_loop(0, TERMS, term, 0)

    def wide(terms, offset):
        total = None
        for k, m in enumerate(terms):
            v = matrix(m, 0, offset)
            v = pltpu.roll(v, 32 * k, 1) if k else v
            total = v if total is None else total + v
        return split(total)

    for g in range(5):
        at = slice(g * 128, (g + 1) * 128)
        for offset, places in ((2, ((wxs, 0, 64),)), (1, ((wxs, 32, 96), (wxs, 128, 192), (wx0, 0, 32))), (0, ((wxs, 160, 224),))):
            hi, lo = wide(range(4 * g, 4 * g + 4), offset)
            for ref, high_at, low_at in places:
                ref[high_at : high_at + N, at] = hi
                ref[low_at : low_at + N, at] = lo
    for g in range(3):
        at = slice(g * 128, (g + 1) * 128)
        for odd in range(2):
            hi, lo = wide([2 * mp + odd for mp in range(4 * g, min(4 * g + 4, PAIRS))], 1)
            wxo[odd * N : (odd + 1) * N, at] = hi
            wxo[64 + odd * N : 64 + (odd + 1) * N, at] = lo


MESH = pl.DeviceIdType.MESH
Y, CORES, ROWS = 4, 2, 16
FAR_FIRST = (10, 6, 9, 11, 14, 2, 8, 5, 7, 13, 15, 1, 3, 4, 12)


def start_copy(src, dst, s, r, peer):
    copy = pltpu.make_async_remote_copy(
        src_ref=src, dst_ref=dst, send_sem=s, recv_sem=r, device_id=peer, device_id_type=MESH
    )
    copy.start()
    return copy


BOX_LINE = N + 8


def lay_out(boxes, lines, xs):
    piece = lax.broadcasted_iota(jnp.int32, (16, 128), 1) // 16

    def octant(at, carry):
        ox, oy, jh = at // 4, at // 2 % 2, at % 2
        rows = [boxes[p * 8 + ox * 4 + oy * 2 + oz, pl.ds(jh, 16, stride=2), :] for p in range(2) for oz in range(2)]
        for j in range(8):
            x = None
            for k in range(4):
                shift = (16 * (k - j)) % 128
                v = pltpu.roll(rows[k], shift, 1) if shift else rows[k]
                x = v if x is None else jnp.where(piece == k, v, x)
            lines[pl.ds(ox * 16 * BOX_LINE + oy * 16 + jh * 8 + j, 16, stride=BOX_LINE), :] = x
        return carry

    lax.fori_loop(0, 8, octant, 0, unroll=4)
    mask = low_half(N)

    def line(i, carry):
        v = lines[pl.ds(pl.multiple_of(i * BOX_LINE, 8), N), :]
        hi = v.astype(bf16).astype(f32)
        at = pl.ds(pl.multiple_of(i * N, N), N)
        xs[at, 0:128] = jnp.where(mask, hi, pltpu.roll(v - hi, 64, 1)).astype(bf16)
        xs[at, 128:256] = v.astype(bf16)
        return carry

    lax.fori_loop(0, N, line, 0, unroll=8)


def lay_back(applied, boxes):
    piece = lax.broadcasted_iota(jnp.int32, (16, 128), 1) // 16

    def octants(at, carry):
        ox, oy, jh = at // 4, at // 2 % 2, at % 2
        start = (oy * 16 + jh * 8) * N + ox * 16
        lines = [applied[pl.ds(pl.multiple_of(start + j * N, 16), 16), :] for j in range(8)]
        for p in range(2):
            for oz in range(2):
                box = None
                for j in range(8):
                    shift = (16 * j - p * 32 - oz * 16) % 128
                    v = pltpu.roll(lines[j], shift, 1) if shift else lines[j]
                    box = v if box is None else jnp.where(piece == j, v, box)
                boxes[p * 8 + ox * 4 + oy * 2 + oz, pl.ds(jh, 16, stride=2), :] = box
        return carry

    lax.fori_loop(0, 8, octants, 0, unroll=2)


def choose(neighbours, col, sel):
    lane = lax.broadcasted_iota(jnp.int32, (N, 128), 1)
    same = lane % N == lax.broadcasted_iota(jnp.int32, (N, 128), 0)
    for d, k in enumerate((1, 5, 4, 0, 3, 2)):
        for g in range(4):
            held = None
            for n in range(4):
                sender = neighbours[k, (g % 2 * 2 + n // 2) * 4 + g // 2 * 2 + n % 2]
                v = jnp.where(sender >= 0, sender % 16 - 2 * col, -1)
                held = v if held is None else jnp.where(lane // N == n, v, held)
            for p in range(2):
                at = slice((d * 2 + p) * N, (d * 2 + p + 1) * N)
                sel[at, g * 128 : (g + 1) * 128] = jnp.where(same & (held == p), 1.0, 0.0).astype(bf16)


def convolve_kernel(fine, slot, neighbours, ops, h, out, own, f, hx, ht,
                    wzo, wzb, wza, wys, wxo, wxs, wx0, sel, folded, leaving, arrived, boxes, lines, xs,
                    t_hi, t_lo, ya, yb, yc, terms, part, centre, from_core, pair_sum, from_y, total,
                    returned, back, s1, r1, s2, r2, s3, r3, s4, r4, s6, r6):
    row, col = lax.axis_index("row"), lax.axis_index("col")
    y, core = col // CORES, col % CORES
    sibling = (row, y * CORES + (1 - core))
    across = [(row, (y + 1 + d) % Y * CORES + core) for d in range(Y - 1)]
    peers = [sibling] + across + [((row + d) % ROWS, col) for d in range(1, ROWS)]
    barrier = pltpu.get_barrier_semaphore()
    for peer in peers:
        pl.semaphore_signal(barrier, inc=1, device_id=peer, device_id_type=MESH)

    for q in range(16):
        own[q] = fine[pl.ds(q // 8 * 256 + q % 8, N, stride=8), :]
    slots = [slot[q] for q in range(16)]
    dest = [v // 128 for v in slots]
    first_row = lax.broadcasted_iota(jnp.int32, (8, 128), 0) == 0
    pl.semaphore_wait(barrier, len(peers))

    arrivals = []
    for d in FAR_FIRST + (0,):
        to = (row + d) % ROWS
        target = arrived.at[row] if d == 0 else leaving.at[d]
        first, last = jnp.int32(16), jnp.int32(-1)
        for q in range(16):
            here = dest[q] == to
            first = jnp.minimum(first, jnp.where(here, q, 16))
            last = jnp.maximum(last, jnp.where(here, q, -1))
        tag = []
        for k, q in enumerate((jnp.minimum(first, 15), jnp.maximum(last, 0))):
            target[k * N : (k + 1) * N, :] = own[q]
            tag.append(jnp.where(last >= 0, slot[q] % 16, -1).astype(f32))
        target[64:72, :] = jnp.where(first_row, tag[0], tag[1])
        if d:
            arrivals.append(start_copy(leaving.at[d], arrived.at[row], s1.at[d], r1.at[d], (to, col)))
    fold(ops, h, f, hx, ht, folded, yb, ya)
    pack(ya, wzo, wzb, wza, wys, wxo, wxs, wx0)
    choose(neighbours, col, sel)
    for copy in arrivals:
        copy.wait_recv()

    def place(group, carry):
        total = [[jnp.zeros((8, 128), f32)] * 4 for n in range(4)]
        for k in range(ROWS):
            for s in range(2):
                tag = jnp.broadcast_to(arrived[k, 64 + s : 65 + s, :], (8, 128))
                data = [arrived[k, s * 32 + c * 8 : s * 32 + c * 8 + 8, :] for c in range(4)]
                for n in range(4):
                    hit = tag == (group * 4 + n).astype(f32)
                    total[n] = [jnp.where(hit, data[c], total[n][c]) for c in range(4)]
        for n in range(4):
            for c in range(4):
                boxes[0, group * 4 + n, c * 8 : (c + 1) * 8, :] = total[n][c]
        return carry

    hops = []
    for p in range(2):
        lax.fori_loop(2 * p, 2 * p + 2, place, 0)
        for k, to in ((1, (row + 1) % ROWS), (2, (row + ROWS - 1) % ROWS)):
            at, n = pl.ds(8 * p, 8), 2 * p + k - 1
            hops.append(start_copy(boxes.at[0, at], boxes.at[k, at], s2.at[n], r2.at[n], (to, col)))
    lay_out(boxes.at[0], lines, xs.at[0])
    for k in (1, 2):
        hops[k - 1].wait_recv()
        hops[k + 1].wait_recv()
        lay_out(boxes.at[k], lines, xs.at[k])

    sides_lines(xs.at[1], xs.at[2], wzb, wza, wys, t_hi, t_lo, ya, yb, yc)
    pairs, sums = [], []
    mask = low_half(128)

    def over_pair(c):
        pairs[c].wait_recv()
        for d in (1, 0, 2, 3):
            to = (y + 1 + d) % Y
            v = part[c, core, to // 2] + from_core[c, to // 2]
            odd = to % 2 == 1
            low = jnp.where(odd, pltpu.roll(v[:128], 64, 1), v[:128])
            high = jnp.where(odd, v[128:], pltpu.roll(v[128:], 64, 1))
            v = jnp.where(mask, low, high)
            if d < Y - 1:
                pair_sum[c, d] = v
                k = c * (Y - 1) + d
                sums.append(start_copy(pair_sum.at[c, d], from_y.at[c, d], s4.at[k], r4.at[k], across[d]))
            else:
                total[c] = v

    for c in range(4):
        sides_columns(8 * c, wxs, wx0, ya, yb, yc, terms)
        hi, lo = split(terms[...])
        summed = dot(hi, sel[...]) + dot(lo, sel[...])
        for k in range(Y):
            part[c, k // 2, k % 2] = summed[:, k * 128 : (k + 1) * 128]
        pairs.append(start_copy(part.at[c, 1 - core], from_core.at[c], s3.at[c], r3.at[c], sibling))
        if c:
            over_pair(c - 1)
    over_pair(3)
    centre_lines(xs.at[0], wzo, wys, t_hi, t_lo, ya)
    centre_columns(wxo, ya, centre)
    for c in range(4):
        for d in range(Y - 1):
            sums[c * (Y - 1) + d].wait_recv()
        v = total[c] + from_y[c, 0] + from_y[c, 1] + from_y[c, 2]
        at = slice(c * 256, c * 256 + 128)
        centre[at, :] = centre[at, :] + v
        at = slice(c * 256 + 128, c * 256 + 256)
        centre[at, :] = centre[at, :] + pltpu.roll(v, 64, 1)

    result = boxes.at[0]
    for hop in hops:
        hop.wait_send()
    lay_back(centre, result)

    def give_back(d, carry):
        to = (row + d) % ROWS
        hit = []
        for s in range(2):
            tag = jnp.broadcast_to(arrived[to, 64 + s : 65 + s, :], (8, 128))
            hit.append([tag == float(k) for k in range(16)])
        for c in range(4):
            rows = slice(c * 8, (c + 1) * 8)
            v = [result[0, rows, :]] * 2
            for k in range(1, 16):
                box = result[k, rows, :]
                v = [jnp.where(hit[s][k], box, v[s]) for s in range(2)]
            for s in range(2):
                returned[d * 2 + s, rows, :] = v[s]
        return carry

    lax.fori_loop(0, ROWS, give_back, 0)
    returns = []
    for d in FAR_FIRST:
        src, dst = returned.at[pl.ds(2 * d, 2)], back.at[pl.ds(row * 2, 2)]
        returns.append(start_copy(src, dst, s6.at[d], r6.at[d], ((row + d) % ROWS, col)))
    for s in range(2):
        back[row * 2 + s] = returned[s]
    for copy in returns:
        copy.wait_recv()
    for q in range(16):
        earlier = jnp.int32(0)
        for k in range(q):
            earlier = jnp.where(dest[k] == dest[q], 1, earlier)
        out[pl.ds(q // 8 * 256 + q % 8, N, stride=8), :] = back[2 * dest[q] + earlier]
    for copy in arrivals + pairs + sums + returns:
        copy.wait_send()


def convolve(fine, slot, neighbours, kernel_ops, filter_matrix):
    vm = pl.BlockSpec(memory_space=pltpu.VMEM)
    sm = pl.BlockSpec(memory_space=pltpu.SMEM)
    low = ((1280, 256), (2560, 256), (2560, 256), (TERMS, 96, 128), (128, 384), (256, 640), (64, 640), (384, 512))
    scratch = [pltpu.VMEM(shape, f32) for shape in ((16, 32, 128), (216, 1024), (32, 1024), (32, 128))]
    scratch += [pltpu.VMEM(shape, bf16) for shape in low]
    scratch += [pltpu.VMEM(shape, f32) for shape in ((216, 1024), (16, 72, 128), (16, 72, 128), (3, 16, 32, 128), (N * BOX_LINE, 128))]
    scratch += [pltpu.VMEM(shape, bf16) for shape in ((3, 1024, 256), (2048, 256), (2048, 256))]
    scratch += [pltpu.VMEM((N * SIDE_LINE, 128), f32)] * 3
    scratch += [
        pltpu.VMEM(shape, f32)
        for shape in (
            (256, 384), (4, 2, 2, 256, 128), (1024, 128), (4, 2, 256, 128), (4, 3, 128, 128), (4, 3, 128, 128),
            (4, 128, 128), (32, 32, 128), (32, 32, 128),
        )
    ]
    scratch += [pltpu.SemaphoreType.DMA((n,)) for n in (16, 16, 4, 4, 4, 4, 12, 12, 16, 16)]
    return pl.pallas_call(
        convolve_kernel,
        out_shape=jax.ShapeDtypeStruct((512, 128), f32),
        in_specs=[vm, sm, sm, vm, vm],
        out_specs=vm,
        scratch_shapes=scratch,
        compiler_params=pltpu.CompilerParams(
            collective_id=1, has_side_effects=True, vmem_limit_bytes=60 * 2**20
        ),
    )(fine, slot, neighbours, kernel_ops, filter_matrix)


def local(fine_coeffs, fine_slot, neighbours, filter_matrix, kernel_ops):
    held_boxes, volume = fine_coeffs.shape
    boxes = jnp.transpose(fine_coeffs.reshape(2, 8, 32, 128), (0, 2, 1, 3)).reshape(512, 128)
    out = convolve(boxes, fine_slot, neighbours.T, jnp.transpose(kernel_ops, (1, 2, 0, 3)), filter_matrix)
    return jnp.transpose(out.reshape(2, 32, 8, 128), (0, 2, 1, 3)).reshape(held_boxes, volume)


def solution(mesh):
    in_specs = (P(("row", "col"), None), P(("row", "col")), P("row", None), P(), P())
    out_specs = P(("row", "col"), None)
    return jax.shard_map(local, mesh=mesh, in_specs=in_specs, out_specs=out_specs, check_vma=False)
```
